256 devices in a mesh: seq: 32 (over x_lo, z, core), expert: 8 (over y, x_hi).
Axes of the slice: x: 4 (x_hi: 2, x_lo: 2; x = x_hi * 2 + x_lo), y: 4, z: 8, core: 2. Of those that a mesh axis runs over, the one named last changes fastest.
Arguments:
- tokens: float32 [1536, 32768], P('expert', 'seq'), as said below
- router: float32 [1536, 64], P('expert'), as said below
- w_in: float32 [32, 1536, 3072], P('expert', 'seq'), may hold values from -0.15625 to 0.15625
- w_out: float32 [32, 1536, 3072], P('expert', 'seq'), may hold values from -0.109375 to 0.109375
- grad_out: float32 [1536, 32768], P('expert', 'seq'), may hold values from -0.6 to 0.6
Outputs:
- grad_tokens: float32 [1536, 32768], P('expert', 'seq')
- grad_router: float32 [1536, 64], P('expert')
- grad_w_in: float32 [32, 1536, 3072], P('expert', 'seq')
- grad_w_out: float32 [32, 1536, 3072], P('expert', 'seq')
The draws below stay inside these ranges and needn't reach their ends.
Inputs may be any that keep to these rules, and one draw needn't show every extreme that they name: Entries are of order one in most tokens; a few tokens may be far larger. `router`: columns of moderate norm.
All inputs are finite; a program needn't handle non-finite values.
Results may differ from the reference program's by a relative error of at most 0.0003.
Values sent between devices are 32-bit elements; how exact they have to be, the bound alone decides.
No kernel may reach another device: no remote copies, remote signals or barrier semaphores. Data moves between devices by JAX's collectives and lax.ppermute only.
A program may use at most 64 MiB of HBM per device.

```python
import math
import jax
import jax.numpy as jnp
from jax import lax

D = 1536
H = 3072
PER_EXPERT = 2
EXPERTS = 32
SLOTS = 64
TOKENS = 32768


def draw_router(key, part):
    own_key = jax.random.fold_in(key, 1)
    return jax.random.normal(own_key, (D, SLOTS), jnp.float32) * (1.0 / math.sqrt(D))


def draw_tokens(key, part):
    own_key = jax.random.fold_in(key, 2)
    return jax.random.normal(own_key, (D, TOKENS), jnp.float32)


def block_scale(key, shape, cuts, smallest, top_value):
    def one(dim, shards_of):
        steps = jax.random.uniform(jax.random.fold_in(jax.random.fold_in(key, 6), dim), (shards_of,), jnp.float32, smallest / len(cuts), top_value / len(cuts))
        return jnp.repeat(jnp.exp(steps), shape[dim] // shards_of).reshape((-1,) + (1,) * (len(shape) - dim - 1))

    factor_of = one(*cuts[0])
    for cut in cuts[1:]:
        factor_of = factor_of * one(*cut)
    return factor_of


def scatter_about(stream_key, shape, width, most, cuts=(), held_as=jnp.bfloat16):
    values = jax.random.normal(stream_key, shape, jnp.float32) * width
    if len(cuts) > 0:
        values = block_scale(stream_key, shape, cuts, -0.22, 0.18) * values
    return jnp.clip(values, min=-most, max=most).astype(held_as)


def setup_inputs(seed: int = 0) -> dict:
    key_of = jax.random.split(jax.random.key(seed), 6)
    return {
        "tokens": draw_tokens(jax.random.fold_in(key_of[5], 71), 0),
        "router": draw_router(jax.random.fold_in(key_of[5], 71), 0),
        "w_in": scatter_about(key_of[2], (EXPERTS, D, H), D ** -0.5, 0.15625, ((0, 8), (1, 32)), jnp.float32),
        "w_out": scatter_about(key_of[3], (EXPERTS, D, H), H ** -0.5, 0.109375, ((0, 8), (1, 32)), jnp.float32),
        "grad_out": scatter_about(key_of[4], (D, TOKENS), 0.1, 0.6, ((0, 8), (1, 32)), jnp.float32),
    }


HIGH = lax.Precision.HIGHEST

def smooth_gate(values):
    return jax.nn.gelu(values, approximate=True)

def product(left, right):
    return jnp.dot(left, right, precision=HIGH, preferred_element_type=jnp.float32)

def reference(tokens, router, w_in, w_out, grad_out):
    rows = tokens.T
    grads = grad_out.T
    logits = product(rows, router)
    dispatch = jax.nn.softmax(logits, axis=0)
    combine = jax.nn.softmax(logits, axis=1)
    slot_in = product(dispatch.T, rows)
    inputs = slot_in.reshape(EXPERTS, PER_EXPERT, D)
    pre = jnp.einsum('epd,edh->eph', inputs, w_in, precision=HIGH)
    act, backward = jax.vjp(smooth_gate, pre)
    slot_out = jnp.einsum('eph,edh->epd', act, w_out, precision=HIGH).reshape(SLOTS, D)
    grad_combine = product(grads, slot_out.T)
    grad_slot_out = product(combine.T, grads).reshape(EXPERTS, PER_EXPERT, D)
    grad_act = jnp.einsum('epd,edh->eph', grad_slot_out, w_out, precision=HIGH)
    grad_pre = backward(grad_act)[0]
    grad_w_out = jnp.einsum('epd,eph->edh', grad_slot_out, act, precision=HIGH)
    grad_w_in = jnp.einsum('epd,eph->edh', inputs, grad_pre, precision=HIGH)
    grad_slot_in = jnp.einsum('eph,edh->epd', grad_pre, w_in, precision=HIGH).reshape(SLOTS, D)
    grad_dispatch = product(rows, grad_slot_in.T)
    row_part = combine * (grad_combine - lax.optimization_barrier(jnp.sum(combine * grad_combine, axis=1, keepdims=True)))
    column_part = dispatch * (grad_dispatch - lax.optimization_barrier(jnp.sum(dispatch * grad_dispatch, axis=0, keepdims=True)))
    grad_logits = row_part + column_part
    grad_rows = product(dispatch, grad_slot_in) + product(grad_logits, router.T)
    grad_router = product(tokens, grad_logits)
    return (grad_rows.T, grad_router, grad_w_in, grad_w_out)
```

```python
import jax
import jax.numpy as jnp
from jax import lax
from jax.sharding import PartitionSpec as P

HIGH = lax.Precision.HIGHEST
S = "seq"
E = "expert"


def smooth_gate(values):
    return jax.nn.gelu(values, approximate=True)


def contract(left, right, left_dim, right_dim):
    return lax.dot_general(
        left,
        right,
        (((left_dim,), (right_dim,)), ((), ())),
        precision=HIGH,
        preferred_element_type=jnp.float32,
    )


def einsum(form, left, right):
    return jnp.einsum(form, left, right, precision=HIGH, preferred_element_type=jnp.float32)


def exchange(blocks, axis, groups=None):
    return lax.all_to_all(blocks, axis, 0, 0, axis_index_groups=groups, tiled=True)


def gather(block, axis, count, groups=None):
    return exchange(jnp.broadcast_to(block[None], (count,) + block.shape), axis, groups)


def merge(tops, sums, rows):
    top = jnp.max(tops, axis=0)
    scale = jnp.exp(tops - top[None])
    return top, jnp.sum(scale * sums, axis=0), jnp.sum(scale[..., None] * rows, axis=0)


def per_device(tokens, router, w_in, w_out, grad_out):
    n_seq, n_exp = lax.axis_size(S), lax.axis_size(E)
    local_experts, width_block, hidden = w_in.shape
    rows_block, local_tokens = tokens.shape
    slots = router.shape[1]
    own_slots = slots // n_exp
    per_expert = own_slots // local_experts
    width = rows_block * n_exp
    piece = local_tokens // n_exp
    core = lax.axis_index(S) % 2
    chips = n_seq // 2
    partner = [(i, i ^ 1) for i in range(n_seq)]
    groups = [[2 * k + c for k in range(chips)] for c in range(2)]
    half = own_slots // 2

    def by_tokens(values):
        return jnp.transpose(values.reshape(rows_block, n_exp, piece), (1, 0, 2))

    folded = jnp.concatenate([router[: rows_block // 2], router[rows_block // 2 :]], axis=1)
    packed = jnp.concatenate(
        [
            by_tokens(tokens),
            by_tokens(grad_out),
            jnp.broadcast_to(folded[None], (n_exp,) + folded.shape),
        ],
        axis=1,
    )
    got = exchange(packed, E)
    x = got[:, :rows_block].reshape(width, piece)
    g = got[:, rows_block : 2 * rows_block].reshape(width, piece)
    r = got[:, 2 * rows_block :]
    router_full = jnp.concatenate([r[:, :, :slots], r[:, :, slots:]], axis=1).reshape(width, slots)

    logits = contract(router_full, x, 0, 0)
    combine = jax.nn.softmax(logits, axis=0)
    local_top = jnp.max(logits, axis=1)
    raised = jnp.exp(logits - local_top[:, None])
    local_sum = jnp.sum(raised, axis=1)
    rows_in = contract(raised, x, 1, 1).reshape(n_exp, own_slots, width)
    rows_out = contract(combine, g, 1, 1).reshape(n_exp, own_slots, width)
    marks = jnp.stack([local_top, local_sum], axis=1).reshape(n_exp, own_slots, 2)
    marks = jnp.pad(marks, ((0, 0), (0, own_slots), (0, 126)))
    sent = jnp.concatenate([jnp.concatenate([rows_in, rows_out], axis=1), marks], axis=2)
    got = exchange(sent, E)
    top, total, rows = merge(
        got[:, :own_slots, width], got[:, :own_slots, width + 1], got[:, :own_slots, :width]
    )
    outer = jnp.sum(got[:, own_slots:, :width], axis=0)

    def by_width(values):
        return jnp.transpose(values.reshape(own_slots, n_seq, width_block), (1, 0, 2))

    def spread(values):
        return jnp.broadcast_to(values[None, :, None], (n_seq, own_slots, 1))

    sent = jnp.concatenate(
        [
            by_width(rows),
            by_width(outer),
            spread(top),
            spread(total),
            jnp.zeros((n_seq, own_slots, 30), jnp.float32),
        ],
        axis=2,
    )
    got = exchange(sent, S)
    w = width_block
    top, total, rows = merge(got[:, :, 2 * w], got[:, :, 2 * w + 1], got[:, :, :w])
    slot_in = rows / total[:, None]
    grad_slot_out = jnp.sum(got[:, :, w : 2 * w], axis=0)

    inputs = slot_in.reshape(local_experts, per_expert, w)
    outers = grad_slot_out.reshape(local_experts, per_expert, w)
    pre_part = einsum("epd,edh->eph", inputs, w_in).reshape(2, half, hidden)
    act_part = einsum("epd,edh->eph", outers, w_out).reshape(2, half, hidden)
    parts = jnp.stack([pre_part, act_part], axis=1)
    mine = lax.dynamic_index_in_dim(parts, core, 0, keepdims=False)
    theirs = lax.dynamic_index_in_dim(parts, 1 - core, 0, keepdims=False)
    mine = mine + lax.ppermute(theirs, S, partner)
    share = half * hidden // chips
    sent = jnp.transpose(mine.reshape(2, chips, share), (1, 0, 2))
    got = jnp.sum(exchange(sent, S, groups), axis=0)
    act, backward = jax.vjp(smooth_gate, got[0])
    grad_pre = backward(got[1])[0]
    got = gather(jnp.stack([act, grad_pre]), S, chips, groups)
    mine = jnp.transpose(got, (1, 0, 2)).reshape(2, half, hidden)
    theirs = lax.ppermute(mine, S, partner)
    both = jnp.where(core == 0, jnp.stack([mine, theirs], 1), jnp.stack([theirs, mine], 1))
    both = both.reshape(2, local_experts, per_expert, hidden)
    act, grad_pre = both[0], both[1]

    slot_out = einsum("eph,edh->epd", act, w_out).reshape(own_slots, w)
    grad_slot_in = einsum("eph,edh->epd", grad_pre, w_in).reshape(own_slots, w)
    grad_w_out = einsum("epd,eph->edh", outers, act)
    grad_w_in = einsum("epd,eph->edh", inputs, grad_pre)
    column_part = jnp.sum(slot_in * grad_slot_in, axis=1)
    sent = jnp.concatenate(
        [
            slot_out,
            grad_slot_in,
            top[:, None],
            total[:, None],
            column_part[:, None],
            jnp.zeros((own_slots, 29), jnp.float32),
        ],
        axis=1,
    )
    got = gather(sent, S, n_seq)

    def to_rows(values):
        return jnp.transpose(values, (1, 0, 2)).reshape(own_slots, width)

    marks = jnp.stack(
        [got[0, :, 2 * w], got[0, :, 2 * w + 1], jnp.sum(got[:, :, 2 * w + 2], axis=0)], axis=1
    )
    marks = jnp.pad(marks, ((0, own_slots), (0, 125)))
    rows = jnp.concatenate([to_rows(got[:, :, :w]), to_rows(got[:, :, w : 2 * w])], axis=0)
    got = gather(jnp.concatenate([rows, marks], axis=1), E, n_exp)
    slot_out = got[:, :own_slots, :width].reshape(slots, width)
    grad_slot_in = got[:, own_slots:, :width].reshape(slots, width)
    marks = got[:, :own_slots, width:].reshape(slots, 128)
    top, total, column_total = marks[:, 0], marks[:, 1], marks[:, 2]

    grad_combine = contract(slot_out, g, 1, 0)
    grad_dispatch = contract(grad_slot_in, x, 1, 0)
    dispatch = raised * (jnp.exp(local_top - top) / total)[:, None]
    grad_logits = combine * (
        grad_combine - jnp.sum(combine * grad_combine, axis=0, keepdims=True)
    ) + dispatch * (grad_dispatch - column_total[:, None])
    got = gather(jnp.concatenate([dispatch, grad_logits], axis=0), E, n_exp)
    spread_all = jnp.transpose(got, (1, 0, 2)).reshape(2 * slots, local_tokens)
    mine = lax.dynamic_slice_in_dim(
        grad_slot_in, lax.axis_index(E) * rows_block, rows_block, 1
    )
    grad_tokens = contract(jnp.concatenate([mine, router.T], axis=0), spread_all, 0, 0)
    router_part = contract(tokens, spread_all[slots:], 1, 1)
    parts = router_part.reshape(2, rows_block // 2, slots)
    mine = lax.dynamic_index_in_dim(parts, core, 0, keepdims=False)
    theirs = lax.dynamic_index_in_dim(parts, 1 - core, 0, keepdims=False)
    mine = mine + lax.ppermute(theirs, S, partner)
    mine = jnp.sum(gather(mine, S, chips, groups), axis=0)
    theirs = lax.ppermute(mine, S, partner)
    grad_router = jnp.where(
        core == 0, jnp.concatenate([mine, theirs]), jnp.concatenate([theirs, mine])
    )
    return (grad_tokens, grad_router, grad_w_in, grad_w_out)


def solution(mesh):
    placed = (
        P("expert", "seq"),
        P("expert", None),
        P("expert", "seq", None),
        P("expert", "seq", None),
        P("expert", "seq"),
    )
    return jax.shard_map(
        per_device,
        mesh=mesh,
        in_specs=placed,
        out_specs=(
            P("expert", "seq"),
            P("expert", None),
            P("expert", "seq", None),
            P("expert", "seq", None),
        ),
        check_vma=False,
    )
```

```python
import functools

import jax
import jax.numpy as jnp
from jax import lax
from jax.experimental import pallas as pl
from jax.experimental.pallas import tpu as pltpu
from jax.sharding import PartitionSpec as P

HIGH = lax.Precision.HIGHEST
S = "seq"
E = "expert"
LANES = 128
F32 = jnp.float32


def contract(left, right, left_dim, right_dim, precision=HIGH):
    return lax.dot_general(
        left,
        right,
        (((left_dim,), (right_dim,)), ((), ())),
        precision=precision,
        preferred_element_type=F32,
    )


def exchange(blocks, axis, groups=None):
    return lax.all_to_all(blocks, axis, 0, 0, axis_index_groups=groups, tiled=True)


def run(kernel, shapes, *values, scratch=(), flops=0):
    single = not isinstance(shapes, list)
    shapes = [shapes] if single else shapes
    size = 4 * sum(v.size for v in values) + 4 * sum(functools.reduce(lambda a, b: a * b, s) for s in shapes)
    spec = pl.BlockSpec(memory_space=pltpu.VMEM)
    out = pl.pallas_call(
        kernel,
        out_shape=[jax.ShapeDtypeStruct(s, F32) for s in shapes],
        in_specs=[spec] * len(values),
        out_specs=[spec] * len(shapes),
        scratch_shapes=[pltpu.VMEM(s, F32) for s in scratch],
        compiler_params=pltpu.CompilerParams(vmem_limit_bytes=40 * 1024 * 1024),
        cost_estimate=pl.CostEstimate(flops=flops, bytes_accessed=size, transcendentals=0),
    )(*values)
    return out[0] if single else out


def row_of(shape):
    return lax.broadcasted_iota(jnp.int32, shape, len(shape) - 2) % 8


def lane_of(shape):
    return lax.broadcasted_iota(jnp.int32, shape, len(shape) - 1)


def swap(values):
    return jnp.concatenate([values[..., 4:8, :], values[..., 0:4, :]], axis=-2)


def core_index():
    return lax.axis_index(S) % 2


def pack_tokens(tokens, grad_out, router, out):
    n, rows = out.shape[0], tokens.shape[0]
    folded = jnp.concatenate([router[: rows // 2], router[rows // 2 :]], axis=1)
    for e in range(n):
        out[e, 0:rows] = tokens[:, e * LANES : (e + 1) * LANES]
        out[e, rows : 2 * rows] = grad_out[:, e * LANES : (e + 1) * LANES]
        out[e, 2 * rows :] = folded


def token_blocks(got):
    n, rows = got.shape[0], got.shape[1] * 2 // 5
    x = got[:, 0:rows].reshape(n * rows, LANES)
    g = got[:, rows : 2 * rows].reshape(n * rows, LANES)
    return x, g


def softmax_rows(got, sent, keep, tops):
    n, rows = got.shape[0], got.shape[1] * 2 // 5
    width = n * rows
    half = rows // 2
    r = got[:, 2 * rows :].reshape(n * half, LANES)
    pair = jnp.concatenate(
        [
            got[:, 0:half].reshape(n * half, LANES),
            got[:, half:rows].reshape(n * half, LANES),
        ],
        axis=1,
    )
    both = contract(r, pair, 0, 0)
    slots = LANES // 2
    logits = both[:slots, :LANES] + both[slots:, LANES:]
    raised = jnp.exp(logits - jnp.max(logits, axis=0, keepdims=True))
    combine = raised / jnp.sum(raised, axis=0, keepdims=True)
    top = jnp.max(logits, axis=1, keepdims=True)
    raised = jnp.exp(logits - top)
    total = jnp.sum(raised, axis=1, keepdims=True)
    x, g = token_blocks(got)
    rows_in = contract(raised, x, 1, 1)
    rows_out = contract(combine, g, 1, 1)
    lane = lane_of((slots, LANES))
    marks = jnp.where(lane == 0, top, jnp.where(lane == 1, total, 0.0))
    plain = jnp.where(lane_of((4, LANES)) == 1, 1.0, 0.0)
    wide_top = jnp.broadcast_to(top, (slots, LANES))
    for j in range(slots // 4):
        e, b, s = j // 2, 8 * (j % 2), slice(4 * j, 4 * j + 4)
        sent[e, b : b + 4, 0:width] = rows_in[s]
        sent[e, b + 4 : b + 8, 0:width] = rows_out[s]
        sent[e, b : b + 4, width:] = marks[s]
        sent[e, b + 4 : b + 8, width:] = plain
        keep[j, 0:4] = combine[s]
        keep[j, 4:8] = raised[s]
        tops[j, 0:4] = wide_top[s]
        tops[j, 4:8] = wide_top[s]


def merge_tokens(got, out):
    n, width = got.shape[0], got.shape[2] - LANES
    wide = out.shape[0] // 2
    piece = width // wide
    marks = [got[e, :, width:] for e in range(n)]
    top = functools.reduce(jnp.maximum, [m[:, 0:1] for m in marks])
    scale = [jnp.exp(m[:, 0:1] - top) for m in marks]
    total = sum(s * m[:, 1:2] for s, m in zip(scale, marks))
    rows = sum(s * got[e, :, 0:width] for e, s in enumerate(scale))
    lane = lane_of((16, LANES))
    tail = jnp.where(lane == piece, top, jnp.where(lane == piece + 1, total, 0.0))
    for c in range(2):
        s = slice(8 * c, 8 * c + 8)
        for k in range(wide):
            out[2 * k + c] = tail[s]
            out[2 * k + c, :, 0:piece] = rows[s, k * piece : (k + 1) * piece]


def hidden_parts(got, w_in, w_out, near_in, near_out, sent, keep, full):
    piece = 2 * w_in.shape[1]
    hidden = w_in.shape[2]
    core = core_index()
    tops = got[:, :, piece : piece + 1]
    top = jnp.max(tops, axis=0)
    rows = jnp.sum(jnp.exp(tops - top[None]) * got[...], axis=0)
    total = rows[:, piece + 1 : piece + 2]
    rows = jnp.where(row_of((8, LANES)) < 4, rows / total, rows)
    lane = lane_of((8, LANES))
    keep[...] = jnp.where(lane == piece, top, jnp.where(lane == piece + 1, total, rows))
    turned = jnp.transpose(rows)
    low, high = turned[0 : piece // 2], turned[piece // 2 : piece]
    own = jnp.where(core == 0, low, high)
    near = jnp.where(core == 0, high, low)
    step = 512
    for a in range(2):
        for kind, mine, theirs in ((0, w_in, near_in), (1, w_out, near_out)):
            for h in range(0, hidden, step):
                left = mine[2 * core + a, :, h : h + step]
                right = theirs[a, :, h : h + step]
                for p in range(2):
                    r = 4 * kind + 2 * a + p
                    part = left * own[:, r : r + 1] + right * near[:, r : r + 1]
                    full[r : r + 1, h : h + step] = jnp.sum(part, axis=0, keepdims=True)
    chips = sent.shape[0]
    share = hidden // chips
    for k in range(chips):
        sent[k, :, 0:share] = full[:, k * share : (k + 1) * share]
        sent[k, :, share:] = jnp.zeros((8, sent.shape[2] - share), F32)


def gate(got, out):
    z = jnp.sum(got[...], axis=0)
    other = swap(z)
    first = row_of(z.shape) < 4
    pre = jnp.where(first, z, other)
    grad = jnp.where(first, other, z)
    c = 0.7978845608028654
    t = jnp.tanh(c * (pre + 0.044715 * (pre * pre * pre)))
    act = 0.5 * pre * (1.0 + t)
    slope = 0.5 * (1.0 + t) + 0.5 * pre * (1.0 - t * t) * (c * (1.0 + 3 * 0.044715 * (pre * pre)))
    both = jnp.where(first, act, grad * slope)
    for k in range(out.shape[0]):
        out[k] = both


def slot_rows(got, keep, w_in, w_out, near_in, near_out, out, full):
    piece = 2 * w_in.shape[1]
    hidden = w_in.shape[2]
    chips = got.shape[0]
    share = hidden // chips
    core = core_index()
    for k in range(chips):
        full[:, k * share : (k + 1) * share] = got[k, :, 0:share]
    lane = lane_of((piece // 2, LANES))
    own = jnp.zeros((piece // 2, LANES), F32)
    near = own
    for a in range(2):
        for kind, mine, theirs in ((0, w_out, near_out), (1, w_in, near_in)):
            for p in range(2):
                r = 4 * kind + 2 * a + p
                line = full[r : r + 1, :]
                col = jnp.sum(mine[2 * core + a] * line, axis=1, keepdims=True)
                own = jnp.where(lane == r, col, own)
                col = jnp.sum(theirs[a] * line, axis=1, keepdims=True)
                near = jnp.where(lane == r, col, near)
    low = jnp.where(core == 0, own, near)
    high = jnp.where(core == 0, near, own)
    square = jnp.concatenate([low, high, jnp.zeros((LANES - piece, LANES), F32)], axis=0)
    rows = jnp.transpose(square)[0:8]
    held = swap(keep[...])
    lane = lane_of((8, LANES))
    column = jnp.sum(jnp.where(lane < piece, held * rows, 0.0), axis=1, keepdims=True)
    tile = jnp.where(lane < piece, rows, jnp.where(lane == piece + 2, column, held))
    for k in range(out.shape[0]):
        out[k] = tile


def join_widths(got, out, line):
    n = got.shape[0] // 2
    width = out.shape[2] - LANES
    piece = width // n
    lane = lane_of((8, LANES))
    for c in range(2):
        s = slice(8 * c, 8 * c + 8)
        for k in range(n):
            line[s, k * piece : (k + 1) * piece] = got[2 * k + c, :, 0:piece]
        added = sum(got[2 * k + c] for k in range(n))
        line[s, width:] = jnp.where(lane == piece + 2, added, got[c])
    for e in range(out.shape[0]):
        out[e] = line[...]


def logit_grads(got, blocks, keep, tops, out, mine):
    n = got.shape[0]
    width = got.shape[2] - LANES
    rows = width // n
    piece = width // 16
    x, g = token_blocks(blocks)
    left = got[:, :, 0:width].reshape(16 * n, width)
    both = contract(left, jnp.concatenate([x, g], axis=1), 1, 0).reshape(2 * n, 8, 2 * LANES)
    first = row_of((2 * n, 8, LANES)) < 4
    grads = jnp.where(first, both[:, :, LANES:], both[:, :, :LANES])
    marks = got[:, :, width:].reshape(2 * n, 8, LANES)
    top = marks[:, :, piece : piece + 1]
    total = marks[:, :, piece + 1 : piece + 2]
    column = marks[:, :, piece + 2 : piece + 3]
    held = keep[...]
    weights = jnp.where(first, held, held * (jnp.exp(tops[...] - top) / total))
    product = jnp.where(first, weights * grads, 0.0)
    line = jnp.sum(jnp.sum(product, axis=0), axis=0, keepdims=True)
    part = weights * (grads - jnp.where(first, line[None], column))
    part = part + swap(part)
    slots = 8 * n
    for e in range(n):
        for j in range(2 * n):
            out[e, 4 * j : 4 * j + 4] = part[j, 0:4]
            out[e, slots + 4 * j : slots + 4 * j + 4] = weights[j, 4:8]
    me = lax.axis_index(E)
    for e in range(n):

        @pl.when(me == e)
        def _():
            for j in range(2 * n):
                mine[4 * j : 4 * j + 4] = got[
                    j // 2, 8 * (j % 2) + 4 : 8 * (j % 2) + 8, e * rows : (e + 1) * rows
                ]


def router_part(got, tokens, mine, theirs):
    n = got.shape[0]
    slots = got.shape[1] // 2
    grads = jnp.concatenate([got[e, 0:slots] for e in range(n)], axis=1)
    part = contract(tokens[...], grads, 1, 1)
    q = part.shape[0] // 4
    low = jnp.concatenate([part[0:q], part[q : 2 * q]], axis=1)
    high = jnp.concatenate([part[2 * q : 3 * q], part[3 * q :]], axis=1)
    core = core_index()
    mine[...] = jnp.where(core == 0, low, high)
    theirs[...] = jnp.where(core == 0, high, low)


def token_grads(got, rows, router, out):
    left = jnp.concatenate([router[...], jnp.transpose(rows[...])], axis=1)
    for e in range(got.shape[0]):
        out[:, e * LANES : (e + 1) * LANES] = contract(left, got[e], 1, 0)


def add_copies(mine, theirs, out):
    both = mine[...] + theirs[...]
    for k in range(out.shape[0]):
        out[k] = both


def add_all(got, out):
    out[...] = jnp.sum(got[...], axis=0)


def unfold(mine, theirs, out):
    core = core_index()
    a, b = mine[...], theirs[...]
    low = jnp.where(core == 0, a, b)
    high = jnp.where(core == 0, b, a)
    q, h = out.shape[0] // 4, LANES // 2
    out[0:q] = low[:, :h]
    out[q : 2 * q] = low[:, h:]
    out[2 * q : 3 * q] = high[:, :h]
    out[3 * q :] = high[:, h:]


def weight_grads(full, near_full, keep, near_keep, grad_in, grad_out):
    w = grad_in.shape[1]
    hidden = grad_in.shape[2]
    core = core_index()
    step = 512
    for base, values, held in ((2 * core, full, keep), (2 - 2 * core, near_full, near_keep)):
        held = held[...]
        part = jnp.where(core == 0, held[:, 0:w], held[:, w : 2 * w])
        cols = jnp.transpose(part)
        for a in range(2):
            for h in range(0, hidden, step):
                s = slice(h, h + step)
                i, j = 2 * a, 2 * a + 1
                grad_out[base + a, :, s] = (
                    cols[:, 4 + i : 5 + i] * values[i : i + 1, s]
                    + cols[:, 4 + j : 5 + j] * values[j : j + 1, s]
                )
                grad_in[base + a, :, s] = (
                    cols[:, i : i + 1] * values[4 + i : 5 + i, s]
                    + cols[:, j : j + 1] * values[4 + j : 5 + j, s]
                )


def per_device(tokens, router, w_in, w_out, grad_out):
    n_seq, n_exp = lax.axis_size(S), lax.axis_size(E)
    experts, width_block, hidden = w_in.shape
    rows_block, local_tokens = tokens.shape
    slots = router.shape[1]
    own_slots = slots // n_exp
    width = rows_block * n_exp
    chips = n_seq // 2
    core = core_index()
    partner = [(i, i ^ 1) for i in range(n_seq)]
    groups = [[2 * k + c for k in range(chips)] for c in range(2)]

    def to_partner(values):
        return lax.ppermute(values, S, partner)

    packed = run(pack_tokens, (n_exp, rows_block * 5 // 2, LANES), tokens, grad_out, router)
    blocks = exchange(packed, E)
    half = experts // 2
    near_in = to_partner(lax.dynamic_slice_in_dim(w_in, half * (1 - core), half, 0))
    near_out = to_partner(lax.dynamic_slice_in_dim(w_out, half * (1 - core), half, 0))

    line = width + LANES
    groups8 = (slots // 4, 8, LANES)
    sent, keep, tops = run(
        softmax_rows, [(n_exp, 2 * own_slots, line), groups8, groups8], blocks
    )
    sent = run(merge_tokens, (n_seq, 8, LANES), exchange(sent, E))
    share = hidden // chips
    cut = -(-share // LANES) * LANES
    sent, held = run(
        hidden_parts,
        [(chips, 8, cut), (8, LANES)],
        exchange(sent, S),
        w_in,
        w_out,
        near_in,
        near_out,
        scratch=[(8, hidden)],
    )
    sent = run(gate, (chips, 8, cut), exchange(sent, S, groups))
    sent, full = run(
        slot_rows,
        [(n_seq, 8, LANES), (8, hidden)],
        exchange(sent, S, groups),
        held,
        w_in,
        w_out,
        near_in,
        near_out,
    )
    near_full = to_partner(full)
    near_held = to_partner(held)
    grad_w_in, grad_w_out = run(
        weight_grads, [w_in.shape, w_out.shape], full, near_full, held, near_held
    )
    sent = run(
        join_widths, (n_exp, 16, line), exchange(sent, S), scratch=[(16, line)]
    )
    sent, mine = run(
        logit_grads,
        [(n_exp, 2 * slots, LANES), (slots, rows_block)],
        exchange(sent, E),
        blocks,
        keep,
        tops,
    )
    spread = exchange(sent, E)
    fold = (rows_block // 4, 2 * slots)
    near, theirs = run(router_part, [fold, fold], spread, tokens)
    grad_tokens = run(token_grads, (rows_block, local_tokens), spread, mine, router)
    sent = run(add_copies, (chips,) + fold, near, to_partner(theirs))
    near = run(add_all, fold, exchange(sent, S, groups))
    grad_router = run(unfold, (rows_block, slots), near, to_partner(near))
    return (grad_tokens, grad_router, grad_w_in, grad_w_out)


def solution(mesh):
    placed = (
        P("expert", "seq"),
        P("expert", None),
        P("expert", "seq", None),
        P("expert", "seq", None),
        P("expert", "seq"),
    )
    return jax.shard_map(
        per_device,
        mesh=mesh,
        in_specs=placed,
        out_specs=(
            P("expert", "seq"),
            P("expert", None),
            P("expert", "seq", None),
            P("expert", "seq", None),
        ),
        check_vma=False,
    )
```

```python
import functools

import jax
import jax.numpy as jnp
from jax import lax
from jax.experimental import pallas as pl
from jax.experimental.pallas import tpu as pltpu
from jax.sharding import PartitionSpec as P

HIGH = lax.Precision.HIGHEST
S = "seq"
E = "expert"
LANES = 128
F32 = jnp.float32


def contract(left, right, left_dim, right_dim, precision=HIGH):
    return lax.dot_general(
        left,
        right,
        (((left_dim,), (right_dim,)), ((), ())),
        precision=precision,
        preferred_element_type=F32,
    )


def exchange(blocks, axis, groups=None):
    return lax.all_to_all(blocks, axis, 0, 0, axis_index_groups=groups, tiled=True)


def run(kernel, shapes, *values, scratch=(), flops=0):
    single = not isinstance(shapes, list)
    shapes = [shapes] if single else shapes
    size = 4 * sum(v.size for v in values) + 4 * sum(functools.reduce(lambda a, b: a * b, s) for s in shapes)
    spec = pl.BlockSpec(memory_space=pltpu.VMEM)
    out = pl.pallas_call(
        kernel,
        out_shape=[jax.ShapeDtypeStruct(s, F32) for s in shapes],
        in_specs=[spec] * len(values),
        out_specs=[spec] * len(shapes),
        scratch_shapes=[pltpu.VMEM(s, F32) for s in scratch],
        compiler_params=pltpu.CompilerParams(vmem_limit_bytes=40 * 1024 * 1024),
        cost_estimate=pl.CostEstimate(flops=flops, bytes_accessed=size, transcendentals=0),
    )(*values)
    return out[0] if single else out


def row_of(shape):
    return lax.broadcasted_iota(jnp.int32, shape, len(shape) - 2) % 8


def lane_of(shape):
    return lax.broadcasted_iota(jnp.int32, shape, len(shape) - 1)


def swap(values):
    return jnp.concatenate([values[..., 4:8, :], values[..., 0:4, :]], axis=-2)


def core_index():
    return lax.axis_index(S) % 2


def pack_tokens(tokens, grad_out, router, out, held, logits, load, moves, stores):
    n, rows = out.shape[0], tokens.shape[0]
    first = pltpu.make_async_copy(tokens, held, load)
    first.start()
    copies = []
    for e in range(n):
        s = pl.ds(e * LANES, LANES)
        for i, values in enumerate((tokens, grad_out)):
            copy = pltpu.make_async_copy(
                values.at[:, s], out.at[e, pl.ds(i * rows, rows)], moves.at[2 * e + i]
            )
            copy.start()
            copies.append(copy)
    first.wait()
    part = contract(router[...], held[...], 1, 0)
    for e in range(n):
        logits[e] = part[:, e * LANES : (e + 1) * LANES]
        copy = pltpu.make_async_copy(
            logits.at[e], out.at[e, pl.ds(2 * rows, logits.shape[1])], stores.at[e]
        )
        copy.start()
        copies.append(copy)
    for copy in copies:
        copy.wait()


def token_blocks(got):
    n, rows = got.shape[0], got.shape[1] * 3 // 7
    x = got[:, 0:rows].reshape(n * rows, LANES)
    g = got[:, rows : 2 * rows].reshape(n * rows, LANES)
    return x, g


def softmax_rows(got, mine, near, keep, tops, both):
    n, rows = got.shape[0], got.shape[1] * 3 // 7
    width = n * rows
    logits = sum(got[e, 2 * rows :] for e in range(n))
    slots = logits.shape[0]
    raised = jnp.exp(logits - jnp.max(logits, axis=0, keepdims=True))
    combine = raised / jnp.sum(raised, axis=0, keepdims=True)
    top = jnp.max(logits, axis=1, keepdims=True)
    raised = jnp.exp(logits - top)
    total = jnp.sum(raised, axis=1, keepdims=True)
    x, g = token_blocks(got)
    rows_in = contract(raised, x, 1, 1)
    rows_out = contract(combine, g, 1, 1)
    lane = lane_of((slots, LANES))
    marks = jnp.where(lane == 0, top, jnp.where(lane == 1, total, 0.0))
    plain = jnp.where(lane_of((4, LANES)) == 1, 1.0, 0.0)
    wide_top = jnp.broadcast_to(top, (slots, LANES))
    for e in range(n):
        for c in range(2):
            s, j = slice(8 * e + 4 * c, 8 * e + 4 * c + 4), n * c + e
            both[c, e, 0:4, 0:width] = rows_in[s]
            both[c, e, 4:8, 0:width] = rows_out[s]
            both[c, e, 0:4, width:] = marks[s]
            both[c, e, 4:8, width:] = plain
            keep[j, 0:4] = combine[s]
            keep[j, 4:8] = raised[s]
            tops[j, 0:4] = wide_top[s]
            tops[j, 4:8] = wide_top[s]
    core = core_index()
    mine[...] = both[core]
    near[...] = both[1 - core]


def merge(parts, width):
    marks = [p[:, width : width + LANES] for p in parts]
    top = functools.reduce(jnp.maximum, [m[:, 0:1] for m in marks])
    scale = [jnp.exp(m[:, 0:1] - top) for m in marks]
    rows = sum(s * p[:, 0:width] for s, p in zip(scale, parts))
    total = sum(s * m[:, 1:2] for s, m in zip(scale, marks))
    return rows, top, total


def merge_cores(mine, near, out):
    width = out.shape[2] - LANES
    lane = lane_of((8, LANES))
    for e in range(out.shape[0]):
        rows, top, total = merge([mine[e], near[e]], width)
        out[e, :, 0:width] = rows
        out[e, :, width:] = jnp.where(lane == 0, top, jnp.where(lane == 1, total, 0.0))


def merge_tokens(got, out):
    n, width = got.shape[0], got.shape[2] - LANES
    wide = out.shape[0]
    piece = width // wide
    rows, top, total = merge([got[e] for e in range(n)], width)
    lane = lane_of((8, LANES))
    tail = jnp.where(lane == piece, top, jnp.where(lane == piece + 1, total, 0.0))
    for k in range(wide):
        out[k] = tail
        out[k, :, 0:piece] = rows[:, k * piece : (k + 1) * piece]


def hidden_parts(got, own_in, own_out, near_in, near_out, sent, keep, full):
    w = own_in.shape[1]
    piece = 2 * w
    hidden = own_in.shape[2]
    core = core_index()
    tops = got[:, :, piece : piece + 1]
    top = jnp.max(tops, axis=0)
    rows = jnp.sum(jnp.exp(tops - top[None]) * got[...], axis=0)
    total = rows[:, piece + 1 : piece + 2]
    rows = jnp.where(row_of((8, LANES)) < 4, rows / total, rows)
    lane = lane_of((8, LANES))
    keep[...] = jnp.where(lane == piece, top, jnp.where(lane == piece + 1, total, rows))
    turned = jnp.transpose(rows)
    low, high = turned[0:w], turned[w:piece]
    own = jnp.where(core == 0, low, high)
    near = jnp.where(core == 0, high, low)
    for a in range(2):
        for kind, mine, theirs in ((0, own_in, near_in), (1, own_out, near_out)):
            r = 4 * kind + 2 * a
            values = [
                jnp.concatenate(
                    [
                        jnp.broadcast_to(own[:, r + p : r + p + 1], (w, LANES)),
                        jnp.broadcast_to(near[:, r + p : r + p + 1], (w, LANES)),
                    ],
                    axis=0,
                )
                for p in range(2)
            ]
            for h in range(0, hidden, LANES):
                s = slice(h, h + LANES)
                block = jnp.concatenate([mine[a, :, s], theirs[a, :, s]], axis=0)
                for p in range(2):
                    full[r + p : r + p + 1, s] = jnp.sum(block * values[p], axis=0, keepdims=True)
    chips = sent.shape[0]
    share = hidden // chips
    for k in range(chips):
        sent[k, :, 0:share] = full[:, k * share : (k + 1) * share]
        sent[k, :, share:] = jnp.zeros((8, sent.shape[2] - share), F32)


def gate(got, out):
    z = jnp.sum(got[...], axis=0)
    other = swap(z)
    first = row_of(z.shape) < 4
    pre = jnp.where(first, z, other)
    grad = jnp.where(first, other, z)
    c = 0.7978845608028654
    t = jnp.tanh(c * (pre + 0.044715 * (pre * pre * pre)))
    act = 0.5 * pre * (1.0 + t)
    slope = 0.5 * (1.0 + t) + 0.5 * pre * (1.0 - t * t) * (c * (1.0 + 3 * 0.044715 * (pre * pre)))
    both = jnp.where(first, act, grad * slope)
    for k in range(out.shape[0]):
        out[k] = both


def slot_rows(got, keep, own_in, own_out, near_in, near_out, out, full):
    w = own_in.shape[1]
    piece = 2 * w
    hidden = own_in.shape[2]
    chips = got.shape[0]
    share = hidden // chips
    core = core_index()
    for k in range(chips):
        full[:, k * share : (k + 1) * share] = got[k, :, 0:share]
    lane = lane_of((piece, LANES))
    cols = jnp.zeros((piece, LANES), F32)
    for a in range(2):
        for kind, mine, theirs in ((0, own_out, near_out), (1, own_in, near_in)):
            r = 4 * kind + 2 * a
            sums = [jnp.zeros((piece, LANES), F32) for _ in range(2)]
            for h in range(0, hidden, LANES):
                s = slice(h, h + LANES)
                block = jnp.concatenate([mine[a, :, s], theirs[a, :, s]], axis=0)
                for p in range(2):
                    sums[p] = sums[p] + block * full[r + p : r + p + 1, s]
            for p in range(2):
                cols = jnp.where(lane == r + p, jnp.sum(sums[p], axis=1, keepdims=True), cols)
    own, near = cols[0:w], cols[w:]
    low = jnp.where(core == 0, own, near)
    high = jnp.where(core == 0, near, own)
    square = jnp.concatenate([low, high, jnp.zeros((LANES - piece, LANES), F32)], axis=0)
    rows = jnp.transpose(square)[0:8]
    held = swap(keep[...])
    lane = lane_of((8, LANES))
    column = jnp.sum(jnp.where(lane < piece, held * rows, 0.0), axis=1, keepdims=True)
    tile = jnp.where(lane < piece, rows, jnp.where(lane == piece + 2, column, held))
    for k in range(out.shape[0]):
        out[k] = tile


def join_widths(got, out, line):
    n = got.shape[0]
    width = out.shape[2] - LANES
    piece = width // n
    lane = lane_of((8, LANES))
    for k in range(n):
        line[:, k * piece : (k + 1) * piece] = got[k, :, 0:piece]
    added = sum(got[k] for k in range(n))
    line[:, width:] = jnp.where(lane == piece + 2, added, got[0])
    for e in range(out.shape[0]):
        out[e] = line[...]


def row_products(got, blocks, out):
    n = got.shape[0]
    width = got.shape[2] - LANES
    x, g = token_blocks(blocks)
    left = got[:, :, 0:width].reshape(8 * n, width)
    both = contract(left, jnp.concatenate([x, g], axis=1), 1, 0)
    out[...] = both.reshape(n, 8, 2 * LANES)


def logit_grads(near, blocks, got, done, keep, tops, out, mine, line):
    n = got.shape[0]
    width = got.shape[2] - LANES
    rows = width // n
    piece = width // 16
    core = core_index()
    x, g = token_blocks(blocks)
    left = near[:, :, 0:width].reshape(8 * n, width)
    other = contract(left, jnp.concatenate([x, g], axis=1), 1, 0).reshape(n, 8, 2 * LANES)

    def order(own, theirs):
        low = jnp.where(core == 0, own, theirs)
        high = jnp.where(core == 0, theirs, own)
        return jnp.concatenate([low, high], axis=0)

    both = order(done[...], other)
    marks = order(got[:, :, width:], near[:, :, width:])
    first = row_of((2 * n, 8, LANES)) < 4
    grads = jnp.where(first, both[:, :, LANES:], both[:, :, :LANES])
    top = marks[:, :, piece : piece + 1]
    total = marks[:, :, piece + 1 : piece + 2]
    column = marks[:, :, piece + 2 : piece + 3]
    held = keep[...]
    weights = jnp.where(first, held, held * (jnp.exp(tops[...] - top) / total))
    product = jnp.where(first, weights * grads, 0.0)
    sums = jnp.sum(jnp.sum(product, axis=0), axis=0, keepdims=True)
    part = weights * (grads - jnp.where(first, sums[None], column))
    part = part + swap(part)
    slots = 8 * n
    for c in range(2):
        for e in range(n):
            i, j = 8 * e + 4 * c, n * c + e
            line[i : i + 4] = part[j, 0:4]
            line[slots + i : slots + i + 4] = weights[j, 4:8]
    for e in range(n):
        out[e] = line[...]
    me = lax.axis_index(E)
    for b in range(n):

        @pl.when(me == b)
        def _():
            s = slice(b * rows, (b + 1) * rows)
            for c in range(2):
                for e in range(n):
                    i = 8 * e + 4 * c
                    mine[i : i + 4] = jnp.where(core == c, got[e, 4:8, s], near[e, 4:8, s])


def router_part(got, tokens, mine, theirs):
    n = got.shape[0]
    slots = got.shape[1] // 2
    grads = jnp.concatenate([got[e, 0:slots] for e in range(n)], axis=1)
    part = contract(tokens[...], grads, 1, 1)
    q = part.shape[0] // 4
    low = jnp.concatenate([part[0:q], part[q : 2 * q]], axis=1)
    high = jnp.concatenate([part[2 * q : 3 * q], part[3 * q :]], axis=1)
    core = core_index()
    mine[...] = jnp.where(core == 0, low, high)
    theirs[...] = jnp.where(core == 0, high, low)


def token_grads(got, rows, router, out):
    left = jnp.transpose(jnp.concatenate([router[...], rows[...]], axis=0))
    for e in range(got.shape[0]):
        out[:, e * LANES : (e + 1) * LANES] = contract(left, got[e], 1, 0)


def add_copies(mine, theirs, out):
    both = mine[...] + theirs[...]
    for k in range(out.shape[0]):
        out[k] = both


def add_all(got, out):
    out[...] = jnp.sum(got[...], axis=0)


def unfold(mine, theirs, out):
    core = core_index()
    a, b = mine[...], theirs[...]
    q, h = out.shape[1] // 4, LANES // 2
    for i, values in enumerate((jnp.where(core == 0, a, b), jnp.where(core == 0, b, a))):
        turned = jnp.transpose(values)
        out[:, 2 * i * q : (2 * i + 1) * q] = turned[:h]
        out[:, (2 * i + 1) * q : (2 * i + 2) * q] = turned[h:]


def weight_grads(full, near_full, keep, near_keep, grad_in, grad_out):
    w = grad_in.shape[1]
    hidden = grad_in.shape[2]
    core = core_index()
    step = 512
    for base, values, held in ((2 * core, full, keep), (2 - 2 * core, near_full, near_keep)):
        held = held[...]
        part = jnp.where(core == 0, held[:, 0:w], held[:, w : 2 * w])
        cols = jnp.transpose(part)
        for a in range(2):
            for h in range(0, hidden, step):
                s = slice(h, h + step)
                i, j = 2 * a, 2 * a + 1
                grad_out[base + a, :, s] = (
                    cols[:, 4 + i : 5 + i] * values[i : i + 1, s]
                    + cols[:, 4 + j : 5 + j] * values[j : j + 1, s]
                )
                grad_in[base + a, :, s] = (
                    cols[:, i : i + 1] * values[4 + i : 5 + i, s]
                    + cols[:, j : j + 1] * values[4 + j : 5 + j, s]
                )


def per_device(tokens, router, w_in, w_out, grad_out):
    n_seq, n_exp = lax.axis_size(S), lax.axis_size(E)
    experts, width_block, hidden = w_in.shape
    rows_block, local_tokens = tokens.shape
    slots = router.shape[1]
    width = rows_block * n_exp
    chips = n_seq // 2
    core = core_index()
    partner = [(i, i ^ 1) for i in range(n_seq)]
    groups = [[2 * k + c for k in range(chips)] for c in range(2)]
    turned = router.T

    def to_partner(values):
        return lax.ppermute(values, S, partner)

    any_spec = pl.BlockSpec(memory_space=pl.ANY)
    packed = pl.pallas_call(
        pack_tokens,
        out_shape=jax.ShapeDtypeStruct((n_exp, 2 * rows_block + slots, LANES), F32),
        in_specs=[any_spec, any_spec, pl.BlockSpec(memory_space=pltpu.VMEM)],
        out_specs=any_spec,
        scratch_shapes=[
            pltpu.VMEM(tokens.shape, F32),
            pltpu.VMEM((n_exp, slots, LANES), F32),
            pltpu.SemaphoreType.DMA,
            pltpu.SemaphoreType.DMA((2 * n_exp,)),
            pltpu.SemaphoreType.DMA((n_exp,)),
        ],
        compiler_params=pltpu.CompilerParams(vmem_limit_bytes=40 * 1024 * 1024),
    )(tokens, grad_out, turned)
    blocks = exchange(packed, E)
    half = experts // 2

    def split(w):
        own = lax.dynamic_slice_in_dim(w, half * core, half, 0)
        return own, to_partner(lax.dynamic_slice_in_dim(w, half * (1 - core), half, 0))

    own_in, near_in = split(w_in)
    own_out, near_out = split(w_out)
    blocks, own_in, own_out, near_in, near_out = lax.optimization_barrier(
        (blocks, own_in, own_out, near_in, near_out)
    )
    weights = (own_in, own_out, near_in, near_out)

    line = width + LANES
    groups8 = (slots // 4, 8, LANES)
    part = (n_exp, 8, line)
    mine, near, keep, tops = run(
        softmax_rows, [part, part, groups8, groups8], blocks, scratch=[(2,) + part]
    )
    sent = run(merge_cores, part, mine, to_partner(near))
    sent = run(merge_tokens, (chips, 8, LANES), exchange(sent, E))
    share = hidden // chips
    cut = -(-share // LANES) * LANES
    sent, held = run(
        hidden_parts,
        [(chips, 8, cut), (8, LANES)],
        exchange(sent, S, groups),
        *weights,
        scratch=[(8, hidden)],
    )
    sent = run(gate, (chips, 8, cut), exchange(sent, S, groups))
    sent, full = run(
        slot_rows, [(chips, 8, LANES), (8, hidden)], exchange(sent, S, groups), held, *weights
    )
    near_full = to_partner(full)
    near_held = to_partner(held)
    sent = run(join_widths, part, exchange(sent, S, groups), scratch=[(8, line)])
    got = exchange(sent, E)
    near = to_partner(got)
    done = run(row_products, (n_exp, 8, 2 * LANES), got, blocks)
    sent, mine = run(
        logit_grads,
        [(n_exp, 2 * slots, LANES), (slots, rows_block)],
        near,
        blocks,
        got,
        done,
        keep,
        tops,
        scratch=[(2 * slots, LANES)],
    )
    spread = exchange(sent, E)
    fold = (rows_block // 4, 2 * slots)
    near, theirs = run(router_part, [fold, fold], spread, tokens)
    sent = run(add_copies, (chips,) + fold, near, to_partner(theirs))
    sent, spread, full, near_full, near_held = lax.optimization_barrier(
        (sent, spread, full, near_full, near_held)
    )
    got = exchange(sent, S, groups)
    grad_w_in, grad_w_out = run(
        weight_grads, [w_in.shape, w_out.shape], full, near_full, held, near_held
    )
    grad_tokens = run(token_grads, (rows_block, local_tokens), spread, mine, turned)
    got, grad_w_in, grad_w_out, grad_tokens = lax.optimization_barrier(
        (got, grad_w_in, grad_w_out, grad_tokens)
    )
    near = run(add_all, fold, got)
    grad_router = run(unfold, (slots, rows_block), near, to_partner(near)).T
    return (grad_tokens, grad_router, grad_w_in, grad_w_out)


def solution(mesh):
    placed = (
        P("expert", "seq"),
        P("expert", None),
        P("expert", "seq", None),
        P("expert", "seq", None),
        P("expert", "seq"),
    )
    return jax.shard_map(
        per_device,
        mesh=mesh,
        in_specs=placed,
        out_specs=(
            P("expert", "seq"),
            P("expert", None),
            P("expert", "seq", None),
            P("expert", "seq", None),
        ),
        check_vma=False,
    )
```

```python
import functools

import jax
import jax.numpy as jnp
from jax import lax
from jax.experimental import pallas as pl
from jax.experimental.pallas import tpu as pltpu
from jax.sharding import PartitionSpec as P

HIGH = lax.Precision.HIGHEST
S = "seq"
E = "expert"
LANES = 128
F32 = jnp.float32


def contract(left, right, left_dim, right_dim, precision=HIGH):
    return lax.dot_general(
        left,
        right,
        (((left_dim,), (right_dim,)), ((), ())),
        precision=precision,
        preferred_element_type=F32,
    )


def exchange(blocks, axis, groups=None):
    return lax.all_to_all(blocks, axis, 0, 0, axis_index_groups=groups, tiled=True)


def run(kernel, shapes, *values, scratch=(), flops=0):
    single = not isinstance(shapes, list)
    shapes = [shapes] if single else shapes
    size = 4 * sum(v.size for v in values) + 4 * sum(functools.reduce(lambda a, b: a * b, s) for s in shapes)
    spec = pl.BlockSpec(memory_space=pltpu.VMEM)
    out = pl.pallas_call(
        kernel,
        out_shape=[jax.ShapeDtypeStruct(s, F32) for s in shapes],
        in_specs=[spec] * len(values),
        out_specs=[spec] * len(shapes),
        scratch_shapes=[pltpu.VMEM(s, F32) for s in scratch],
        compiler_params=pltpu.CompilerParams(vmem_limit_bytes=40 * 1024 * 1024),
        cost_estimate=pl.CostEstimate(flops=flops, bytes_accessed=size, transcendentals=0),
    )(*values)
    return out[0] if single else out


def row_of(shape):
    return lax.broadcasted_iota(jnp.int32, shape, len(shape) - 2) % 8


def lane_of(shape):
    return lax.broadcasted_iota(jnp.int32, shape, len(shape) - 1)


def swap(values):
    return jnp.concatenate([values[..., 4:8, :], values[..., 0:4, :]], axis=-2)


def core_index():
    return lax.axis_index(S) % 2


def seats(n):
    place = {}
    for b in range(2):
        for e in range(n):
            place[b, e] = (8 * b + 4 * (e >> 1 & 1) + 2 * (e & 1) + (e >> 2)) ^ 1
    return place


def logit_parts(router, tokens, out):
    part = contract(router[...], tokens[...], 1, 0)
    for i in range(out.shape[0]):
        out[i] = part[:, i * LANES : (i + 1) * LANES]


def add_spread(got, out, own):
    total = jnp.sum(got[...], axis=0)
    own[...] = total
    for e in range(out.shape[0]):
        out[e] = total


def partial_rows(got, tokens, grad_out, mine, near, both):
    n, slots = got.shape[0], got.shape[1]
    logits = jnp.concatenate([got[e] for e in range(n)], axis=1)
    raised = jnp.exp(logits - jnp.max(logits, axis=0, keepdims=True))
    combine = raised / jnp.sum(raised, axis=0, keepdims=True)
    top = jnp.max(logits, axis=1, keepdims=True)
    raised = jnp.exp(logits - top)
    total = jnp.sum(raised, axis=1, keepdims=True)
    rows_in = contract(raised, tokens[...], 1, 1)
    rows_out = contract(combine, grad_out[...], 1, 1)
    piece = rows_in.shape[1] // 2
    lane = lane_of((slots, LANES))
    marks = jnp.where(lane == piece, top, jnp.where(lane == piece + 1, total, 0.0))
    plain = jnp.where(lane_of((4, LANES)) == piece + 1, 1.0, 0.0)
    for (b, e), k in seats(n).items():
        for c in range(2):
            s, w = slice(8 * e + 4 * c, 8 * e + 4 * c + 4), slice(b * piece, (b + 1) * piece)
            both[c, k, 0:4] = marks[s]
            both[c, k, 4:8] = plain
            both[c, k, 0:4, 0:piece] = rows_in[s, w]
            both[c, k, 4:8, 0:piece] = rows_out[s, w]
    core = core_index()
    mine[...] = both[core]
    near[...] = both[1 - core]


def merge(parts, piece):
    top = functools.reduce(jnp.maximum, [p[:, piece : piece + 1] for p in parts])
    rows = sum(jnp.exp(p[:, piece : piece + 1] - top) * p for p in parts)
    return jnp.where(lane_of(rows.shape) == piece, top, rows)


def merge_cores(mine, near, out, piece):
    for k in range(out.shape[0]):
        out[k] = merge([mine[k], near[k]], piece)


def merge_chips(got, out, piece):
    out[...] = merge([got[k] for k in range(got.shape[0])], piece)


def hidden_parts(got, own_in, own_out, near_in, near_out, sent, keep, full):
    w = own_in.shape[1]
    piece = 2 * w
    hidden = own_in.shape[2]
    core = core_index()
    rows = got[...]
    scaled = (row_of((8, LANES)) < 4) & (lane_of((8, LANES)) < piece)
    rows = jnp.where(scaled, rows / rows[:, piece + 1 : piece + 2], rows)
    keep[...] = rows
    turned = jnp.transpose(rows)
    low, high = turned[0:w], turned[w:piece]
    own = jnp.where(core == 0, low, high)
    near = jnp.where(core == 0, high, low)
    for a in range(2):
        for kind, mine, theirs in ((0, own_in, near_in), (1, own_out, near_out)):
            r = 4 * kind + 2 * a
            values = [
                jnp.concatenate(
                    [
                        jnp.broadcast_to(own[:, r + p : r + p + 1], (w, LANES)),
                        jnp.broadcast_to(near[:, r + p : r + p + 1], (w, LANES)),
                    ],
                    axis=0,
                )
                for p in range(2)
            ]
            for h in range(0, hidden, LANES):
                s = slice(h, h + LANES)
                block = jnp.concatenate([mine[a, :, s], theirs[a, :, s]], axis=0)
                for p in range(2):
                    full[r + p : r + p + 1, s] = jnp.sum(block * values[p], axis=0, keepdims=True)
    chips = sent.shape[0]
    share = hidden // chips
    for k in range(chips):
        sent[k, :, 0:share] = full[:, k * share : (k + 1) * share]
        sent[k, :, share:] = jnp.zeros((8, sent.shape[2] - share), F32)


def gate(got, out):
    z = jnp.sum(got[...], axis=0)
    other = swap(z)
    first = row_of(z.shape) < 4
    pre = jnp.where(first, z, other)
    grad = jnp.where(first, other, z)
    c = 0.7978845608028654
    t = jnp.tanh(c * (pre + 0.044715 * (pre * pre * pre)))
    act = 0.5 * pre * (1.0 + t)
    slope = 0.5 * (1.0 + t) + 0.5 * pre * (1.0 - t * t) * (c * (1.0 + 3 * 0.044715 * (pre * pre)))
    both = jnp.where(first, act, grad * slope)
    for k in range(out.shape[0]):
        out[k] = both


def slot_rows(got, keep, own_in, own_out, near_in, near_out, out, full):
    w = own_in.shape[1]
    piece = 2 * w
    hidden = own_in.shape[2]
    chips = got.shape[0]
    share = hidden // chips
    core = core_index()
    for k in range(chips):
        full[:, k * share : (k + 1) * share] = got[k, :, 0:share]
    lane = lane_of((piece, LANES))
    cols = jnp.zeros((piece, LANES), F32)
    for a in range(2):
        for kind, mine, theirs in ((0, own_out, near_out), (1, own_in, near_in)):
            r = 4 * kind + 2 * a
            sums = [jnp.zeros((piece, LANES), F32) for _ in range(2)]
            for h in range(0, hidden, LANES):
                s = slice(h, h + LANES)
                block = jnp.concatenate([mine[a, :, s], theirs[a, :, s]], axis=0)
                for p in range(2):
                    sums[p] = sums[p] + block * full[r + p : r + p + 1, s]
            for p in range(2):
                cols = jnp.where(lane == r + p, jnp.sum(sums[p], axis=1, keepdims=True), cols)
    own, near = cols[0:w], cols[w:]
    low = jnp.where(core == 0, own, near)
    high = jnp.where(core == 0, near, own)
    square = jnp.concatenate([low, high, jnp.zeros((LANES - piece, LANES), F32)], axis=0)
    rows = jnp.transpose(square)[0:8]
    held = swap(keep[...])
    lane = lane_of((8, LANES))
    column = jnp.sum(jnp.where(lane < piece, held * rows, 0.0), axis=1, keepdims=True)
    out[...] = jnp.where(lane < piece, rows, jnp.where(lane == piece + 2, column, held))


def copies(tile, out):
    value = tile[...]
    for k in range(out.shape[0]):
        out[k] = value


def width_products(mine, near, tokens, grad_out, out, rows, marks, outs):
    n = out.shape[0]
    slots = rows.shape[0]
    piece = rows.shape[1] // 2
    core = core_index()
    added = []
    for c in range(2):
        for (b, e), k in seats(n).items():
            tile = jnp.where(core == c, mine[k], near[k])
            s, w = slice(8 * e + 4 * c, 8 * e + 4 * c + 4), slice(b * piece, (b + 1) * piece)
            outs[s, w] = tile[0:4, 0:piece]
            rows[s, w] = tile[4:8, 0:piece]
            if b == 0:
                marks[s] = tile[4:8]
            else:
                added.append((s, tile[4:8, piece + 2 : piece + 3]))
    lane = lane_of((4, LANES))
    for s, column in added:
        marks[s] = marks[s] + jnp.where(lane == piece + 2, column, 0.0)
    combine = contract(outs[...], grad_out[...], 1, 0)
    dispatch = contract(rows[...], tokens[...], 1, 0) - marks[:, piece + 2 : piece + 3]
    for i in range(n):
        s = slice(i * LANES, (i + 1) * LANES)
        out[i, 0:slots] = combine[:, s]
        out[i, slots:] = dispatch[:, s]


def logit_grads(got, own, marks, out, piece):
    slots = own.shape[0]
    total = jnp.sum(got[...], axis=0)
    logits = own[...]
    raised = jnp.exp(logits - jnp.max(logits, axis=0, keepdims=True))
    combine = raised / jnp.sum(raised, axis=0, keepdims=True)
    dispatch = jnp.exp(logits - marks[:, piece : piece + 1]) / marks[:, piece + 1 : piece + 2]
    first, second = total[:slots], total[slots:]
    grads = combine * (first - jnp.sum(combine * first, axis=0, keepdims=True)) + dispatch * second
    for e in range(out.shape[0]):
        out[e] = grads


def router_part(got, tokens, mine, theirs):
    n = got.shape[0]
    grads = jnp.concatenate([got[e] for e in range(n)], axis=1)
    part = contract(tokens[...], grads, 1, 1)
    q = part.shape[0] // 4
    low = jnp.concatenate([part[0:q], part[q : 2 * q]], axis=1)
    high = jnp.concatenate([part[2 * q : 3 * q], part[3 * q :]], axis=1)
    core = core_index()
    mine[...] = jnp.where(core == 0, low, high)
    theirs[...] = jnp.where(core == 0, high, low)


def token_grads(got, logits, rows, marks, router, out, piece):
    left = jnp.transpose(jnp.concatenate([router[...], rows[...]], axis=0))
    top, total = marks[:, piece : piece + 1], marks[:, piece + 1 : piece + 2]
    for e in range(got.shape[0]):
        dispatch = jnp.exp(logits[e] - top) / total
        right = jnp.concatenate([got[e], dispatch], axis=0)
        out[:, e * LANES : (e + 1) * LANES] = contract(left, right, 1, 0)


def add_copies(mine, theirs, out):
    both = mine[...] + theirs[...]
    for k in range(out.shape[0]):
        out[k] = both


def add_all(got, out):
    out[...] = jnp.sum(got[...], axis=0)


def unfold(mine, theirs, out):
    core = core_index()
    a, b = mine[...], theirs[...]
    q, h = out.shape[1] // 4, LANES // 2
    for i, values in enumerate((jnp.where(core == 0, a, b), jnp.where(core == 0, b, a))):
        turned = jnp.transpose(values)
        out[:, 2 * i * q : (2 * i + 1) * q] = turned[:h]
        out[:, (2 * i + 1) * q : (2 * i + 2) * q] = turned[h:]


def weight_grads(full, near_full, keep, near_keep, grad_in, grad_out):
    w = grad_in.shape[1]
    hidden = grad_in.shape[2]
    core = core_index()
    step = 512
    for base, values, held in ((2 * core, full, keep), (2 - 2 * core, near_full, near_keep)):
        held = held[...]
        part = jnp.where(core == 0, held[:, 0:w], held[:, w : 2 * w])
        cols = jnp.transpose(part)
        for a in range(2):
            for h in range(0, hidden, step):
                s = slice(h, h + step)
                i, j = 2 * a, 2 * a + 1
                grad_out[base + a, :, s] = (
                    cols[:, 4 + i : 5 + i] * values[i : i + 1, s]
                    + cols[:, 4 + j : 5 + j] * values[j : j + 1, s]
                )
                grad_in[base + a, :, s] = (
                    cols[:, i : i + 1] * values[4 + i : 5 + i, s]
                    + cols[:, j : j + 1] * values[4 + j : 5 + j, s]
                )


def per_device(tokens, router, w_in, w_out, grad_out):
    n_seq, n_exp = lax.axis_size(S), lax.axis_size(E)
    experts, width_block, hidden = w_in.shape
    rows_block, local_tokens = tokens.shape
    slots = router.shape[1]
    chips = n_seq // 2
    piece = 2 * width_block
    core = core_index()
    partner = [(i, i ^ 1) for i in range(n_seq)]
    groups = [[2 * k + c for k in range(chips)] for c in range(2)]
    turned = router.T
    to_owner = [
        ((2 * k + c) * n_exp + f, (2 * (2 * f + b) + c) * n_exp + e)
        for (b, e), k in seats(n_exp).items()
        for c in range(2)
        for f in range(n_exp)
    ]
    from_owner = [(there, here) for here, there in to_owner]

    def to_partner(values):
        return lax.ppermute(values, S, partner)

    sent = run(logit_parts, (n_exp, slots, LANES), turned, tokens)
    sent, own = run(
        add_spread, [(n_exp, slots, LANES), (slots, LANES)], exchange(sent, E)
    )
    logits = exchange(sent, E)
    half = experts // 2

    def split(w):
        own = lax.dynamic_slice_in_dim(w, half * core, half, 0)
        return own, to_partner(lax.dynamic_slice_in_dim(w, half * (1 - core), half, 0))

    own_in, near_in = split(w_in)
    own_out, near_out = split(w_out)
    logits, own_in, own_out, near_in, near_out = lax.optimization_barrier(
        (logits, own_in, own_out, near_in, near_out)
    )
    weights = (own_in, own_out, near_in, near_out)

    tiles = (chips, 8, LANES)
    mine, near = run(
        partial_rows, [tiles, tiles], logits, tokens, grad_out, scratch=[(2,) + tiles]
    )
    sent = run(functools.partial(merge_cores, piece=piece), tiles, mine, to_partner(near))
    tile = run(
        functools.partial(merge_chips, piece=piece), (8, LANES), exchange(sent, S, groups)
    )
    share = hidden // chips
    cut = -(-share // LANES) * LANES
    sent, held = run(
        hidden_parts,
        [(chips, 8, cut), (8, LANES)],
        lax.ppermute(tile, (S, E), to_owner),
        *weights,
        scratch=[(8, hidden)],
    )
    sent = run(gate, (chips, 8, cut), exchange(sent, S, groups))
    tile, full = run(
        slot_rows, [(8, LANES), (8, hidden)], exchange(sent, S, groups), held, *weights
    )
    sent = run(copies, tiles, lax.ppermute(tile, (S, E), from_owner))
    mine = exchange(sent, S, groups)
    near = to_partner(mine)
    sent, rows, marks = run(
        width_products,
        [(n_exp, 2 * slots, LANES), (slots, rows_block), (slots, LANES)],
        mine,
        near,
        tokens,
        grad_out,
        scratch=[(slots, rows_block)],
    )
    sent = run(
        functools.partial(logit_grads, piece=piece),
        (n_exp, slots, LANES),
        exchange(sent, E),
        own,
        marks,
    )
    grads = exchange(sent, E)
    fold = (rows_block // 4, 2 * slots)
    near, theirs = run(router_part, [fold, fold], grads, tokens)
    sent = run(add_copies, (chips,) + fold, near, to_partner(theirs))
    near_full = to_partner(full)
    near_held = to_partner(held)
    sent, grads, full, near_full, near_held = lax.optimization_barrier(
        (sent, grads, full, near_full, near_held)
    )
    got = exchange(sent, S, groups)
    grad_w_in, grad_w_out = run(
        weight_grads, [w_in.shape, w_out.shape], full, near_full, held, near_held
    )
    grad_tokens = run(
        functools.partial(token_grads, piece=piece),
        (rows_block, local_tokens),
        grads,
        logits,
        rows,
        marks,
        turned,
    )
    got, grad_w_in, grad_w_out, grad_tokens = lax.optimization_barrier(
        (got, grad_w_in, grad_w_out, grad_tokens)
    )
    near = run(add_all, fold, got)
    grad_router = run(unfold, (slots, rows_block), near, to_partner(near)).T
    return (grad_tokens, grad_router, grad_w_in, grad_w_out)


def solution(mesh):
    placed = (
        P("expert", "seq"),
        P("expert", None),
        P("expert", "seq", None),
        P("expert", "seq", None),
        P("expert", "seq"),
    )
    return jax.shard_map(
        per_device,
        mesh=mesh,
        in_specs=placed,
        out_specs=(
            P("expert", "seq"),
            P("expert", None),
            P("expert", "seq", None),
            P("expert", "seq", None),
        ),
        check_vma=False,
    )
```

```python
import functools

import jax
import jax.numpy as jnp
from jax import lax
from jax.experimental import pallas as pl
from jax.experimental.pallas import tpu as pltpu
from jax.sharding import PartitionSpec as P

FULL = lax.Precision.HIGHEST
THREE = lax.Precision.HIGH
S = "seq"
E = "expert"
LANES = 128
F32 = jnp.float32


def contract(left, right, left_dim, right_dim, precision=FULL):
    return lax.dot_general(
        left,
        right,
        (((left_dim,), (right_dim,)), ((), ())),
        precision=precision,
        preferred_element_type=F32,
    )


def exchange(blocks, axis, groups=None):
    return lax.all_to_all(blocks, axis, 0, 0, axis_index_groups=groups, tiled=True)


def run(kernel, shapes, *values, scratch=(), flops=0):
    single = not isinstance(shapes, list)
    shapes = [shapes] if single else shapes
    size = 4 * sum(v.size for v in values) + 4 * sum(functools.reduce(lambda a, b: a * b, s) for s in shapes)
    spec = pl.BlockSpec(memory_space=pltpu.VMEM)
    out = pl.pallas_call(
        kernel,
        out_shape=[jax.ShapeDtypeStruct(s, F32) for s in shapes],
        in_specs=[spec] * len(values),
        out_specs=[spec] * len(shapes),
        scratch_shapes=[pltpu.VMEM(s, F32) for s in scratch],
        compiler_params=pltpu.CompilerParams(vmem_limit_bytes=40 * 1024 * 1024),
        cost_estimate=pl.CostEstimate(flops=flops, bytes_accessed=size, transcendentals=0),
    )(*values)
    return out[0] if single else out


def row_of(shape):
    return lax.broadcasted_iota(jnp.int32, shape, len(shape) - 2) % 8


def lane_of(shape):
    return lax.broadcasted_iota(jnp.int32, shape, len(shape) - 1)


def swap(values):
    return jnp.concatenate([values[..., 4:8, :], values[..., 0:4, :]], axis=-2)


def core_index():
    return lax.axis_index(S) % 2


SEATS = (0xE680F7D5, 0xB291A3C4)


def seat(b, e, column):
    index = 2 * (((e >> 1) - (column >> 1)) & 3) + ((e ^ column) & 1)
    if isinstance(column, int):
        value = SEATS[b] >> (4 * index) & 15
    else:
        word = SEATS[b] - (1 << 32 if SEATS[b] >> 31 else 0)
        value = lax.shift_right_logical(jnp.int32(word), 4 * index) & 15
    return (((value >> 3) ^ (column >> 2)) << 3) | (((value & 7) + 2 * (column & 3)) & 7)


def seats(n):
    column = lax.axis_index(E)
    return [(b, e, seat(b, e, column)) for b in range(2) for e in range(n)]


def logit_parts(router, tokens, out, left, right, sems):
    n = right.shape[0]
    cut = right.shape[2]
    copies = [pltpu.make_async_copy(router, left, sems.at[n])]
    for i in range(n):
        block = tokens.at[:, pl.ds(i * cut, cut)]
        copies.append(pltpu.make_async_copy(block, right.at[i], sems.at[i]))
    for copy in copies:
        copy.start()
    copies[0].wait()
    for i in range(n):
        copies[i + 1].wait()
        part = contract(left[...], right[i], 1, 0)
        for j in range(cut // LANES):
            out[i * (cut // LANES) + j] = part[:, j * LANES : (j + 1) * LANES]


def split_weights(w_in, w_out, own_in, own_out, far_in, far_out, sems):
    core = core_index()
    half = own_in.shape[0]
    copies = []
    for i, (whole, own, far) in enumerate(((w_in, own_in, far_in), (w_out, own_out, far_out))):
        for j, (part, place) in enumerate(((far, 1 - core), (own, core))):
            block = whole.at[pl.ds(half * place, half)]
            copies.append(pltpu.make_async_copy(block, part, sems.at[2 * i + j]))
    for copy in copies:
        copy.start()
    for copy in copies:
        copy.wait()


def add_spread(got, out):
    total = jnp.sum(got[...], axis=0)
    for e in range(out.shape[0]):
        out[e] = total


def partial_rows(got, tokens, grad_out, mine, near, shares, both):
    n, slots = got.shape[0], got.shape[1]
    logits = jnp.concatenate([got[e] for e in range(n)], axis=1)
    raised = jnp.exp(logits - jnp.max(logits, axis=0, keepdims=True))
    combine = raised / jnp.sum(raised, axis=0, keepdims=True)
    shares[...] = combine
    top = jnp.max(logits, axis=1, keepdims=True)
    raised = jnp.exp(logits - top)
    total = jnp.sum(raised, axis=1, keepdims=True)
    rows_in = contract(raised, tokens[...], 1, 1)
    rows_out = contract(combine, grad_out[...], 1, 1, THREE)
    piece = rows_in.shape[1] // 2
    lane = lane_of((slots, LANES))
    marks = jnp.where(lane == piece, top, jnp.where(lane == piece + 1, total, 0.0))
    plain = jnp.where(lane_of((4, LANES)) == piece + 1, 1.0, 0.0)
    for b, e, k in seats(n):
        for c in range(2):
            s, w = slice(8 * e + 4 * c, 8 * e + 4 * c + 4), slice(b * piece, (b + 1) * piece)
            both[c, k, 0:4] = marks[s]
            both[c, k, 4:8] = plain
            both[c, k, 0:4, 0:piece] = rows_in[s, w]
            both[c, k, 4:8, 0:piece] = rows_out[s, w]
    core = core_index()
    mine[...] = both[core]
    near[...] = both[1 - core]


def merge(parts, piece):
    top = functools.reduce(jnp.maximum, [p[:, piece : piece + 1] for p in parts])
    rows = sum(jnp.exp(p[:, piece : piece + 1] - top) * p for p in parts)
    return jnp.where(lane_of(rows.shape) == piece, top, rows)


def merge_cores(mine, near, out, piece):
    for k in range(out.shape[0]):
        out[k] = merge([mine[k], near[k]], piece)


def merge_chips(got, out, piece):
    out[...] = merge([got[k] for k in range(got.shape[0])], piece)


def hidden_parts(got, own_in, own_out, near_in, near_out, sent, keep, full):
    w = own_in.shape[1]
    piece = 2 * w
    hidden = own_in.shape[2]
    core = core_index()
    rows = got[...]
    scaled = (row_of((8, LANES)) < 4) & (lane_of((8, LANES)) < piece)
    rows = jnp.where(scaled, rows / rows[:, piece + 1 : piece + 2], rows)
    keep[...] = rows
    turned = jnp.transpose(rows)
    low, high = turned[0:w], turned[w:piece]
    own = jnp.where(core == 0, low, high)
    near = jnp.where(core == 0, high, low)
    for a in range(2):
        for kind, mine, theirs in ((0, own_in, near_in), (1, own_out, near_out)):
            r = 4 * kind + 2 * a
            values = [
                jnp.concatenate(
                    [
                        jnp.broadcast_to(own[:, r + p : r + p + 1], (w, LANES)),
                        jnp.broadcast_to(near[:, r + p : r + p + 1], (w, LANES)),
                    ],
                    axis=0,
                )
                for p in range(2)
            ]
            for h in range(0, hidden, LANES):
                s = slice(h, h + LANES)
                block = jnp.concatenate([mine[a, :, s], theirs[a, :, s]], axis=0)
                for p in range(2):
                    full[r + p : r + p + 1, s] = jnp.sum(block * values[p], axis=0, keepdims=True)
    chips = sent.shape[0]
    share = hidden // chips
    for k in range(chips):
        sent[k, :, 0:share] = full[:, k * share : (k + 1) * share]
        sent[k, :, share:] = jnp.zeros((8, sent.shape[2] - share), F32)


def gate(got, out):
    z = jnp.sum(got[...], axis=0)
    other = swap(z)
    first = row_of(z.shape) < 4
    pre = jnp.where(first, z, other)
    grad = jnp.where(first, other, z)
    c = 0.7978845608028654
    t = jnp.tanh(c * (pre + 0.044715 * (pre * pre * pre)))
    act = 0.5 * pre * (1.0 + t)
    slope = 0.5 * (1.0 + t) + 0.5 * pre * (1.0 - t * t) * (c * (1.0 + 3 * 0.044715 * (pre * pre)))
    both = jnp.where(first, act, grad * slope)
    for k in range(out.shape[0]):
        out[k] = both


def slot_rows(got, keep, own_in, own_out, near_in, near_out, out, full):
    w = own_in.shape[1]
    piece = 2 * w
    hidden = own_in.shape[2]
    chips = got.shape[0]
    share = hidden // chips
    core = core_index()
    for k in range(chips):
        full[:, k * share : (k + 1) * share] = got[k, :, 0:share]
    lane = lane_of((piece, LANES))
    cols = jnp.zeros((piece, LANES), F32)
    for a in range(2):
        for kind, mine, theirs in ((0, own_out, near_out), (1, own_in, near_in)):
            r = 4 * kind + 2 * a
            sums = [jnp.zeros((piece, LANES), F32) for _ in range(2)]
            for h in range(0, hidden, LANES):
                s = slice(h, h + LANES)
                block = jnp.concatenate([mine[a, :, s], theirs[a, :, s]], axis=0)
                for p in range(2):
                    sums[p] = sums[p] + block * full[r + p : r + p + 1, s]
            for p in range(2):
                cols = jnp.where(lane == r + p, jnp.sum(sums[p], axis=1, keepdims=True), cols)
    own, near = cols[0:w], cols[w:]
    low = jnp.where(core == 0, own, near)
    high = jnp.where(core == 0, near, own)
    square = jnp.concatenate([low, high, jnp.zeros((LANES - piece, LANES), F32)], axis=0)
    rows = jnp.transpose(square)[0:8]
    held = swap(keep[...])
    lane = lane_of((8, LANES))
    column = jnp.sum(jnp.where(lane < piece, held * rows, 0.0), axis=1, keepdims=True)
    out[...] = jnp.where(lane < piece, rows, jnp.where(lane == piece + 2, column, held))


def copies(tile, out):
    value = tile[...]
    for k in range(out.shape[0]):
        out[k] = value


def width_products(mine, near, tokens, grad_out, logits, shares, out, weights, rows, outs, marks):
    n = out.shape[0]
    piece = rows.shape[1] // 2
    core = core_index()
    added = []
    for c in range(2):
        for b, e, k in seats(n):
            tile = jnp.where(core == c, mine[k], near[k])
            s, w = slice(8 * e + 4 * c, 8 * e + 4 * c + 4), slice(b * piece, (b + 1) * piece)
            outs[s, w] = tile[0:4, 0:piece]
            rows[s, w] = tile[4:8, 0:piece]
            if b == 0:
                marks[s] = tile[4:8]
            else:
                added.append((s, tile[4:8, piece + 2 : piece + 3]))
    lane = lane_of((4, LANES))
    for s, column in added:
        marks[s] = marks[s] + jnp.where(lane == piece + 2, column, 0.0)
    top, total, column = (marks[:, piece + i : piece + i + 1] for i in range(3))
    first = contract(outs[...], grad_out[...], 1, 0, THREE)
    second = contract(rows[...], tokens[...], 1, 0) - column
    for i in range(n):
        s = slice(i * LANES, (i + 1) * LANES)
        combine = shares[:, s]
        dispatch = jnp.exp(logits[i] - top) / total
        weights[i] = dispatch
        part = combine * first[:, s]
        line = jnp.sum(part, axis=0, keepdims=True)
        out[i] = part - combine * line + dispatch * second[:, s]


def router_part(got, tokens, mine, theirs):
    n = got.shape[0]
    grads = jnp.concatenate([got[e] for e in range(n)], axis=1)
    part = contract(tokens[...], grads, 1, 1, THREE)
    q = part.shape[0] // 4
    low = jnp.concatenate([part[0:q], part[q : 2 * q]], axis=1)
    high = jnp.concatenate([part[2 * q : 3 * q], part[3 * q :]], axis=1)
    core = core_index()
    mine[...] = jnp.where(core == 0, low, high)
    theirs[...] = jnp.where(core == 0, high, low)


def token_grads(got, weights, rows, router, out):
    left = jnp.transpose(jnp.concatenate([router[...], rows[...]], axis=0))
    for e in range(got.shape[0]):
        right = jnp.concatenate([got[e], weights[e]], axis=0)
        out[:, e * LANES : (e + 1) * LANES] = contract(left, right, 1, 0, THREE)


def add_copies(mine, theirs, out):
    both = mine[...] + theirs[...]
    for k in range(out.shape[0]):
        out[k] = both


def add_all(got, out):
    out[...] = jnp.sum(got[...], axis=0)


def unfold(mine, theirs, out):
    core = core_index()
    a, b = mine[...], theirs[...]
    q, h = out.shape[1] // 4, LANES // 2
    for i, values in enumerate((jnp.where(core == 0, a, b), jnp.where(core == 0, b, a))):
        turned = jnp.transpose(values)
        out[:, 2 * i * q : (2 * i + 1) * q] = turned[:h]
        out[:, (2 * i + 1) * q : (2 * i + 2) * q] = turned[h:]


def weight_grads(full, near_full, keep, near_keep, grad_in, grad_out):
    w = grad_in.shape[1]
    hidden = grad_in.shape[2]
    core = core_index()
    step = 512
    for base, values, held in ((2 * core, full, keep), (2 - 2 * core, near_full, near_keep)):
        held = held[...]
        part = jnp.where(core == 0, held[:, 0:w], held[:, w : 2 * w])
        cols = jnp.transpose(part)
        for a in range(2):
            for h in range(0, hidden, step):
                s = slice(h, h + step)
                i, j = 2 * a, 2 * a + 1
                grad_out[base + a, :, s] = (
                    cols[:, 4 + i : 5 + i] * values[i : i + 1, s]
                    + cols[:, 4 + j : 5 + j] * values[j : j + 1, s]
                )
                grad_in[base + a, :, s] = (
                    cols[:, i : i + 1] * values[4 + i : 5 + i, s]
                    + cols[:, j : j + 1] * values[4 + j : 5 + j, s]
                )


def per_device(tokens, router, w_in, w_out, grad_out):
    n_seq, n_exp = lax.axis_size(S), lax.axis_size(E)
    experts, width_block, hidden = w_in.shape
    rows_block, local_tokens = tokens.shape
    slots = router.shape[1]
    chips = n_seq // 2
    piece = 2 * width_block
    core = core_index()
    partner = [(i, i ^ 1) for i in range(n_seq)]
    groups = [[2 * k + c for k in range(chips)] for c in range(2)]
    turned = router.T
    spread = (n_exp, slots, LANES)
    to_owner = [
        ((2 * seat(b, e, f) + c) * n_exp + f, (2 * (2 * f + b) + c) * n_exp + e)
        for b in range(2)
        for e in range(n_exp)
        for c in range(2)
        for f in range(n_exp)
    ]
    from_owner = [(there, here) for here, there in to_owner]

    def to_partner(values):
        return lax.ppermute(values, S, partner)

    any_spec = pl.BlockSpec(memory_space=pl.ANY)
    vmem_spec = pl.BlockSpec(memory_space=pltpu.VMEM)
    limit = pltpu.CompilerParams(vmem_limit_bytes=40 * 1024 * 1024)
    sent = pl.pallas_call(
        logit_parts,
        out_shape=jax.ShapeDtypeStruct(spread, F32),
        in_specs=[any_spec, any_spec],
        out_specs=vmem_spec,
        scratch_shapes=[
            pltpu.VMEM(turned.shape, F32),
            pltpu.VMEM((4, rows_block, local_tokens // 4), F32),
            pltpu.SemaphoreType.DMA((5,)),
        ],
        compiler_params=pltpu.CompilerParams(vmem_limit_bytes=60 * 1024 * 1024),
    )(turned, tokens)
    sent = run(add_spread, spread, exchange(sent, E))
    sent, w_in, w_out = lax.optimization_barrier((sent, w_in, w_out))
    logits = exchange(sent, E)
    half = (experts // 2,) + w_in.shape[1:]
    own_in, own_out, far_in, far_out = pl.pallas_call(
        split_weights,
        out_shape=[jax.ShapeDtypeStruct(half, F32)] * 4,
        in_specs=[any_spec, any_spec],
        out_specs=[vmem_spec, vmem_spec, any_spec, any_spec],
        scratch_shapes=[pltpu.SemaphoreType.DMA((4,))],
        compiler_params=limit,
    )(w_in, w_out)
    logits, own_in, own_out, far_in, far_out = lax.optimization_barrier(
        (logits, own_in, own_out, far_in, far_out)
    )
    weights = (own_in, own_out, to_partner(far_in), to_partner(far_out))

    tiles = (chips, 8, LANES)
    mine, near, shares = run(
        partial_rows,
        [tiles, tiles, (slots, local_tokens)],
        logits,
        tokens,
        grad_out,
        scratch=[(2,) + tiles],
    )
    sent = run(functools.partial(merge_cores, piece=piece), tiles, mine, to_partner(near))
    tile = run(
        functools.partial(merge_chips, piece=piece), (8, LANES), exchange(sent, S, groups)
    )
    share = hidden // chips
    cut = -(-share // LANES) * LANES
    sent, held = run(
        hidden_parts,
        [(chips, 8, cut), (8, LANES)],
        lax.ppermute(tile, (S, E), to_owner),
        *weights,
        scratch=[(8, hidden)],
    )
    sent = run(gate, (chips, 8, cut), exchange(sent, S, groups))
    tile, full = run(
        slot_rows, [(8, LANES), (8, hidden)], exchange(sent, S, groups), held, *weights
    )
    sent = run(copies, tiles, lax.ppermute(tile, (S, E), from_owner))
    mine = exchange(sent, S, groups)
    near = to_partner(mine)
    sent, weights, rows = run(
        width_products,
        [spread, spread, (slots, rows_block)],
        mine,
        near,
        tokens,
        grad_out,
        logits,
        shares,
        scratch=[(slots, rows_block), (slots, LANES)],
    )
    sent = run(add_spread, spread, exchange(sent, E))
    sent, full, held = lax.optimization_barrier((sent, full, held))
    grads = exchange(sent, E)
    grad_w_in, grad_w_out = run(
        weight_grads,
        [w_in.shape, w_out.shape],
        full,
        to_partner(full),
        held,
        to_partner(held),
    )
    grads, grad_w_in, grad_w_out = lax.optimization_barrier((grads, grad_w_in, grad_w_out))
    fold = (rows_block // 4, 2 * slots)
    near, theirs = run(router_part, [fold, fold], grads, tokens)
    sent = run(add_copies, (chips,) + fold, near, to_partner(theirs))
    got, weights, rows = lax.optimization_barrier((exchange(sent, S, groups), weights, rows))
    near = run(add_all, fold, got)
    grad_tokens = run(
        token_grads, (rows_block, local_tokens), grads, weights, rows, turned
    )
    grad_router = run(unfold, (slots, rows_block), near, to_partner(near)).T
    return (grad_tokens, grad_router, grad_w_in, grad_w_out)


def solution(mesh):
    placed = (
        P("expert", "seq"),
        P("expert", None),
        P("expert", "seq", None),
        P("expert", "seq", None),
        P("expert", "seq"),
    )
    return jax.shard_map(
        per_device,
        mesh=mesh,
        in_specs=placed,
        out_specs=(
            P("expert", "seq"),
            P("expert", None),
            P("expert", "seq", None),
            P("expert", "seq", None),
        ),
        check_vma=False,
    )
```

```python
import functools

import jax
import jax.numpy as jnp
from jax import lax
from jax.experimental import pallas as pl
from jax.experimental.pallas import tpu as pltpu
from jax.sharding import PartitionSpec as P

FULL = lax.Precision.HIGHEST
THREE = lax.Precision.HIGH
S = "seq"
E = "expert"
LANES = 128
F32 = jnp.float32


def contract(left, right, left_dim, right_dim, precision=FULL):
    return lax.dot_general(
        left,
        right,
        (((left_dim,), (right_dim,)), ((), ())),
        precision=precision,
        preferred_element_type=F32,
    )


def exchange(blocks, axis, groups=None):
    return lax.all_to_all(blocks, axis, 0, 0, axis_index_groups=groups, tiled=True)


def run(kernel, shapes, *values, scratch=(), flops=0):
    single = not isinstance(shapes, list)
    shapes = [shapes] if single else shapes
    size = 4 * sum(v.size for v in values) + 4 * sum(functools.reduce(lambda a, b: a * b, s) for s in shapes)
    spec = pl.BlockSpec(memory_space=pltpu.VMEM)
    out = pl.pallas_call(
        kernel,
        out_shape=[jax.ShapeDtypeStruct(s, F32) for s in shapes],
        in_specs=[spec] * len(values),
        out_specs=[spec] * len(shapes),
        scratch_shapes=[pltpu.VMEM(s, F32) for s in scratch],
        compiler_params=pltpu.CompilerParams(vmem_limit_bytes=40 * 1024 * 1024),
        cost_estimate=pl.CostEstimate(flops=flops, bytes_accessed=size, transcendentals=0),
    )(*values)
    return out[0] if single else out


def row_of(shape):
    return lax.broadcasted_iota(jnp.int32, shape, len(shape) - 2) % 8


def lane_of(shape):
    return lax.broadcasted_iota(jnp.int32, shape, len(shape) - 1)


def swap(values):
    return jnp.concatenate([values[..., 4:8, :], values[..., 0:4, :]], axis=-2)


def core_index():
    return lax.axis_index(S) % 2


SEATS = (0xE680F7D5, 0xB291A3C4)


def seat(b, e, column):
    index = 2 * (((e >> 1) - (column >> 1)) & 3) + ((e ^ column) & 1)
    if isinstance(column, int):
        value = SEATS[b] >> (4 * index) & 15
    else:
        word = SEATS[b] - (1 << 32 if SEATS[b] >> 31 else 0)
        value = lax.shift_right_logical(jnp.int32(word), 4 * index) & 15
    return (((value >> 3) ^ (column >> 2)) << 3) | (((value & 7) + 2 * (column & 3)) & 7)


def seats(n):
    column = lax.axis_index(E)
    return [(b, e, seat(b, e, column)) for b in range(2) for e in range(n)]


def logit_parts(router, tokens, out, left, right, parts, sems, stores):
    n, _, cut = right.shape
    each = cut // LANES
    copies = [pltpu.make_async_copy(router, left, sems.at[n])]
    for i in range(n):
        block = tokens.at[:, pl.ds(i * cut, cut)]
        copies.append(pltpu.make_async_copy(block, right.at[i], sems.at[i]))
    for copy in copies:
        copy.start()
    copies[0].wait()
    moves = []
    for i in range(n):
        copies[i + 1].wait()
        part = contract(left[...], right[i], 1, 0)
        for j in range(each):
            parts[i * each + j] = part[:, j * LANES : (j + 1) * LANES]
        s = pl.ds(i * each, each)
        moves.append(pltpu.make_async_copy(parts.at[s], out.at[s], stores.at[i]))
        moves[i].start()
    for move in moves:
        move.wait()


def stage(w_in, w_out, tokens, grad_out, far_in, far_out, own_in, own_out, x, g, sems):
    core = core_index()
    half = own_in.shape[0]
    pairs = [(tokens, x), (grad_out, g)]
    for whole, own, far in ((w_in, own_in, far_in), (w_out, own_out, far_out)):
        pairs.append((whole.at[pl.ds(half * (1 - core), half)], far))
        pairs.append((whole.at[pl.ds(half * core, half)], own))
    copies = [pltpu.make_async_copy(a, b, sems.at[i]) for i, (a, b) in enumerate(pairs)]
    for copy in copies:
        copy.start()
    for copy in copies:
        copy.wait()


def add_spread(got, out):
    total = jnp.sum(got[...], axis=0)
    for e in range(out.shape[0]):
        out[e] = total


def partial_rows(got, tokens, grad_out, mine, near, shares, both):
    n, slots = got.shape[0], got.shape[1]
    logits = jnp.concatenate([got[e] for e in range(n)], axis=1)
    raised = jnp.exp(logits - jnp.max(logits, axis=0, keepdims=True))
    combine = raised / jnp.sum(raised, axis=0, keepdims=True)
    shares[...] = combine
    top = jnp.max(logits, axis=1, keepdims=True)
    raised = jnp.exp(logits - top)
    total = jnp.sum(raised, axis=1, keepdims=True)
    rows_in = contract(raised, tokens[...], 1, 1)
    rows_out = contract(combine, grad_out[...], 1, 1, THREE)
    piece = rows_in.shape[1] // 2
    lane = lane_of((slots, LANES))
    marks = jnp.where(lane == piece, top, jnp.where(lane == piece + 1, total, 0.0))
    plain = jnp.where(lane_of((4, LANES)) == piece + 1, 1.0, 0.0)
    for b, e, k in seats(n):
        for c in range(2):
            s, w = slice(8 * e + 4 * c, 8 * e + 4 * c + 4), slice(b * piece, (b + 1) * piece)
            both[c, k, 0:4] = marks[s]
            both[c, k, 4:8] = plain
            both[c, k, 0:4, 0:piece] = rows_in[s, w]
            both[c, k, 4:8, 0:piece] = rows_out[s, w]
    core = core_index()
    mine[...] = both[core]
    near[...] = both[1 - core]


def merge(parts, piece):
    top = functools.reduce(jnp.maximum, [p[:, piece : piece + 1] for p in parts])
    rows = sum(jnp.exp(p[:, piece : piece + 1] - top) * p for p in parts)
    return jnp.where(lane_of(rows.shape) == piece, top, rows)


def merge_cores(mine, near, out, piece):
    for k in range(out.shape[0]):
        out[k] = merge([mine[k], near[k]], piece)


def merge_chips(got, out, piece):
    out[...] = merge([got[k] for k in range(got.shape[0])], piece)


def hidden_parts(got, own_in, own_out, near_in, near_out, sent, keep, full):
    w = own_in.shape[1]
    piece = 2 * w
    hidden = own_in.shape[2]
    core = core_index()
    rows = got[...]
    scaled = (row_of((8, LANES)) < 4) & (lane_of((8, LANES)) < piece)
    rows = jnp.where(scaled, rows / rows[:, piece + 1 : piece + 2], rows)
    keep[...] = rows
    turned = jnp.transpose(rows)
    low, high = turned[0:w], turned[w:piece]
    own = jnp.where(core == 0, low, high)
    near = jnp.where(core == 0, high, low)
    for a in range(2):
        for kind, mine, theirs in ((0, own_in, near_in), (1, own_out, near_out)):
            r = 4 * kind + 2 * a
            values = [
                jnp.concatenate(
                    [
                        jnp.broadcast_to(own[:, r + p : r + p + 1], (w, LANES)),
                        jnp.broadcast_to(near[:, r + p : r + p + 1], (w, LANES)),
                    ],
                    axis=0,
                )
                for p in range(2)
            ]
            for h in range(0, hidden, LANES):
                s = slice(h, h + LANES)
                block = jnp.concatenate([mine[a, :, s], theirs[a, :, s]], axis=0)
                for p in range(2):
                    full[r + p : r + p + 1, s] = jnp.sum(block * values[p], axis=0, keepdims=True)
    chips = sent.shape[0]
    share = hidden // chips
    for k in range(chips):
        sent[k, :, 0:share] = full[:, k * share : (k + 1) * share]
        sent[k, :, share:] = jnp.zeros((8, sent.shape[2] - share), F32)


def gate(got, out):
    z = jnp.sum(got[...], axis=0)
    other = swap(z)
    first = row_of(z.shape) < 4
    pre = jnp.where(first, z, other)
    grad = jnp.where(first, other, z)
    c = 0.7978845608028654
    t = jnp.tanh(c * (pre + 0.044715 * (pre * pre * pre)))
    act = 0.5 * pre * (1.0 + t)
    slope = 0.5 * (1.0 + t) + 0.5 * pre * (1.0 - t * t) * (c * (1.0 + 3 * 0.044715 * (pre * pre)))
    both = jnp.where(first, act, grad * slope)
    for k in range(out.shape[0]):
        out[k] = both


def slot_rows(got, keep, own_in, own_out, near_in, near_out, out, full):
    w = own_in.shape[1]
    piece = 2 * w
    hidden = own_in.shape[2]
    chips = got.shape[0]
    share = hidden // chips
    core = core_index()
    for k in range(chips):
        full[:, k * share : (k + 1) * share] = got[k, :, 0:share]
    lane = lane_of((piece, LANES))
    cols = jnp.zeros((piece, LANES), F32)
    for a in range(2):
        for kind, mine, theirs in ((0, own_out, near_out), (1, own_in, near_in)):
            r = 4 * kind + 2 * a
            sums = [jnp.zeros((piece, LANES), F32) for _ in range(2)]
            for h in range(0, hidden, LANES):
                s = slice(h, h + LANES)
                block = jnp.concatenate([mine[a, :, s], theirs[a, :, s]], axis=0)
                for p in range(2):
                    sums[p] = sums[p] + block * full[r + p : r + p + 1, s]
            for p in range(2):
                cols = jnp.where(lane == r + p, jnp.sum(sums[p], axis=1, keepdims=True), cols)
    own, near = cols[0:w], cols[w:]
    low = jnp.where(core == 0, own, near)
    high = jnp.where(core == 0, near, own)
    square = jnp.concatenate([low, high, jnp.zeros((LANES - piece, LANES), F32)], axis=0)
    rows = jnp.transpose(square)[0:8]
    held = swap(keep[...])
    lane = lane_of((8, LANES))
    column = jnp.sum(jnp.where(lane < piece, held * rows, 0.0), axis=1, keepdims=True)
    out[...] = jnp.where(lane < piece, rows, jnp.where(lane == piece + 2, column, held))


def copies(tile, out):
    value = tile[...]
    for k in range(out.shape[0]):
        out[k] = value


def width_products(mine, near, tokens, grad_out, logits, shares, out, weights, rows, outs, marks):
    n = out.shape[0]
    piece = rows.shape[1] // 2
    core = core_index()
    added = []
    for c in range(2):
        for b, e, k in seats(n):
            tile = jnp.where(core == c, mine[k], near[k])
            s, w = slice(8 * e + 4 * c, 8 * e + 4 * c + 4), slice(b * piece, (b + 1) * piece)
            outs[s, w] = tile[0:4, 0:piece]
            rows[s, w] = tile[4:8, 0:piece]
            if b == 0:
                marks[s] = tile[4:8]
            else:
                added.append((s, tile[4:8, piece + 2 : piece + 3]))
    lane = lane_of((4, LANES))
    for s, column in added:
        marks[s] = marks[s] + jnp.where(lane == piece + 2, column, 0.0)
    top, total, column = (marks[:, piece + i : piece + i + 1] for i in range(3))
    first = contract(outs[...], grad_out[...], 1, 0, THREE)
    second = contract(rows[...], tokens[...], 1, 0) - column
    for i in range(n):
        s = slice(i * LANES, (i + 1) * LANES)
        combine = shares[:, s]
        dispatch = jnp.exp(logits[i] - top) / total
        weights[i] = dispatch
        part = combine * first[:, s]
        line = jnp.sum(part, axis=0, keepdims=True)
        out[i] = part - combine * line + dispatch * second[:, s]


def router_part(got, tokens, mine, theirs):
    n = got.shape[0]
    grads = jnp.concatenate([got[e] for e in range(n)], axis=1)
    part = contract(tokens[...], grads, 1, 1, THREE)
    q = part.shape[0] // 4
    low = jnp.concatenate([part[0:q], part[q : 2 * q]], axis=1)
    high = jnp.concatenate([part[2 * q : 3 * q], part[3 * q :]], axis=1)
    core = core_index()
    mine[...] = jnp.where(core == 0, low, high)
    theirs[...] = jnp.where(core == 0, high, low)


def token_grads(got, weights, rows, router, out):
    left = jnp.transpose(jnp.concatenate([router[...], rows[...]], axis=0))
    for e in range(got.shape[0]):
        right = jnp.concatenate([got[e], weights[e]], axis=0)
        out[:, e * LANES : (e + 1) * LANES] = contract(left, right, 1, 0, THREE)


def add_copies(mine, theirs, out):
    both = mine[...] + theirs[...]
    for k in range(out.shape[0]):
        out[k] = both


def add_all(got, out):
    out[...] = jnp.sum(got[...], axis=0)


def unfold(mine, theirs, out):
    core = core_index()
    a, b = mine[...], theirs[...]
    q, h = out.shape[1] // 4, LANES // 2
    for i, values in enumerate((jnp.where(core == 0, a, b), jnp.where(core == 0, b, a))):
        turned = jnp.transpose(values)
        out[:, 2 * i * q : (2 * i + 1) * q] = turned[:h]
        out[:, (2 * i + 1) * q : (2 * i + 2) * q] = turned[h:]


def weight_grads(full, near_full, keep, near_keep, grad_in, grad_out):
    w = grad_in.shape[1]
    hidden = grad_in.shape[2]
    core = core_index()
    step = 512
    for base, values, held in ((2 * core, full, keep), (2 - 2 * core, near_full, near_keep)):
        held = held[...]
        part = jnp.where(core == 0, held[:, 0:w], held[:, w : 2 * w])
        cols = jnp.transpose(part)
        for a in range(2):
            for h in range(0, hidden, step):
                s = slice(h, h + step)
                i, j = 2 * a, 2 * a + 1
                grad_out[base + a, :, s] = (
                    cols[:, 4 + i : 5 + i] * values[i : i + 1, s]
                    + cols[:, 4 + j : 5 + j] * values[j : j + 1, s]
                )
                grad_in[base + a, :, s] = (
                    cols[:, i : i + 1] * values[4 + i : 5 + i, s]
                    + cols[:, j : j + 1] * values[4 + j : 5 + j, s]
                )


def per_device(tokens, router, w_in, w_out, grad_out):
    n_seq, n_exp = lax.axis_size(S), lax.axis_size(E)
    experts, width_block, hidden = w_in.shape
    rows_block, local_tokens = tokens.shape
    slots = router.shape[1]
    chips = n_seq // 2
    piece = 2 * width_block
    core = core_index()
    partner = [(i, i ^ 1) for i in range(n_seq)]
    groups = [[2 * k + c for k in range(chips)] for c in range(2)]
    turned = router.T
    spread = (n_exp, slots, LANES)
    to_owner = [
        ((2 * seat(b, e, f) + c) * n_exp + f, (2 * (2 * f + b) + c) * n_exp + e)
        for b in range(2)
        for e in range(n_exp)
        for c in range(2)
        for f in range(n_exp)
    ]
    from_owner = [(there, here) for here, there in to_owner]

    def to_partner(values):
        return lax.ppermute(values, S, partner)

    def in_hbm(values):
        return pltpu.with_memory_space_constraint(values, pltpu.HBM)

    far_spec = pl.BlockSpec(memory_space=pltpu.HBM)
    vmem_spec = pl.BlockSpec(memory_space=pltpu.VMEM)
    limit = pltpu.CompilerParams(vmem_limit_bytes=40 * 1024 * 1024)
    sent = pl.pallas_call(
        logit_parts,
        out_shape=pltpu.HBM(spread, F32),
        in_specs=[far_spec, far_spec],
        out_specs=far_spec,
        scratch_shapes=[
            pltpu.VMEM(turned.shape, F32),
            pltpu.VMEM((4, rows_block, local_tokens // 4), F32),
            pltpu.VMEM(spread, F32),
            pltpu.SemaphoreType.DMA((5,)),
            pltpu.SemaphoreType.DMA((4,)),
        ],
        compiler_params=limit,
    )(in_hbm(turned), in_hbm(tokens))
    sent, w_in, w_out, grad_out = lax.optimization_barrier((sent, w_in, w_out, grad_out))
    got = exchange(sent, E)
    half = (experts // 2,) + w_in.shape[1:]
    staged = pl.pallas_call(
        stage,
        out_shape=[pltpu.HBM(half, F32)] * 2
        + [pltpu.VMEM(half, F32)] * 2
        + [pltpu.VMEM(tokens.shape, F32)] * 2,
        in_specs=[far_spec] * 4,
        out_specs=[far_spec] * 2 + [vmem_spec] * 4,
        scratch_shapes=[pltpu.SemaphoreType.DMA((6,))],
        compiler_params=limit,
    )(in_hbm(w_in), in_hbm(w_out), in_hbm(tokens), in_hbm(grad_out))
    got, far_in, far_out, own_in, own_out, tokens, grad_out = lax.optimization_barrier(
        (got, *staged)
    )
    logits = exchange(run(add_spread, spread, got), E)
    weights = (own_in, own_out, to_partner(far_in), to_partner(far_out))

    tiles = (chips, 8, LANES)
    mine, near, shares = run(
        partial_rows,
        [tiles, tiles, (slots, local_tokens)],
        logits,
        tokens,
        grad_out,
        scratch=[(2,) + tiles],
    )
    sent = run(functools.partial(merge_cores, piece=piece), tiles, mine, to_partner(near))
    tile = run(
        functools.partial(merge_chips, piece=piece), (8, LANES), exchange(sent, S, groups)
    )
    share = hidden // chips
    cut = -(-share // LANES) * LANES
    sent, held = run(
        hidden_parts,
        [(chips, 8, cut), (8, LANES)],
        lax.ppermute(tile, (S, E), to_owner),
        *weights,
        scratch=[(8, hidden)],
    )
    sent = run(gate, (chips, 8, cut), exchange(sent, S, groups))
    tile, full = run(
        slot_rows, [(8, LANES), (8, hidden)], exchange(sent, S, groups), held, *weights
    )
    sent = run(copies, tiles, lax.ppermute(tile, (S, E), from_owner))
    mine = exchange(sent, S, groups)
    near = to_partner(mine)
    sent, weights, rows = run(
        width_products,
        [spread, spread, (slots, rows_block)],
        mine,
        near,
        tokens,
        grad_out,
        logits,
        shares,
        scratch=[(slots, rows_block), (slots, LANES)],
    )
    sent = run(add_spread, spread, exchange(sent, E))
    sent, full, held = lax.optimization_barrier((sent, full, held))
    grads = exchange(sent, E)
    grad_w_in, grad_w_out = run(
        weight_grads,
        [w_in.shape, w_out.shape],
        full,
        to_partner(full),
        held,
        to_partner(held),
    )
    grads, grad_w_in, grad_w_out = lax.optimization_barrier((grads, grad_w_in, grad_w_out))
    fold = (rows_block // 4, 2 * slots)
    near, theirs = run(router_part, [fold, fold], grads, tokens)
    sent = run(add_copies, (chips,) + fold, near, to_partner(theirs))
    got, weights, rows = lax.optimization_barrier((exchange(sent, S, groups), weights, rows))
    near = run(add_all, fold, got)
    grad_tokens = run(
        token_grads, (rows_block, local_tokens), grads, weights, rows, turned
    )
    grad_router = run(unfold, (slots, rows_block), near, to_partner(near)).T
    return (grad_tokens, grad_router, grad_w_in, grad_w_out)


def solution(mesh):
    placed = (
        P("expert", "seq"),
        P("expert", None),
        P("expert", "seq", None),
        P("expert", "seq", None),
        P("expert", "seq"),
    )
    return jax.shard_map(
        per_device,
        mesh=mesh,
        in_specs=placed,
        out_specs=(
            P("expert", "seq"),
            P("expert", None),
            P("expert", "seq", None),
            P("expert", "seq", None),
        ),
        check_vma=False,
    )
```

```python
import functools

import jax
import jax.numpy as jnp
from jax import lax
from jax.experimental import pallas as pl
from jax.experimental.pallas import tpu as pltpu
from jax.sharding import PartitionSpec as P

FULL = lax.Precision.HIGHEST
THREE = lax.Precision.HIGH
S = "seq"
E = "expert"
LANES = 128
F32 = jnp.float32


def contract(left, right, left_dim, right_dim, precision=FULL):
    return lax.dot_general(
        left,
        right,
        (((left_dim,), (right_dim,)), ((), ())),
        precision=precision,
        preferred_element_type=F32,
    )


def exchange(blocks, axis, groups=None):
    return lax.all_to_all(blocks, axis, 0, 0, axis_index_groups=groups, tiled=True)


def run(kernel, shapes, *values, scratch=(), flops=0):
    single = not isinstance(shapes, list)
    shapes = [shapes] if single else shapes
    size = 4 * sum(v.size for v in values) + 4 * sum(functools.reduce(lambda a, b: a * b, s) for s in shapes)
    spec = pl.BlockSpec(memory_space=pltpu.VMEM)
    out = pl.pallas_call(
        kernel,
        out_shape=[jax.ShapeDtypeStruct(s, F32) for s in shapes],
        in_specs=[spec] * len(values),
        out_specs=[spec] * len(shapes),
        scratch_shapes=[pltpu.VMEM(s, F32) for s in scratch],
        compiler_params=pltpu.CompilerParams(vmem_limit_bytes=40 * 1024 * 1024),
        cost_estimate=pl.CostEstimate(flops=flops, bytes_accessed=size, transcendentals=0),
    )(*values)
    return out[0] if single else out


def row_of(shape):
    return lax.broadcasted_iota(jnp.int32, shape, len(shape) - 2) % 8


def lane_of(shape):
    return lax.broadcasted_iota(jnp.int32, shape, len(shape) - 1)


def swap(values):
    return jnp.concatenate([values[..., 4:8, :], values[..., 0:4, :]], axis=-2)


def core_index():
    return lax.axis_index(S) % 2


SEATS = (0xE680F7D5, 0xB291A3C4)


def seat(b, e, column):
    index = 2 * (((e >> 1) - (column >> 1)) & 3) + ((e ^ column) & 1)
    if isinstance(column, int):
        value = SEATS[b] >> (4 * index) & 15
    else:
        word = SEATS[b] - (1 << 32 if SEATS[b] >> 31 else 0)
        value = lax.shift_right_logical(jnp.int32(word), 4 * index) & 15
    return (((value >> 3) ^ (column >> 2)) << 3) | (((value & 7) + 2 * (column & 3)) & 7)


def seats(n):
    column = lax.axis_index(E)
    return [(b, e, seat(b, e, column)) for b in range(2) for e in range(n)]


def logit_parts(router, tokens, out, left, right, parts, sems, stores):
    n, _, cut = right.shape
    each = cut // LANES
    copies = [pltpu.make_async_copy(router, left, sems.at[n])]
    for i in range(n):
        block = tokens.at[:, pl.ds(i * cut, cut)]
        copies.append(pltpu.make_async_copy(block, right.at[i], sems.at[i]))
    for copy in copies:
        copy.start()
    copies[0].wait()
    moves = []
    for i in range(n):
        copies[i + 1].wait()
        part = contract(left[...], right[i], 1, 0)
        for j in range(each):
            parts[i * each + j] = part[:, j * LANES : (j + 1) * LANES]
        s = pl.ds(i * each, each)
        moves.append(pltpu.make_async_copy(parts.at[s], out.at[s], stores.at[i]))
        moves[i].start()
    for move in moves:
        move.wait()


def stage(w_in, w_out, tokens, grad_out, far_in, far_out, own_in, own_out, x, g, held, sems):
    core = core_index()
    half = own_in.shape[0]
    far = pl.ds(half * (1 - core), half)
    near = pl.ds(half * core, half)
    pairs = [
        (w_in.at[far], held.at[0]),
        (w_out.at[far], held.at[1]),
        (grad_out, g),
        (tokens, x),
        (w_in.at[near], own_in),
        (w_out.at[near], own_out),
    ]
    copies = [pltpu.make_async_copy(a, b, sems.at[i]) for i, (a, b) in enumerate(pairs)]
    for copy in copies:
        copy.start()
    for i, out in enumerate((far_in, far_out)):
        copies[i].wait()
        copies.append(pltpu.make_async_copy(held.at[i], out, sems.at[6 + i]))
        copies[-1].start()
    for copy in copies[2:]:
        copy.wait()


def add_spread(got, out):
    total = jnp.sum(got[...], axis=0)
    for e in range(out.shape[0]):
        out[e] = total


def partial_rows(got, tokens, grad_out, mine, near, shares, both):
    n, slots = got.shape[0], got.shape[1]
    logits = jnp.concatenate([got[e] for e in range(n)], axis=1)
    raised = jnp.exp(logits - jnp.max(logits, axis=0, keepdims=True))
    combine = raised / jnp.sum(raised, axis=0, keepdims=True)
    shares[...] = combine
    top = jnp.max(logits, axis=1, keepdims=True)
    raised = jnp.exp(logits - top)
    total = jnp.sum(raised, axis=1, keepdims=True)
    rows_in = contract(raised, tokens[...], 1, 1)
    rows_out = contract(combine, grad_out[...], 1, 1, THREE)
    piece = rows_in.shape[1] // 2
    lane = lane_of((slots, LANES))
    marks = jnp.where(lane == piece, top, jnp.where(lane == piece + 1, total, 0.0))
    plain = jnp.where(lane_of((4, LANES)) == piece + 1, 1.0, 0.0)
    for b, e, k in seats(n):
        for c in range(2):
            s, w = slice(8 * e + 4 * c, 8 * e + 4 * c + 4), slice(b * piece, (b + 1) * piece)
            both[c, k, 0:4] = marks[s]
            both[c, k, 4:8] = plain
            both[c, k, 0:4, 0:piece] = rows_in[s, w]
            both[c, k, 4:8, 0:piece] = rows_out[s, w]
    core = core_index()
    mine[...] = both[core]
    near[...] = both[1 - core]


def merge(parts, piece):
    top = functools.reduce(jnp.maximum, [p[:, piece : piece + 1] for p in parts])
    rows = sum(jnp.exp(p[:, piece : piece + 1] - top) * p for p in parts)
    return jnp.where(lane_of(rows.shape) == piece, top, rows)


def merge_cores(mine, near, out, piece):
    for k in range(out.shape[0]):
        out[k] = merge([mine[k], near[k]], piece)


def merge_chips(got, out, piece):
    out[...] = merge([got[k] for k in range(got.shape[0])], piece)


def hidden_parts(got, own_in, own_out, near_in, near_out, sent, keep, full):
    w = own_in.shape[1]
    piece = 2 * w
    hidden = own_in.shape[2]
    core = core_index()
    rows = got[...]
    scaled = (row_of((8, LANES)) < 4) & (lane_of((8, LANES)) < piece)
    rows = jnp.where(scaled, rows / rows[:, piece + 1 : piece + 2], rows)
    keep[...] = rows
    turned = jnp.transpose(rows)
    low, high = turned[0:w], turned[w:piece]
    own = jnp.where(core == 0, low, high)
    near = jnp.where(core == 0, high, low)
    for a in range(2):
        for kind, mine, theirs in ((0, own_in, near_in), (1, own_out, near_out)):
            r = 4 * kind + 2 * a
            values = [
                jnp.concatenate(
                    [
                        jnp.broadcast_to(own[:, r + p : r + p + 1], (w, LANES)),
                        jnp.broadcast_to(near[:, r + p : r + p + 1], (w, LANES)),
                    ],
                    axis=0,
                )
                for p in range(2)
            ]
            for h in range(0, hidden, LANES):
                s = slice(h, h + LANES)
                block = jnp.concatenate([mine[a, :, s], theirs[a, :, s]], axis=0)
                for p in range(2):
                    full[r + p : r + p + 1, s] = jnp.sum(block * values[p], axis=0, keepdims=True)
    chips = sent.shape[0]
    share = hidden // chips
    for k in range(chips):
        sent[k, :, 0:share] = full[:, k * share : (k + 1) * share]
        sent[k, :, share:] = jnp.zeros((8, sent.shape[2] - share), F32)


def gate(got, out):
    z = jnp.sum(got[...], axis=0)
    other = swap(z)
    first = row_of(z.shape) < 4
    pre = jnp.where(first, z, other)
    grad = jnp.where(first, other, z)
    c = 0.7978845608028654
    t = jnp.tanh(c * (pre + 0.044715 * (pre * pre * pre)))
    act = 0.5 * pre * (1.0 + t)
    slope = 0.5 * (1.0 + t) + 0.5 * pre * (1.0 - t * t) * (c * (1.0 + 3 * 0.044715 * (pre * pre)))
    both = jnp.where(first, act, grad * slope)
    for k in range(out.shape[0]):
        out[k] = both


def slot_rows(got, keep, own_in, own_out, near_in, near_out, out, full):
    w = own_in.shape[1]
    piece = 2 * w
    hidden = own_in.shape[2]
    chips = got.shape[0]
    share = hidden // chips
    core = core_index()
    for k in range(chips):
        full[:, k * share : (k + 1) * share] = got[k, :, 0:share]
    lane = lane_of((piece, LANES))
    cols = jnp.zeros((piece, LANES), F32)
    for a in range(2):
        for kind, mine, theirs in ((0, own_out, near_out), (1, own_in, near_in)):
            r = 4 * kind + 2 * a
            sums = [jnp.zeros((piece, LANES), F32) for _ in range(2)]
            for h in range(0, hidden, LANES):
                s = slice(h, h + LANES)
                block = jnp.concatenate([mine[a, :, s], theirs[a, :, s]], axis=0)
                for p in range(2):
                    sums[p] = sums[p] + block * full[r + p : r + p + 1, s]
            for p in range(2):
                cols = jnp.where(lane == r + p, jnp.sum(sums[p], axis=1, keepdims=True), cols)
    own, near = cols[0:w], cols[w:]
    low = jnp.where(core == 0, own, near)
    high = jnp.where(core == 0, near, own)
    square = jnp.concatenate([low, high, jnp.zeros((LANES - piece, LANES), F32)], axis=0)
    rows = jnp.transpose(square)[0:8]
    held = swap(keep[...])
    lane = lane_of((8, LANES))
    column = jnp.sum(jnp.where(lane < piece, held * rows, 0.0), axis=1, keepdims=True)
    out[...] = jnp.where(lane < piece, rows, jnp.where(lane == piece + 2, column, held))


def copies(tile, out):
    value = tile[...]
    for k in range(out.shape[0]):
        out[k] = value


def width_products(mine, near, tokens, grad_out, logits, shares, out, weights, rows, outs, marks):
    n = out.shape[0]
    piece = rows.shape[1] // 2
    core = core_index()
    added = []
    for c in range(2):
        for b, e, k in seats(n):
            tile = jnp.where(core == c, mine[k], near[k])
            s, w = slice(8 * e + 4 * c, 8 * e + 4 * c + 4), slice(b * piece, (b + 1) * piece)
            outs[s, w] = tile[0:4, 0:piece]
            rows[s, w] = tile[4:8, 0:piece]
            if b == 0:
                marks[s] = tile[4:8]
            else:
                added.append((s, tile[4:8, piece + 2 : piece + 3]))
    lane = lane_of((4, LANES))
    for s, column in added:
        marks[s] = marks[s] + jnp.where(lane == piece + 2, column, 0.0)
    top, total, column = (marks[:, piece + i : piece + i + 1] for i in range(3))
    first = contract(outs[...], grad_out[...], 1, 0, THREE)
    second = contract(rows[...], tokens[...], 1, 0) - column
    for i in range(n):
        s = slice(i * LANES, (i + 1) * LANES)
        combine = shares[:, s]
        dispatch = jnp.exp(logits[i] - top) / total
        weights[i] = dispatch
        part = combine * first[:, s]
        line = jnp.sum(part, axis=0, keepdims=True)
        out[i] = part - combine * line + dispatch * second[:, s]


def router_part(got, tokens, mine, theirs):
    n = got.shape[0]
    grads = jnp.concatenate([got[e] for e in range(n)], axis=1)
    part = contract(tokens[...], grads, 1, 1, THREE)
    q = part.shape[0] // 4
    low = jnp.concatenate([part[0:q], part[q : 2 * q]], axis=1)
    high = jnp.concatenate([part[2 * q : 3 * q], part[3 * q :]], axis=1)
    core = core_index()
    mine[...] = jnp.where(core == 0, low, high)
    theirs[...] = jnp.where(core == 0, high, low)


def token_grads(got, weights, rows, router, out):
    left = jnp.transpose(jnp.concatenate([router[...], rows[...]], axis=0))
    for e in range(got.shape[0]):
        right = jnp.concatenate([got[e], weights[e]], axis=0)
        out[:, e * LANES : (e + 1) * LANES] = contract(left, right, 1, 0, THREE)


def add_copies(mine, theirs, out):
    both = mine[...] + theirs[...]
    for k in range(out.shape[0]):
        out[k] = both


def add_all(got, out):
    out[...] = jnp.sum(got[...], axis=0)


def unfold(mine, theirs, out):
    core = core_index()
    a, b = mine[...], theirs[...]
    q, h = out.shape[1] // 4, LANES // 2
    for i, values in enumerate((jnp.where(core == 0, a, b), jnp.where(core == 0, b, a))):
        turned = jnp.transpose(values)
        out[:, 2 * i * q : (2 * i + 1) * q] = turned[:h]
        out[:, (2 * i + 1) * q : (2 * i + 2) * q] = turned[h:]


def weight_grads(full, near_full, keep, near_keep, grad_in, grad_out):
    w = grad_in.shape[1]
    hidden = grad_in.shape[2]
    core = core_index()
    step = 512
    for base, values, held in ((2 * core, full, keep), (2 - 2 * core, near_full, near_keep)):
        held = held[...]
        part = jnp.where(core == 0, held[:, 0:w], held[:, w : 2 * w])
        cols = jnp.transpose(part)
        for a in range(2):
            for h in range(0, hidden, step):
                s = slice(h, h + step)
                i, j = 2 * a, 2 * a + 1
                grad_out[base + a, :, s] = (
                    cols[:, 4 + i : 5 + i] * values[i : i + 1, s]
                    + cols[:, 4 + j : 5 + j] * values[j : j + 1, s]
                )
                grad_in[base + a, :, s] = (
                    cols[:, i : i + 1] * values[4 + i : 5 + i, s]
                    + cols[:, j : j + 1] * values[4 + j : 5 + j, s]
                )


def per_device(tokens, router, w_in, w_out, grad_out):
    n_seq, n_exp = lax.axis_size(S), lax.axis_size(E)
    experts, width_block, hidden = w_in.shape
    rows_block, local_tokens = tokens.shape
    slots = router.shape[1]
    chips = n_seq // 2
    piece = 2 * width_block
    core = core_index()
    partner = [(i, i ^ 1) for i in range(n_seq)]
    groups = [[2 * k + c for k in range(chips)] for c in range(2)]
    turned = router.T
    spread = (n_exp, slots, LANES)
    to_owner = [
        ((2 * seat(b, e, f) + c) * n_exp + f, (2 * (2 * f + b) + c) * n_exp + e)
        for b in range(2)
        for e in range(n_exp)
        for c in range(2)
        for f in range(n_exp)
    ]
    from_owner = [(there, here) for here, there in to_owner]

    def to_partner(values):
        return lax.ppermute(values, S, partner)

    def in_hbm(values):
        return pltpu.with_memory_space_constraint(values, pltpu.HBM)

    far_spec = pl.BlockSpec(memory_space=pltpu.HBM)
    vmem_spec = pl.BlockSpec(memory_space=pltpu.VMEM)
    limit = pltpu.CompilerParams(vmem_limit_bytes=40 * 1024 * 1024)
    sent = pl.pallas_call(
        logit_parts,
        out_shape=pltpu.HBM(spread, F32),
        in_specs=[far_spec, far_spec],
        out_specs=far_spec,
        scratch_shapes=[
            pltpu.VMEM(turned.shape, F32),
            pltpu.VMEM((4, rows_block, local_tokens // 4), F32),
            pltpu.VMEM(spread, F32),
            pltpu.SemaphoreType.DMA((5,)),
            pltpu.SemaphoreType.DMA((4,)),
        ],
        compiler_params=limit,
    )(in_hbm(turned), in_hbm(tokens))
    sent, w_in, w_out, grad_out = lax.optimization_barrier((sent, w_in, w_out, grad_out))
    got = exchange(sent, E)
    half = (experts // 2,) + w_in.shape[1:]
    staged = pl.pallas_call(
        stage,
        out_shape=[pltpu.HBM(half, F32)] * 2
        + [pltpu.VMEM(half, F32)] * 2
        + [pltpu.VMEM(tokens.shape, F32)] * 2,
        in_specs=[far_spec] * 4,
        out_specs=[far_spec] * 2 + [vmem_spec] * 4,
        scratch_shapes=[pltpu.VMEM((2,) + half, F32), pltpu.SemaphoreType.DMA((8,))],
        compiler_params=limit,
    )(in_hbm(w_in), in_hbm(w_out), in_hbm(tokens), in_hbm(grad_out))
    got, far_in, far_out, own_in, own_out, tokens, grad_out = lax.optimization_barrier(
        (got, *staged)
    )
    logits = exchange(run(add_spread, spread, got), E)
    weights = (own_in, own_out, to_partner(far_in), to_partner(far_out))

    tiles = (chips, 8, LANES)
    mine, near, shares = run(
        partial_rows,
        [tiles, tiles, (slots, local_tokens)],
        logits,
        tokens,
        grad_out,
        scratch=[(2,) + tiles],
    )
    sent = run(functools.partial(merge_cores, piece=piece), tiles, mine, to_partner(near))
    tile = run(
        functools.partial(merge_chips, piece=piece), (8, LANES), exchange(sent, S, groups)
    )
    share = hidden // chips
    cut = -(-share // LANES) * LANES
    sent, held = run(
        hidden_parts,
        [(chips, 8, cut), (8, LANES)],
        lax.ppermute(tile, (S, E), to_owner),
        *weights,
        scratch=[(8, hidden)],
    )
    sent = run(gate, (chips, 8, cut), exchange(sent, S, groups))
    tile, full = run(
        slot_rows, [(8, LANES), (8, hidden)], exchange(sent, S, groups), held, *weights
    )
    sent = run(copies, tiles, lax.ppermute(tile, (S, E), from_owner))
    mine = exchange(sent, S, groups)
    near = to_partner(mine)
    sent, weights, rows = run(
        width_products,
        [spread, spread, (slots, rows_block)],
        mine,
        near,
        tokens,
        grad_out,
        logits,
        shares,
        scratch=[(slots, rows_block), (slots, LANES)],
    )
    sent = run(add_spread, spread, exchange(sent, E))
    sent, full, held = lax.optimization_barrier((sent, full, held))
    grads = exchange(sent, E)
    grad_w_in, grad_w_out = run(
        weight_grads,
        [w_in.shape, w_out.shape],
        full,
        to_partner(full),
        held,
        to_partner(held),
    )
    grads, grad_w_in, grad_w_out = lax.optimization_barrier((grads, grad_w_in, grad_w_out))
    fold = (rows_block // 4, 2 * slots)
    near, theirs = run(router_part, [fold, fold], grads, tokens)
    sent = run(add_copies, (chips,) + fold, near, to_partner(theirs))
    got, weights, rows = lax.optimization_barrier((exchange(sent, S, groups), weights, rows))
    near = run(add_all, fold, got)
    grad_tokens = run(
        token_grads, (rows_block, local_tokens), grads, weights, rows, turned
    )
    grad_router = run(unfold, (slots, rows_block), near, to_partner(near)).T
    return (grad_tokens, grad_router, grad_w_in, grad_w_out)


def solution(mesh):
    placed = (
        P("expert", "seq"),
        P("expert", None),
        P("expert", "seq", None),
        P("expert", "seq", None),
        P("expert", "seq"),
    )
    return jax.shard_map(
        per_device,
        mesh=mesh,
        in_specs=placed,
        out_specs=(
            P("expert", "seq"),
            P("expert", None),
            P("expert", "seq", None),
            P("expert", "seq", None),
        ),
        check_vma=False,
    )
```

```python
import functools

import jax
import jax.numpy as jnp
from jax import lax
from jax.experimental import pallas as pl
from jax.experimental.pallas import tpu as pltpu
from jax.sharding import PartitionSpec as P

FULL = lax.Precision.HIGHEST
THREE = lax.Precision.HIGH
S = "seq"
E = "expert"
LANES = 128
F32 = jnp.float32


def contract(left, right, left_dim, right_dim, precision=FULL):
    return lax.dot_general(
        left,
        right,
        (((left_dim,), (right_dim,)), ((), ())),
        precision=precision,
        preferred_element_type=F32,
    )


def exchange(blocks, axis, groups=None):
    return lax.all_to_all(blocks, axis, 0, 0, axis_index_groups=groups, tiled=True)


def run(kernel, shapes, *values, scratch=(), flops=0):
    single = not isinstance(shapes, list)
    shapes = [shapes] if single else shapes
    size = 4 * sum(v.size for v in values) + 4 * sum(functools.reduce(lambda a, b: a * b, s) for s in shapes)
    spec = pl.BlockSpec(memory_space=pltpu.VMEM)
    out = pl.pallas_call(
        kernel,
        out_shape=[jax.ShapeDtypeStruct(s, F32) for s in shapes],
        in_specs=[spec] * len(values),
        out_specs=[spec] * len(shapes),
        scratch_shapes=[pltpu.VMEM(s, F32) for s in scratch],
        compiler_params=pltpu.CompilerParams(vmem_limit_bytes=40 * 1024 * 1024),
        cost_estimate=pl.CostEstimate(flops=flops, bytes_accessed=size, transcendentals=0),
    )(*values)
    return out[0] if single else out


def row_of(shape):
    return lax.broadcasted_iota(jnp.int32, shape, len(shape) - 2) % 8


def lane_of(shape):
    return lax.broadcasted_iota(jnp.int32, shape, len(shape) - 1)


def swap(values):
    return jnp.concatenate([values[..., 4:8, :], values[..., 0:4, :]], axis=-2)


def core_index():
    return lax.axis_index(S) % 2


SEATS = (0xE680F7D5, 0xB291A3C4)


def seat(b, e, column):
    index = 2 * (((e >> 1) - (column >> 1)) & 3) + ((e ^ column) & 1)
    if isinstance(column, int):
        value = SEATS[b] >> (4 * index) & 15
    else:
        word = SEATS[b] - (1 << 32 if SEATS[b] >> 31 else 0)
        value = lax.shift_right_logical(jnp.int32(word), 4 * index) & 15
    return (((value >> 3) ^ (column >> 2)) << 3) | (((value & 7) + 2 * (column & 3)) & 7)


def seats(n):
    column = lax.axis_index(E)
    return [(b, e, seat(b, e, column)) for b in range(2) for e in range(n)]


def logit_parts(router, tokens, out, left, right, parts, sems, stores):
    n, _, cut = right.shape
    each = cut // LANES
    copies = [pltpu.make_async_copy(router, left, sems.at[n])]
    for i in range(n):
        block = tokens.at[:, pl.ds(i * cut, cut)]
        copies.append(pltpu.make_async_copy(block, right.at[i], sems.at[i]))
    for copy in copies:
        copy.start()
    copies[0].wait()
    moves = []
    for i in range(n):
        copies[i + 1].wait()
        part = contract(left[...], right[i], 1, 0)
        for j in range(each):
            parts[i * each + j] = part[:, j * LANES : (j + 1) * LANES]
        s = pl.ds(i * each, each)
        moves.append(pltpu.make_async_copy(parts.at[s], out.at[s], stores.at[i]))
        moves[i].start()
    for move in moves:
        move.wait()


def stage(w_in, w_out, tokens, far_in, far_out, own_in, own_out, x, held, sems):
    core = core_index()
    half = own_in.shape[0]
    far = pl.ds(half * (1 - core), half)
    near = pl.ds(half * core, half)
    pairs = [
        (w_in.at[far], held.at[0]),
        (w_out.at[far], held.at[1]),
        (tokens, x),
        (w_in.at[near], own_in),
        (w_out.at[near], own_out),
    ]
    copies = [pltpu.make_async_copy(a, b, sems.at[i]) for i, (a, b) in enumerate(pairs)]
    for copy in copies:
        copy.start()
    for i, out in enumerate((far_in, far_out)):
        copies[i].wait()
        copies.append(pltpu.make_async_copy(held.at[i], out, sems.at[5 + i]))
        copies[-1].start()
    for copy in copies[2:]:
        copy.wait()


def add_spread(got, out):
    total = jnp.sum(got[...], axis=0)
    for e in range(out.shape[0]):
        out[e] = total


def partial_rows(got, tokens, grad_out, mine, near, shares, both):
    n, slots = got.shape[0], got.shape[1]
    logits = jnp.concatenate([got[e] for e in range(n)], axis=1)
    raised = jnp.exp(logits - jnp.max(logits, axis=0, keepdims=True))
    combine = raised / jnp.sum(raised, axis=0, keepdims=True)
    shares[...] = combine
    top = jnp.max(logits, axis=1, keepdims=True)
    raised = jnp.exp(logits - top)
    total = jnp.sum(raised, axis=1, keepdims=True)
    rows_in = contract(raised, tokens[...], 1, 1)
    rows_out = contract(combine, grad_out[...], 1, 1, THREE)
    piece = rows_in.shape[1] // 2
    lane = lane_of((slots, LANES))
    marks = jnp.where(lane == piece, top, jnp.where(lane == piece + 1, total, 0.0))
    plain = jnp.where(lane_of((4, LANES)) == piece + 1, 1.0, 0.0)
    for b, e, k in seats(n):
        for c in range(2):
            s, w = slice(8 * e + 4 * c, 8 * e + 4 * c + 4), slice(b * piece, (b + 1) * piece)
            both[c, k, 0:4] = marks[s]
            both[c, k, 4:8] = plain
            both[c, k, 0:4, 0:piece] = rows_in[s, w]
            both[c, k, 4:8, 0:piece] = rows_out[s, w]
    core = core_index()
    mine[...] = both[core]
    near[...] = both[1 - core]


def merge(parts, piece):
    top = functools.reduce(jnp.maximum, [p[:, piece : piece + 1] for p in parts])
    rows = sum(jnp.exp(p[:, piece : piece + 1] - top) * p for p in parts)
    return jnp.where(lane_of(rows.shape) == piece, top, rows)


def merge_cores(mine, near, out, piece):
    for k in range(out.shape[0]):
        out[k] = merge([mine[k], near[k]], piece)


def merge_chips(got, out, piece):
    out[...] = merge([got[k] for k in range(got.shape[0])], piece)


def hidden_parts(got, own_in, own_out, near_in, near_out, sent, keep, full):
    w = own_in.shape[1]
    piece = 2 * w
    hidden = own_in.shape[2]
    core = core_index()
    rows = got[...]
    scaled = (row_of((8, LANES)) < 4) & (lane_of((8, LANES)) < piece)
    rows = jnp.where(scaled, rows / rows[:, piece + 1 : piece + 2], rows)
    keep[...] = rows
    turned = jnp.transpose(rows)
    low, high = turned[0:w], turned[w:piece]
    own = jnp.where(core == 0, low, high)
    near = jnp.where(core == 0, high, low)
    for a in range(2):
        for kind, mine, theirs in ((0, own_in, near_in), (1, own_out, near_out)):
            r = 4 * kind + 2 * a
            values = [
                jnp.concatenate(
                    [
                        jnp.broadcast_to(own[:, r + p : r + p + 1], (w, LANES)),
                        jnp.broadcast_to(near[:, r + p : r + p + 1], (w, LANES)),
                    ],
                    axis=0,
                )
                for p in range(2)
            ]
            for h in range(0, hidden, LANES):
                s = slice(h, h + LANES)
                block = jnp.concatenate([mine[a, :, s], theirs[a, :, s]], axis=0)
                for p in range(2):
                    full[r + p : r + p + 1, s] = jnp.sum(block * values[p], axis=0, keepdims=True)
    chips = sent.shape[0]
    share = hidden // chips
    for k in range(chips):
        sent[k, :, 0:share] = full[:, k * share : (k + 1) * share]
        sent[k, :, share:] = jnp.zeros((8, sent.shape[2] - share), F32)


def gate(got, out):
    z = jnp.sum(got[...], axis=0)
    other = swap(z)
    first = row_of(z.shape) < 4
    pre = jnp.where(first, z, other)
    grad = jnp.where(first, other, z)
    c = 0.7978845608028654
    t = jnp.tanh(c * (pre + 0.044715 * (pre * pre * pre)))
    act = 0.5 * pre * (1.0 + t)
    slope = 0.5 * (1.0 + t) + 0.5 * pre * (1.0 - t * t) * (c * (1.0 + 3 * 0.044715 * (pre * pre)))
    both = jnp.where(first, act, grad * slope)
    for k in range(out.shape[0]):
        out[k] = both


def slot_rows(got, keep, own_in, own_out, near_in, near_out, out, full):
    w = own_in.shape[1]
    piece = 2 * w
    hidden = own_in.shape[2]
    chips = got.shape[0]
    share = hidden // chips
    core = core_index()
    for k in range(chips):
        full[:, k * share : (k + 1) * share] = got[k, :, 0:share]
    lane = lane_of((piece, LANES))
    cols = jnp.zeros((piece, LANES), F32)
    for a in range(2):
        for kind, mine, theirs in ((0, own_out, near_out), (1, own_in, near_in)):
            r = 4 * kind + 2 * a
            sums = [jnp.zeros((piece, LANES), F32) for _ in range(2)]
            for h in range(0, hidden, LANES):
                s = slice(h, h + LANES)
                block = jnp.concatenate([mine[a, :, s], theirs[a, :, s]], axis=0)
                for p in range(2):
                    sums[p] = sums[p] + block * full[r + p : r + p + 1, s]
            for p in range(2):
                cols = jnp.where(lane == r + p, jnp.sum(sums[p], axis=1, keepdims=True), cols)
    own, near = cols[0:w], cols[w:]
    low = jnp.where(core == 0, own, near)
    high = jnp.where(core == 0, near, own)
    square = jnp.concatenate([low, high, jnp.zeros((LANES - piece, LANES), F32)], axis=0)
    rows = jnp.transpose(square)[0:8]
    held = swap(keep[...])
    lane = lane_of((8, LANES))
    column = jnp.sum(jnp.where(lane < piece, held * rows, 0.0), axis=1, keepdims=True)
    out[...] = jnp.where(lane < piece, rows, jnp.where(lane == piece + 2, column, held))


def copies(tile, out):
    value = tile[...]
    for k in range(out.shape[0]):
        out[k] = value


def width_products(mine, near, tokens, grad_out, logits, shares, out, weights, rows, outs, marks):
    n = out.shape[0]
    piece = rows.shape[1] // 2
    core = core_index()
    added = []
    for c in range(2):
        for b, e, k in seats(n):
            tile = jnp.where(core == c, mine[k], near[k])
            s, w = slice(8 * e + 4 * c, 8 * e + 4 * c + 4), slice(b * piece, (b + 1) * piece)
            outs[s, w] = tile[0:4, 0:piece]
            rows[s, w] = tile[4:8, 0:piece]
            if b == 0:
                marks[s] = tile[4:8]
            else:
                added.append((s, tile[4:8, piece + 2 : piece + 3]))
    lane = lane_of((4, LANES))
    for s, column in added:
        marks[s] = marks[s] + jnp.where(lane == piece + 2, column, 0.0)
    top, total, column = (marks[:, piece + i : piece + i + 1] for i in range(3))
    first = contract(outs[...], grad_out[...], 1, 0, THREE)
    second = contract(rows[...], tokens[...], 1, 0) - column
    for i in range(n):
        s = slice(i * LANES, (i + 1) * LANES)
        combine = shares[:, s]
        dispatch = jnp.exp(logits[i] - top) / total
        weights[i] = dispatch
        part = combine * first[:, s]
        line = jnp.sum(part, axis=0, keepdims=True)
        out[i] = part - combine * line + dispatch * second[:, s]


def router_part(got, tokens, mine, theirs):
    n = got.shape[0]
    grads = jnp.concatenate([got[e] for e in range(n)], axis=1)
    part = contract(tokens[...], grads, 1, 1, THREE)
    q = part.shape[0] // 4
    low = jnp.concatenate([part[0:q], part[q : 2 * q]], axis=1)
    high = jnp.concatenate([part[2 * q : 3 * q], part[3 * q :]], axis=1)
    core = core_index()
    mine[...] = jnp.where(core == 0, low, high)
    theirs[...] = jnp.where(core == 0, high, low)


def token_grads(got, weights, rows, router, out):
    left = jnp.transpose(jnp.concatenate([router[...], rows[...]], axis=0))
    for e in range(got.shape[0]):
        right = jnp.concatenate([got[e], weights[e]], axis=0)
        out[:, e * LANES : (e + 1) * LANES] = contract(left, right, 1, 0, THREE)


def add_copies(mine, theirs, out):
    both = mine[...] + theirs[...]
    for k in range(out.shape[0]):
        out[k] = both


def add_all(got, out):
    out[...] = jnp.sum(got[...], axis=0)


def unfold(mine, theirs, out):
    core = core_index()
    a, b = mine[...], theirs[...]
    q, h = out.shape[1] // 4, LANES // 2
    for i, values in enumerate((jnp.where(core == 0, a, b), jnp.where(core == 0, b, a))):
        turned = jnp.transpose(values)
        out[:, 2 * i * q : (2 * i + 1) * q] = turned[:h]
        out[:, (2 * i + 1) * q : (2 * i + 2) * q] = turned[h:]


def weight_grads(full, near_full, keep, near_keep, grad_in, grad_out):
    w = grad_in.shape[1]
    hidden = grad_in.shape[2]
    core = core_index()
    step = 512
    for base, values, held in ((2 * core, full, keep), (2 - 2 * core, near_full, near_keep)):
        held = held[...]
        part = jnp.where(core == 0, held[:, 0:w], held[:, w : 2 * w])
        cols = jnp.transpose(part)
        for a in range(2):
            for h in range(0, hidden, step):
                s = slice(h, h + step)
                i, j = 2 * a, 2 * a + 1
                grad_out[base + a, :, s] = (
                    cols[:, 4 + i : 5 + i] * values[i : i + 1, s]
                    + cols[:, 4 + j : 5 + j] * values[j : j + 1, s]
                )
                grad_in[base + a, :, s] = (
                    cols[:, i : i + 1] * values[4 + i : 5 + i, s]
                    + cols[:, j : j + 1] * values[4 + j : 5 + j, s]
                )


def per_device(tokens, router, w_in, w_out, grad_out):
    n_seq, n_exp = lax.axis_size(S), lax.axis_size(E)
    experts, width_block, hidden = w_in.shape
    rows_block, local_tokens = tokens.shape
    slots = router.shape[1]
    chips = n_seq // 2
    piece = 2 * width_block
    core = core_index()
    partner = [(i, i ^ 1) for i in range(n_seq)]
    groups = [[2 * k + c for k in range(chips)] for c in range(2)]
    turned = router.T
    spread = (n_exp, slots, LANES)
    to_owner = [
        ((2 * seat(b, e, f) + c) * n_exp + f, (2 * (2 * f + b) + c) * n_exp + e)
        for b in range(2)
        for e in range(n_exp)
        for c in range(2)
        for f in range(n_exp)
    ]
    from_owner = [(there, here) for here, there in to_owner]

    def to_partner(values):
        return lax.ppermute(values, S, partner)

    def in_hbm(values):
        return pltpu.with_memory_space_constraint(values, pltpu.HBM)

    far_spec = pl.BlockSpec(memory_space=pltpu.HBM)
    vmem_spec = pl.BlockSpec(memory_space=pltpu.VMEM)
    limit = pltpu.CompilerParams(vmem_limit_bytes=40 * 1024 * 1024)
    sent = pl.pallas_call(
        logit_parts,
        out_shape=pltpu.HBM(spread, F32),
        in_specs=[far_spec, far_spec],
        out_specs=far_spec,
        scratch_shapes=[
            pltpu.VMEM(turned.shape, F32),
            pltpu.VMEM((4, rows_block, local_tokens // 4), F32),
            pltpu.VMEM(spread, F32),
            pltpu.SemaphoreType.DMA((5,)),
            pltpu.SemaphoreType.DMA((4,)),
        ],
        compiler_params=limit,
    )(in_hbm(turned), in_hbm(tokens))
    sent, w_in, w_out = lax.optimization_barrier((sent, w_in, w_out))
    got = exchange(sent, E)
    half = (experts // 2,) + w_in.shape[1:]
    staged = pl.pallas_call(
        stage,
        out_shape=[pltpu.HBM(half, F32)] * 2
        + [pltpu.VMEM(half, F32)] * 2
        + [pltpu.VMEM(tokens.shape, F32)],
        in_specs=[far_spec] * 3,
        out_specs=[far_spec] * 2 + [vmem_spec] * 3,
        scratch_shapes=[pltpu.VMEM((2,) + half, F32), pltpu.SemaphoreType.DMA((7,))],
        compiler_params=limit,
    )(in_hbm(w_in), in_hbm(w_out), in_hbm(tokens))
    got, far_in, far_out, own_in, own_out, tokens = lax.optimization_barrier((got, *staged))
    logits = exchange(run(add_spread, spread, got), E)
    weights = (own_in, own_out, to_partner(far_in), to_partner(far_out))

    tiles = (chips, 8, LANES)
    mine, near, shares = run(
        partial_rows,
        [tiles, tiles, (slots, local_tokens)],
        logits,
        tokens,
        grad_out,
        scratch=[(2,) + tiles],
    )
    sent = run(functools.partial(merge_cores, piece=piece), tiles, mine, to_partner(near))
    tile = run(
        functools.partial(merge_chips, piece=piece), (8, LANES), exchange(sent, S, groups)
    )
    share = hidden // chips
    cut = -(-share // LANES) * LANES
    sent, held = run(
        hidden_parts,
        [(chips, 8, cut), (8, LANES)],
        lax.ppermute(tile, (S, E), to_owner),
        *weights,
        scratch=[(8, hidden)],
    )
    sent = run(gate, (chips, 8, cut), exchange(sent, S, groups))
    tile, full = run(
        slot_rows, [(8, LANES), (8, hidden)], exchange(sent, S, groups), held, *weights
    )
    grad_w_in, grad_w_out = run(
        weight_grads,
        [w_in.shape, w_out.shape],
        full,
        to_partner(full),
        held,
        to_partner(held),
    )
    tile, grad_w_in, grad_w_out = lax.optimization_barrier(
        (lax.ppermute(tile, (S, E), from_owner), grad_w_in, grad_w_out)
    )
    sent = run(copies, tiles, tile)
    mine = exchange(sent, S, groups)
    near = to_partner(mine)
    sent, weights, rows = run(
        width_products,
        [spread, spread, (slots, rows_block)],
        mine,
        near,
        tokens,
        grad_out,
        logits,
        shares,
        scratch=[(slots, rows_block), (slots, LANES)],
    )
    sent = run(add_spread, spread, exchange(sent, E))
    grads = exchange(sent, E)
    fold = (rows_block // 4, 2 * slots)
    near, theirs = run(router_part, [fold, fold], grads, tokens)
    sent = run(add_copies, (chips,) + fold, near, to_partner(theirs))
    got, weights, rows = lax.optimization_barrier((exchange(sent, S, groups), weights, rows))
    near = run(add_all, fold, got)
    grad_tokens = run(
        token_grads, (rows_block, local_tokens), grads, weights, rows, turned
    )
    grad_router = run(unfold, (slots, rows_block), near, to_partner(near)).T
    return (grad_tokens, grad_router, grad_w_in, grad_w_out)


def solution(mesh):
    placed = (
        P("expert", "seq"),
        P("expert", None),
        P("expert", "seq", None),
        P("expert", "seq", None),
        P("expert", "seq"),
    )
    return jax.shard_map(
        per_device,
        mesh=mesh,
        in_specs=placed,
        out_specs=(
            P("expert", "seq"),
            P("expert", None),
            P("expert", "seq", None),
            P("expert", "seq", None),
        ),
        check_vma=False,
    )
```

```python
import functools

import jax
import jax.numpy as jnp
from jax import lax
from jax.experimental import pallas as pl
from jax.experimental.pallas import tpu as pltpu
from jax.sharding import PartitionSpec as P

FULL = lax.Precision.HIGHEST
THREE = lax.Precision.HIGH
S = "seq"
E = "expert"
LANES = 128
F32 = jnp.float32


def contract(left, right, left_dim, right_dim, precision=FULL):
    return lax.dot_general(
        left,
        right,
        (((left_dim,), (right_dim,)), ((), ())),
        precision=precision,
        preferred_element_type=F32,
    )


def exchange(blocks, axis, groups=None):
    return lax.all_to_all(blocks, axis, 0, 0, axis_index_groups=groups, tiled=True)


def run(kernel, shapes, *values, scratch=(), flops=0):
    single = not isinstance(shapes, list)
    shapes = [shapes] if single else shapes
    size = 4 * sum(v.size for v in values) + 4 * sum(functools.reduce(lambda a, b: a * b, s) for s in shapes)
    spec = pl.BlockSpec(memory_space=pltpu.VMEM)
    out = pl.pallas_call(
        kernel,
        out_shape=[jax.ShapeDtypeStruct(s, F32) for s in shapes],
        in_specs=[spec] * len(values),
        out_specs=[spec] * len(shapes),
        scratch_shapes=[pltpu.VMEM(s, F32) for s in scratch],
        compiler_params=pltpu.CompilerParams(vmem_limit_bytes=40 * 1024 * 1024),
        cost_estimate=pl.CostEstimate(flops=flops, bytes_accessed=size, transcendentals=0),
    )(*values)
    return out[0] if single else out


def row_of(shape):
    return lax.broadcasted_iota(jnp.int32, shape, len(shape) - 2) % 8


def lane_of(shape):
    return lax.broadcasted_iota(jnp.int32, shape, len(shape) - 1)


def swap(values):
    return jnp.concatenate([values[..., 4:8, :], values[..., 0:4, :]], axis=-2)


def core_index():
    return lax.axis_index(S) % 2


SEATS = (0xE680F7D5, 0xB291A3C4)


def seat(b, e, column):
    index = 2 * (((e >> 1) - (column >> 1)) & 3) + ((e ^ column) & 1)
    if isinstance(column, int):
        value = SEATS[b] >> (4 * index) & 15
    else:
        word = SEATS[b] - (1 << 32 if SEATS[b] >> 31 else 0)
        value = lax.shift_right_logical(jnp.int32(word), 4 * index) & 15
    return (((value >> 3) ^ (column >> 2)) << 3) | (((value & 7) + 2 * (column & 3)) & 7)


def seats(n):
    column = lax.axis_index(E)
    return [(b, e, seat(b, e, column)) for b in range(2) for e in range(n)]


def logit_parts(router, tokens, out, left, right, parts, sems, stores):
    n, _, cut = right.shape
    each = cut // LANES
    copies = [pltpu.make_async_copy(router, left, sems.at[n])]
    for i in range(n):
        block = tokens.at[:, pl.ds(i * cut, cut)]
        copies.append(pltpu.make_async_copy(block, right.at[i], sems.at[i]))
    for copy in copies:
        copy.start()
    copies[0].wait()
    moves = []
    for i in range(n):
        copies[i + 1].wait()
        part = contract(left[...], right[i], 1, 0)
        for j in range(each):
            parts[i * each + j] = part[:, j * LANES : (j + 1) * LANES]
        s = pl.ds(i * each, each)
        moves.append(pltpu.make_async_copy(parts.at[s], out.at[s], stores.at[i]))
        moves[i].start()
    for move in moves:
        move.wait()


def stage(w_in, w_out, tokens, far_in, far_out, own_in, own_out, x, held, sems):
    core = core_index()
    half = own_in.shape[0]
    far = pl.ds(half * (1 - core), half)
    near = pl.ds(half * core, half)
    pairs = [
        (w_in.at[far], held.at[0]),
        (w_out.at[far], held.at[1]),
        (tokens, x),
        (w_in.at[near], own_in),
        (w_out.at[near], own_out),
    ]
    copies = [pltpu.make_async_copy(a, b, sems.at[i]) for i, (a, b) in enumerate(pairs)]
    for copy in copies:
        copy.start()
    for i, out in enumerate((far_in, far_out)):
        copies[i].wait()
        copies.append(pltpu.make_async_copy(held.at[i], out, sems.at[5 + i]))
        copies[-1].start()
    for copy in copies[2:]:
        copy.wait()


def add_spread(got, out):
    total = jnp.sum(got[...], axis=0)
    for e in range(out.shape[0]):
        out[e] = total


def partial_rows(got, tokens, grad_out, mine, near, shares, both):
    n, slots = got.shape[0], got.shape[1]
    logits = jnp.concatenate([got[e] for e in range(n)], axis=1)
    raised = jnp.exp(logits - jnp.max(logits, axis=0, keepdims=True))
    combine = raised / jnp.sum(raised, axis=0, keepdims=True)
    shares[...] = combine
    top = jnp.max(logits, axis=1, keepdims=True)
    raised = jnp.exp(logits - top)
    total = jnp.sum(raised, axis=1, keepdims=True)
    rows_in = contract(raised, tokens[...], 1, 1)
    rows_out = contract(combine, grad_out[...], 1, 1, THREE)
    piece = rows_in.shape[1] // 2
    lane = lane_of((slots, LANES))
    marks = jnp.where(lane == piece, top, jnp.where(lane == piece + 1, total, 0.0))
    plain = jnp.where(lane_of((4, LANES)) == piece + 1, 1.0, 0.0)
    for b, e, k in seats(n):
        for c in range(2):
            s, w = slice(8 * e + 4 * c, 8 * e + 4 * c + 4), slice(b * piece, (b + 1) * piece)
            both[c, k, 0:4] = marks[s]
            both[c, k, 4:8] = plain
            both[c, k, 0:4, 0:piece] = rows_in[s, w]
            both[c, k, 4:8, 0:piece] = rows_out[s, w]
    core = core_index()
    mine[...] = both[core]
    near[...] = both[1 - core]


def merge(parts, piece):
    top = functools.reduce(jnp.maximum, [p[:, piece : piece + 1] for p in parts])
    rows = sum(jnp.exp(p[:, piece : piece + 1] - top) * p for p in parts)
    return jnp.where(lane_of(rows.shape) == piece, top, rows)


def merge_cores(mine, near, out, piece):
    for k in range(out.shape[0]):
        out[k] = merge([mine[k], near[k]], piece)


def merge_chips(got, out, piece):
    out[...] = merge([got[k] for k in range(got.shape[0])], piece)


def hidden_parts(got, own_in, own_out, near_in, near_out, sent, keep, full):
    w = own_in.shape[1]
    piece = 2 * w
    hidden = own_in.shape[2]
    core = core_index()
    rows = got[...]
    scaled = (row_of((8, LANES)) < 4) & (lane_of((8, LANES)) < piece)
    rows = jnp.where(scaled, rows / rows[:, piece + 1 : piece + 2], rows)
    keep[...] = rows
    turned = jnp.transpose(rows)
    low, high = turned[0:w], turned[w:piece]
    own = jnp.where(core == 0, low, high)
    near = jnp.where(core == 0, high, low)
    for a in range(2):
        for kind, mine, theirs in ((0, own_in, near_in), (1, own_out, near_out)):
            r = 4 * kind + 2 * a
            values = [
                jnp.concatenate(
                    [
                        jnp.broadcast_to(own[:, r + p : r + p + 1], (w, LANES)),
                        jnp.broadcast_to(near[:, r + p : r + p + 1], (w, LANES)),
                    ],
                    axis=0,
                )
                for p in range(2)
            ]
            for h in range(0, hidden, LANES):
                s = slice(h, h + LANES)
                block = jnp.concatenate([mine[a, :, s], theirs[a, :, s]], axis=0)
                for p in range(2):
                    full[r + p : r + p + 1, s] = jnp.sum(block * values[p], axis=0, keepdims=True)
    chips = sent.shape[0]
    share = hidden // chips
    for k in range(chips):
        sent[k, :, 0:share] = full[:, k * share : (k + 1) * share]
        sent[k, :, share:] = jnp.zeros((8, sent.shape[2] - share), F32)


def gate(got, out):
    z = jnp.sum(got[...], axis=0)
    other = swap(z)
    first = row_of(z.shape) < 4
    pre = jnp.where(first, z, other)
    grad = jnp.where(first, other, z)
    c = 0.7978845608028654
    t = jnp.tanh(c * (pre + 0.044715 * (pre * pre * pre)))
    act = 0.5 * pre * (1.0 + t)
    slope = 0.5 * (1.0 + t) + 0.5 * pre * (1.0 - t * t) * (c * (1.0 + 3 * 0.044715 * (pre * pre)))
    both = jnp.where(first, act, grad * slope)
    for k in range(out.shape[0]):
        out[k] = both


def slot_rows(got, keep, own_in, own_out, near_in, near_out, out, full):
    w = own_in.shape[1]
    piece = 2 * w
    hidden = own_in.shape[2]
    chips = got.shape[0]
    share = hidden // chips
    core = core_index()
    for k in range(chips):
        full[:, k * share : (k + 1) * share] = got[k, :, 0:share]
    lane = lane_of((piece, LANES))
    cols = jnp.zeros((piece, LANES), F32)
    for a in range(2):
        for kind, mine, theirs in ((0, own_out, near_out), (1, own_in, near_in)):
            r = 4 * kind + 2 * a
            sums = [jnp.zeros((piece, LANES), F32) for _ in range(2)]
            for h in range(0, hidden, LANES):
                s = slice(h, h + LANES)
                block = jnp.concatenate([mine[a, :, s], theirs[a, :, s]], axis=0)
                for p in range(2):
                    sums[p] = sums[p] + block * full[r + p : r + p + 1, s]
            for p in range(2):
                cols = jnp.where(lane == r + p, jnp.sum(sums[p], axis=1, keepdims=True), cols)
    own, near = cols[0:w], cols[w:]
    low = jnp.where(core == 0, own, near)
    high = jnp.where(core == 0, near, own)
    square = jnp.concatenate([low, high, jnp.zeros((LANES - piece, LANES), F32)], axis=0)
    rows = jnp.transpose(square)[0:8]
    held = swap(keep[...])
    lane = lane_of((8, LANES))
    column = jnp.sum(jnp.where(lane < piece, held * rows, 0.0), axis=1, keepdims=True)
    out[...] = jnp.where(lane < piece, rows, jnp.where(lane == piece + 2, column, held))


def copies(tile, out):
    value = tile[...]
    for k in range(out.shape[0]):
        out[k] = value


def width_products(mine, near, tokens, grad_out, logits, shares, out, weights, rows, outs, marks):
    n = out.shape[0]
    piece = rows.shape[1] // 2
    core = core_index()
    added = []
    for c in range(2):
        for b, e, k in seats(n):
            tile = jnp.where(core == c, mine[k], near[k])
            s, w = slice(8 * e + 4 * c, 8 * e + 4 * c + 4), slice(b * piece, (b + 1) * piece)
            outs[s, w] = tile[0:4, 0:piece]
            rows[s, w] = tile[4:8, 0:piece]
            if b == 0:
                marks[s] = tile[4:8]
            else:
                added.append((s, tile[4:8, piece + 2 : piece + 3]))
    lane = lane_of((4, LANES))
    for s, column in added:
        marks[s] = marks[s] + jnp.where(lane == piece + 2, column, 0.0)
    top, total, column = (marks[:, piece + i : piece + i + 1] for i in range(3))
    first = contract(outs[...], grad_out[...], 1, 0, THREE)
    second = contract(rows[...], tokens[...], 1, 0) - column
    for i in range(n):
        s = slice(i * LANES, (i + 1) * LANES)
        combine = shares[:, s]
        dispatch = jnp.exp(logits[i] - top) / total
        weights[i] = dispatch
        part = combine * first[:, s]
        line = jnp.sum(part, axis=0, keepdims=True)
        out[i] = part - combine * line + dispatch * second[:, s]


def router_part(got, tokens, mine, theirs):
    n = got.shape[0]
    grads = jnp.concatenate([got[e] for e in range(n)], axis=1)
    part = contract(tokens[...], grads, 1, 1, THREE)
    q = part.shape[0] // 4
    low = jnp.concatenate([part[0:q], part[q : 2 * q]], axis=1)
    high = jnp.concatenate([part[2 * q : 3 * q], part[3 * q :]], axis=1)
    core = core_index()
    mine[...] = jnp.where(core == 0, low, high)
    theirs[...] = jnp.where(core == 0, high, low)


def token_grads(got, weights, rows, router, out):
    left = jnp.transpose(jnp.concatenate([router[...], rows[...]], axis=0))
    for e in range(got.shape[0]):
        right = jnp.concatenate([got[e], weights[e]], axis=0)
        out[:, e * LANES : (e + 1) * LANES] = contract(left, right, 1, 0, THREE)


def add_copies(mine, theirs, out):
    both = mine[...] + theirs[...]
    for k in range(out.shape[0]):
        out[k] = both


def add_all(got, out):
    out[...] = jnp.sum(got[...], axis=0)


def unfold(mine, theirs, out):
    core = core_index()
    a, b = mine[...], theirs[...]
    q, h = out.shape[1] // 4, LANES // 2
    for i, values in enumerate((jnp.where(core == 0, a, b), jnp.where(core == 0, b, a))):
        turned = jnp.transpose(values)
        out[:, 2 * i * q : (2 * i + 1) * q] = turned[:h]
        out[:, (2 * i + 1) * q : (2 * i + 2) * q] = turned[h:]


def weight_grads(values, held, grad_in, grad_out, part_in, part_out, sems, first):
    w, hidden = part_in.shape[1:]
    core = core_index()
    base = 2 * core if first else 2 - 2 * core
    tile = held[...]
    cols = jnp.transpose(jnp.where(core == 0, tile[:, 0:w], tile[:, w : 2 * w]))
    step = 512
    copies = []
    for a in range(2):
        i, j = 2 * a, 2 * a + 1
        for n, (part, out, r, q) in enumerate(
            ((part_out, grad_out, 4, 0), (part_in, grad_in, 0, 4))
        ):
            for h in range(0, hidden, step):
                s = slice(h, h + step)
                part[a, :, s] = (
                    cols[:, r + i : r + i + 1] * values[q + i : q + i + 1, s]
                    + cols[:, r + j : r + j + 1] * values[q + j : q + j + 1, s]
                )
            copy = pltpu.make_async_copy(part.at[a], out.at[base + a], sems.at[2 * a + n])
            copy.start()
            copies.append(copy)
    for copy in copies:
        copy.wait()


def own_weight_grads(full, held, grad_in, grad_out, full_on, held_on, part_in, part_out, sems):
    full_on[...] = full[...]
    held_on[...] = held[...]
    weight_grads(full, held, grad_in, grad_out, part_in, part_out, sems, True)


def near_weight_grads(full, held, _, __, grad_in, grad_out, part_in, part_out, sems):
    weight_grads(full, held, grad_in, grad_out, part_in, part_out, sems, False)


def per_device(tokens, router, w_in, w_out, grad_out):
    n_seq, n_exp = lax.axis_size(S), lax.axis_size(E)
    experts, width_block, hidden = w_in.shape
    rows_block, local_tokens = tokens.shape
    slots = router.shape[1]
    chips = n_seq // 2
    piece = 2 * width_block
    core = core_index()
    partner = [(i, i ^ 1) for i in range(n_seq)]
    groups = [[2 * k + c for k in range(chips)] for c in range(2)]
    turned = router.T
    spread = (n_exp, slots, LANES)
    to_owner = [
        ((2 * seat(b, e, f) + c) * n_exp + f, (2 * (2 * f + b) + c) * n_exp + e)
        for b in range(2)
        for e in range(n_exp)
        for c in range(2)
        for f in range(n_exp)
    ]
    from_owner = [(there, here) for here, there in to_owner]

    def to_partner(values):
        return lax.ppermute(values, S, partner)

    def in_hbm(values):
        return pltpu.with_memory_space_constraint(values, pltpu.HBM)

    far_spec = pl.BlockSpec(memory_space=pltpu.HBM)
    vmem_spec = pl.BlockSpec(memory_space=pltpu.VMEM)
    limit = pltpu.CompilerParams(vmem_limit_bytes=40 * 1024 * 1024)
    sent = pl.pallas_call(
        logit_parts,
        out_shape=pltpu.HBM(spread, F32),
        in_specs=[far_spec, far_spec],
        out_specs=far_spec,
        scratch_shapes=[
            pltpu.VMEM(turned.shape, F32),
            pltpu.VMEM((1, rows_block, local_tokens), F32),
            pltpu.VMEM(spread, F32),
            pltpu.SemaphoreType.DMA((2,)),
            pltpu.SemaphoreType.DMA((1,)),
        ],
        compiler_params=limit,
    )(in_hbm(turned), in_hbm(tokens))
    sent, w_in, w_out = lax.optimization_barrier((sent, w_in, w_out))
    got = exchange(sent, E)
    half = (experts // 2,) + w_in.shape[1:]
    staged = pl.pallas_call(
        stage,
        out_shape=[pltpu.HBM(half, F32)] * 2
        + [pltpu.VMEM(half, F32)] * 2
        + [pltpu.VMEM(tokens.shape, F32)],
        in_specs=[far_spec] * 3,
        out_specs=[far_spec] * 2 + [vmem_spec] * 3,
        scratch_shapes=[pltpu.VMEM((2,) + half, F32), pltpu.SemaphoreType.DMA((7,))],
        compiler_params=limit,
    )(in_hbm(w_in), in_hbm(w_out), in_hbm(tokens))
    got, far_in, far_out, own_in, own_out, tokens = lax.optimization_barrier((got, *staged))
    logits = exchange(run(add_spread, spread, got), E)
    weights = (own_in, own_out, to_partner(far_in), to_partner(far_out))

    tiles = (chips, 8, LANES)
    mine, near, shares = run(
        partial_rows,
        [tiles, tiles, (slots, local_tokens)],
        logits,
        tokens,
        grad_out,
        scratch=[(2,) + tiles],
    )
    sent = run(functools.partial(merge_cores, piece=piece), tiles, mine, to_partner(near))
    tile = run(
        functools.partial(merge_chips, piece=piece), (8, LANES), exchange(sent, S, groups)
    )
    share = hidden // chips
    cut = -(-share // LANES) * LANES
    sent, held = run(
        hidden_parts,
        [(chips, 8, cut), (8, LANES)],
        lax.ppermute(tile, (S, E), to_owner),
        *weights,
        scratch=[(8, hidden)],
    )
    sent = run(gate, (chips, 8, cut), exchange(sent, S, groups))
    tile, full = run(
        slot_rows, [(8, LANES), (8, hidden)], exchange(sent, S, groups), held, *weights
    )
    parts = [pltpu.VMEM(half, F32)] * 2 + [pltpu.SemaphoreType.DMA((4,))]
    whole = [pltpu.HBM(w_in.shape, F32)] * 2
    *w_grads, full, held = pl.pallas_call(
        own_weight_grads,
        out_shape=whole + [jax.ShapeDtypeStruct(v.shape, F32) for v in (full, held)],
        in_specs=[vmem_spec] * 2,
        out_specs=[far_spec] * 2 + [vmem_spec] * 2,
        scratch_shapes=parts,
        compiler_params=limit,
    )(full, held)
    tile, full, held, *w_grads = lax.optimization_barrier(
        (lax.ppermute(tile, (S, E), from_owner), full, held, *w_grads)
    )
    mine = exchange(run(copies, tiles, tile), S, groups)
    mine, full, held = lax.optimization_barrier((mine, full, held))
    near, full, held = lax.optimization_barrier(
        (to_partner(mine), to_partner(full), to_partner(held))
    )
    sent, weights, rows = run(
        width_products,
        [spread, spread, (slots, rows_block)],
        mine,
        near,
        tokens,
        grad_out,
        logits,
        shares,
        scratch=[(slots, rows_block), (slots, LANES)],
    )
    sent = run(add_spread, spread, exchange(sent, E))
    grads = exchange(sent, E)
    fold = (rows_block // 4, 2 * slots)
    near, theirs = run(router_part, [fold, fold], grads, tokens)
    w_grads = pl.pallas_call(
        near_weight_grads,
        out_shape=whole,
        in_specs=[vmem_spec] * 2 + [far_spec] * 2,
        out_specs=[far_spec] * 2,
        scratch_shapes=parts,
        input_output_aliases={2: 0, 3: 1},
        compiler_params=limit,
    )(full, held, *(in_hbm(g) for g in w_grads))
    theirs, grad_w_in, grad_w_out = lax.optimization_barrier((to_partner(theirs), *w_grads))
    sent = run(add_copies, (chips,) + fold, near, theirs)
    got, weights, rows = lax.optimization_barrier((exchange(sent, S, groups), weights, rows))
    near = run(add_all, fold, got)
    grad_tokens = run(
        token_grads, (rows_block, local_tokens), grads, weights, rows, turned
    )
    grad_router = run(unfold, (slots, rows_block), near, to_partner(near)).T
    return (grad_tokens, grad_router, grad_w_in, grad_w_out)


def solution(mesh):
    placed = (
        P("expert", "seq"),
        P("expert", None),
        P("expert", "seq", None),
        P("expert", "seq", None),
        P("expert", "seq"),
    )
    return jax.shard_map(
        per_device,
        mesh=mesh,
        in_specs=placed,
        out_specs=(
            P("expert", "seq"),
            P("expert", None),
            P("expert", "seq", None),
            P("expert", "seq", None),
        ),
        check_vma=False,
    )
```

```python
import functools

import jax
import jax.numpy as jnp
from jax import lax
from jax.experimental import pallas as pl
from jax.experimental.pallas import tpu as pltpu
from jax.sharding import PartitionSpec as P

FULL = lax.Precision.HIGHEST
THREE = lax.Precision.HIGH
S = "seq"
E = "expert"
LANES = 128
F32 = jnp.float32


def contract(left, right, left_dim, right_dim, precision=FULL):
    return lax.dot_general(
        left,
        right,
        (((left_dim,), (right_dim,)), ((), ())),
        precision=precision,
        preferred_element_type=F32,
    )


def exchange(blocks, axis, groups=None):
    return lax.all_to_all(blocks, axis, 0, 0, axis_index_groups=groups, tiled=True)


def run(kernel, shapes, *values, scratch=(), flops=0):
    single = not isinstance(shapes, list)
    shapes = [shapes] if single else shapes
    size = 4 * sum(v.size for v in values) + 4 * sum(functools.reduce(lambda a, b: a * b, s) for s in shapes)
    spec = pl.BlockSpec(memory_space=pltpu.VMEM)
    out = pl.pallas_call(
        kernel,
        out_shape=[jax.ShapeDtypeStruct(s, F32) for s in shapes],
        in_specs=[spec] * len(values),
        out_specs=[spec] * len(shapes),
        scratch_shapes=[pltpu.VMEM(s, F32) for s in scratch],
        compiler_params=pltpu.CompilerParams(vmem_limit_bytes=16 * 1024 * 1024),
        cost_estimate=pl.CostEstimate(flops=flops, bytes_accessed=size, transcendentals=0),
    )(*values)
    return out[0] if single else out


def row_of(shape):
    return lax.broadcasted_iota(jnp.int32, shape, len(shape) - 2) % 8


def lane_of(shape):
    return lax.broadcasted_iota(jnp.int32, shape, len(shape) - 1)


def swap(values):
    return jnp.concatenate([values[..., 4:8, :], values[..., 0:4, :]], axis=-2)


def core_index():
    return lax.axis_index(S) % 2


SEATS = (0xE680F7D5, 0xB291A3C4)


def seat(b, e, column):
    index = 2 * (((e >> 1) - (column >> 1)) & 3) + ((e ^ column) & 1)
    if isinstance(column, int):
        value = SEATS[b] >> (4 * index) & 15
    else:
        word = SEATS[b] - (1 << 32 if SEATS[b] >> 31 else 0)
        value = lax.shift_right_logical(jnp.int32(word), 4 * index) & 15
    return (((value >> 3) ^ (column >> 2)) << 3) | (((value & 7) + 2 * (column & 3)) & 7)


def seats(n):
    column = lax.axis_index(E)
    return [(b, e, seat(b, e, column)) for b in range(2) for e in range(n)]


def start_up(router, tokens, w_in, w_out, out, x, far_in, far_out, left, held, sems):
    half = held.shape[1]
    far = pl.ds(half * (1 - core_index()), half)
    pairs = [
        (router, left),
        (tokens, x),
        (w_in.at[far], held.at[0]),
        (w_out.at[far], held.at[1]),
    ]
    copies = [pltpu.make_async_copy(a, b, sems.at[i]) for i, (a, b) in enumerate(pairs)]
    for copy in copies:
        copy.start()
    copies[0].wait()
    copies[1].wait()
    for i, place in enumerate((far_in, far_out)):
        copies[2 + i].wait()
        copies.append(pltpu.make_async_copy(held.at[i], place, sems.at[4 + i]))
        copies[-1].start()
    part = contract(left[...], x[...], 1, 0)
    for i in range(out.shape[0]):
        out[i] = part[:, i * LANES : (i + 1) * LANES]
    for copy in copies[4:]:
        copy.wait()


def load_own(w_in, w_out, own_in, own_out, sems):
    half = own_in.shape[0]
    own = pl.ds(half * core_index(), half)
    copies = [
        pltpu.make_async_copy(w_in.at[own], own_in, sems.at[0]),
        pltpu.make_async_copy(w_out.at[own], own_out, sems.at[1]),
    ]
    for copy in copies:
        copy.start()
    for copy in copies:
        copy.wait()


def add_spread(got, out):
    total = jnp.sum(got[...], axis=0)
    for e in range(out.shape[0]):
        out[e] = total


def partial_rows(got, tokens, grad_out, mine, near, shares, both):
    n, slots = got.shape[0], got.shape[1]
    logits = jnp.concatenate([got[e] for e in range(n)], axis=1)
    raised = jnp.exp(logits - jnp.max(logits, axis=0, keepdims=True))
    combine = raised / jnp.sum(raised, axis=0, keepdims=True)
    shares[...] = combine
    top = jnp.max(logits, axis=1, keepdims=True)
    raised = jnp.exp(logits - top)
    total = jnp.sum(raised, axis=1, keepdims=True)
    rows_in = contract(raised, tokens[...], 1, 1)
    rows_out = contract(combine, grad_out[...], 1, 1, THREE)
    piece = rows_in.shape[1] // 2
    lane = lane_of((slots, LANES))
    marks = jnp.where(lane == piece, top, jnp.where(lane == piece + 1, total, 0.0))
    plain = jnp.where(lane_of((4, LANES)) == piece + 1, 1.0, 0.0)
    for b, e, k in seats(n):
        for c in range(2):
            s, w = slice(8 * e + 4 * c, 8 * e + 4 * c + 4), slice(b * piece, (b + 1) * piece)
            both[c, k, 0:4] = marks[s]
            both[c, k, 4:8] = plain
            both[c, k, 0:4, 0:piece] = rows_in[s, w]
            both[c, k, 4:8, 0:piece] = rows_out[s, w]
    core = core_index()
    mine[...] = both[core]
    near[...] = both[1 - core]


def merge(parts, piece):
    top = functools.reduce(jnp.maximum, [p[:, piece : piece + 1] for p in parts])
    rows = sum(jnp.exp(p[:, piece : piece + 1] - top) * p for p in parts)
    return jnp.where(lane_of(rows.shape) == piece, top, rows)


def merge_cores(mine, near, out, piece):
    for k in range(out.shape[0]):
        out[k] = merge([mine[k], near[k]], piece)


def merge_chips(got, out, piece):
    out[...] = merge([got[k] for k in range(got.shape[0])], piece)


def hidden_parts(got, own_in, own_out, near_in, near_out, sent, keep, full):
    w = own_in.shape[1]
    piece = 2 * w
    hidden = own_in.shape[2]
    core = core_index()
    rows = got[...]
    scaled = (row_of((8, LANES)) < 4) & (lane_of((8, LANES)) < piece)
    rows = jnp.where(scaled, rows / rows[:, piece + 1 : piece + 2], rows)
    keep[...] = rows
    turned = jnp.transpose(rows)
    low, high = turned[0:w], turned[w:piece]
    own = jnp.where(core == 0, low, high)
    near = jnp.where(core == 0, high, low)
    for a in range(2):
        for kind, mine, theirs in ((0, own_in, near_in), (1, own_out, near_out)):
            r = 4 * kind + 2 * a
            values = [
                jnp.concatenate(
                    [
                        jnp.broadcast_to(own[:, r + p : r + p + 1], (w, LANES)),
                        jnp.broadcast_to(near[:, r + p : r + p + 1], (w, LANES)),
                    ],
                    axis=0,
                )
                for p in range(2)
            ]
            for h in range(0, hidden, LANES):
                s = slice(h, h + LANES)
                block = jnp.concatenate([mine[a, :, s], theirs[a, :, s]], axis=0)
                for p in range(2):
                    full[r + p : r + p + 1, s] = jnp.sum(block * values[p], axis=0, keepdims=True)
    chips = sent.shape[0]
    share = hidden // chips
    for k in range(chips):
        sent[k, :, 0:share] = full[:, k * share : (k + 1) * share]
        sent[k, :, share:] = jnp.zeros((8, sent.shape[2] - share), F32)


def gate(got, out):
    z = jnp.sum(got[...], axis=0)
    other = swap(z)
    first = row_of(z.shape) < 4
    pre = jnp.where(first, z, other)
    grad = jnp.where(first, other, z)
    c = 0.7978845608028654
    t = jnp.tanh(c * (pre + 0.044715 * (pre * pre * pre)))
    act = 0.5 * pre * (1.0 + t)
    slope = 0.5 * (1.0 + t) + 0.5 * pre * (1.0 - t * t) * (c * (1.0 + 3 * 0.044715 * (pre * pre)))
    both = jnp.where(first, act, grad * slope)
    for k in range(out.shape[0]):
        out[k] = both


def slot_rows(got, keep, own_in, own_out, near_in, near_out, out, full):
    w = own_in.shape[1]
    piece = 2 * w
    hidden = own_in.shape[2]
    chips = got.shape[0]
    share = hidden // chips
    core = core_index()
    for k in range(chips):
        full[:, k * share : (k + 1) * share] = got[k, :, 0:share]
    lane = lane_of((piece, LANES))
    cols = jnp.zeros((piece, LANES), F32)
    for a in range(2):
        for kind, mine, theirs in ((0, own_out, near_out), (1, own_in, near_in)):
            r = 4 * kind + 2 * a
            sums = [jnp.zeros((piece, LANES), F32) for _ in range(2)]
            for h in range(0, hidden, LANES):
                s = slice(h, h + LANES)
                block = jnp.concatenate([mine[a, :, s], theirs[a, :, s]], axis=0)
                for p in range(2):
                    sums[p] = sums[p] + block * full[r + p : r + p + 1, s]
            for p in range(2):
                cols = jnp.where(lane == r + p, jnp.sum(sums[p], axis=1, keepdims=True), cols)
    own, near = cols[0:w], cols[w:]
    low = jnp.where(core == 0, own, near)
    high = jnp.where(core == 0, near, own)
    square = jnp.concatenate([low, high, jnp.zeros((LANES - piece, LANES), F32)], axis=0)
    rows = jnp.transpose(square)[0:8]
    held = swap(keep[...])
    lane = lane_of((8, LANES))
    column = jnp.sum(jnp.where(lane < piece, held * rows, 0.0), axis=1, keepdims=True)
    out[...] = jnp.where(lane < piece, rows, jnp.where(lane == piece + 2, column, held))


def copies(tile, out):
    value = tile[...]
    for k in range(out.shape[0]):
        out[k] = value


def width_products(mine, near, tokens, grad_out, logits, shares, out, weights, rows, outs, marks):
    n = out.shape[0]
    piece = rows.shape[1] // 2
    core = core_index()
    added = []
    for c in range(2):
        for b, e, k in seats(n):
            tile = jnp.where(core == c, mine[k], near[k])
            s, w = slice(8 * e + 4 * c, 8 * e + 4 * c + 4), slice(b * piece, (b + 1) * piece)
            outs[s, w] = tile[0:4, 0:piece]
            rows[s, w] = tile[4:8, 0:piece]
            if b == 0:
                marks[s] = tile[4:8]
            else:
                added.append((s, tile[4:8, piece + 2 : piece + 3]))
    lane = lane_of((4, LANES))
    for s, column in added:
        marks[s] = marks[s] + jnp.where(lane == piece + 2, column, 0.0)
    top, total, column = (marks[:, piece + i : piece + i + 1] for i in range(3))
    first = contract(outs[...], grad_out[...], 1, 0, THREE)
    second = contract(rows[...], tokens[...], 1, 0) - column
    for i in range(n):
        s = slice(i * LANES, (i + 1) * LANES)
        combine = shares[:, s]
        dispatch = jnp.exp(logits[i] - top) / total
        weights[i] = dispatch
        part = combine * first[:, s]
        line = jnp.sum(part, axis=0, keepdims=True)
        out[i] = part - combine * line + dispatch * second[:, s]


def router_part(got, tokens, mine, theirs):
    n = got.shape[0]
    grads = jnp.concatenate([got[e] for e in range(n)], axis=1)
    part = contract(tokens[...], grads, 1, 1, THREE)
    q = part.shape[0] // 4
    low = jnp.concatenate([part[0:q], part[q : 2 * q]], axis=1)
    high = jnp.concatenate([part[2 * q : 3 * q], part[3 * q :]], axis=1)
    core = core_index()
    mine[...] = jnp.where(core == 0, low, high)
    theirs[...] = jnp.where(core == 0, high, low)


def token_grads(got, weights, rows, router, out):
    left = jnp.transpose(jnp.concatenate([router[...], rows[...]], axis=0))
    for e in range(got.shape[0]):
        right = jnp.concatenate([got[e], weights[e]], axis=0)
        out[:, e * LANES : (e + 1) * LANES] = contract(left, right, 1, 0, THREE)


def add_copies(mine, theirs, out):
    both = mine[...] + theirs[...]
    for k in range(out.shape[0]):
        out[k] = both


def add_all(got, out):
    out[...] = jnp.sum(got[...], axis=0)


def unfold(mine, theirs, out):
    core = core_index()
    a, b = mine[...], theirs[...]
    q, h = out.shape[1] // 4, LANES // 2
    for i, values in enumerate((jnp.where(core == 0, a, b), jnp.where(core == 0, b, a))):
        turned = jnp.transpose(values)
        out[:, 2 * i * q : (2 * i + 1) * q] = turned[:h]
        out[:, (2 * i + 1) * q : (2 * i + 2) * q] = turned[h:]


def weight_grads(full, near_full, keep, near_keep, grad_in, grad_out):
    w = grad_in.shape[1]
    hidden = grad_in.shape[2]
    core = core_index()
    step = 512
    for base, values, held in ((2 * core, full, keep), (2 - 2 * core, near_full, near_keep)):
        held = held[...]
        part = jnp.where(core == 0, held[:, 0:w], held[:, w : 2 * w])
        cols = jnp.transpose(part)
        for a in range(2):
            for h in range(0, hidden, step):
                s = slice(h, h + step)
                i, j = 2 * a, 2 * a + 1
                grad_out[base + a, :, s] = (
                    cols[:, 4 + i : 5 + i] * values[i : i + 1, s]
                    + cols[:, 4 + j : 5 + j] * values[j : j + 1, s]
                )
                grad_in[base + a, :, s] = (
                    cols[:, i : i + 1] * values[4 + i : 5 + i, s]
                    + cols[:, j : j + 1] * values[4 + j : 5 + j, s]
                )


def per_device(tokens, router, w_in, w_out, grad_out):
    n_seq, n_exp = lax.axis_size(S), lax.axis_size(E)
    experts, width_block, hidden = w_in.shape
    rows_block, local_tokens = tokens.shape
    slots = router.shape[1]
    chips = n_seq // 2
    piece = 2 * width_block
    core = core_index()
    partner = [(i, i ^ 1) for i in range(n_seq)]
    groups = [[2 * k + c for k in range(chips)] for c in range(2)]
    turned = router.T
    spread = (n_exp, slots, LANES)
    to_owner = [
        ((2 * seat(b, e, f) + c) * n_exp + f, (2 * (2 * f + b) + c) * n_exp + e)
        for b in range(2)
        for e in range(n_exp)
        for c in range(2)
        for f in range(n_exp)
    ]
    from_owner = [(there, here) for here, there in to_owner]

    def to_partner(values):
        return lax.ppermute(values, S, partner)

    def in_hbm(values):
        return pltpu.with_memory_space_constraint(values, pltpu.HBM)

    far_spec = pl.BlockSpec(memory_space=pltpu.HBM)
    vmem_spec = pl.BlockSpec(memory_space=pltpu.VMEM)
    limit = pltpu.CompilerParams(vmem_limit_bytes=16 * 1024 * 1024)
    half = (experts // 2,) + w_in.shape[1:]
    sent, tokens, far_in, far_out = pl.pallas_call(
        start_up,
        out_shape=[
            pltpu.VMEM(spread, F32),
            pltpu.VMEM(tokens.shape, F32),
            pltpu.HBM(half, F32),
            pltpu.HBM(half, F32),
        ],
        in_specs=[far_spec] * 4,
        out_specs=[vmem_spec] * 2 + [far_spec] * 2,
        scratch_shapes=[
            pltpu.VMEM(turned.shape, F32),
            pltpu.VMEM((2,) + half, F32),
            pltpu.SemaphoreType.DMA((6,)),
        ],
        compiler_params=limit,
    )(in_hbm(turned), in_hbm(tokens), in_hbm(w_in), in_hbm(w_out))
    near_in, near_out = to_partner(far_in), to_partner(far_out)
    logits = exchange(run(add_spread, spread, exchange(sent, E)), E)

    tiles = (chips, 8, LANES)
    mine, near, shares = run(
        partial_rows,
        [tiles, tiles, (slots, local_tokens)],
        logits,
        tokens,
        grad_out,
        scratch=[(2,) + tiles],
    )
    sent = run(functools.partial(merge_cores, piece=piece), tiles, mine, to_partner(near))
    tile = run(
        functools.partial(merge_chips, piece=piece), (8, LANES), exchange(sent, S, groups)
    )
    tile, w_in, w_out = lax.optimization_barrier((tile, w_in, w_out))
    own_in, own_out = pl.pallas_call(
        load_own,
        out_shape=[pltpu.VMEM(half, F32)] * 2,
        in_specs=[far_spec] * 2,
        out_specs=[vmem_spec] * 2,
        scratch_shapes=[pltpu.SemaphoreType.DMA((2,))],
        compiler_params=limit,
    )(in_hbm(w_in), in_hbm(w_out))
    tile, own_in, own_out = lax.optimization_barrier(
        (lax.ppermute(tile, (S, E), to_owner), own_in, own_out)
    )
    weights = (own_in, own_out, near_in, near_out)
    share = hidden // chips
    cut = -(-share // LANES) * LANES
    sent, held = run(
        hidden_parts,
        [(chips, 8, cut), (8, LANES)],
        tile,
        *weights,
        scratch=[(8, hidden)],
    )
    sent = run(gate, (chips, 8, cut), exchange(sent, S, groups))
    tile, full = run(
        slot_rows, [(8, LANES), (8, hidden)], exchange(sent, S, groups), held, *weights
    )
    grad_w_in, grad_w_out = run(
        weight_grads,
        [w_in.shape, w_out.shape],
        full,
        to_partner(full),
        held,
        to_partner(held),
    )
    tile, grad_w_in, grad_w_out = lax.optimization_barrier(
        (lax.ppermute(tile, (S, E), from_owner), grad_w_in, grad_w_out)
    )
    sent = run(copies, tiles, tile)
    mine = exchange(sent, S, groups)
    near = to_partner(mine)
    sent, weights, rows = run(
        width_products,
        [spread, spread, (slots, rows_block)],
        mine,
        near,
        tokens,
        grad_out,
        logits,
        shares,
        scratch=[(slots, rows_block), (slots, LANES)],
    )
    sent = run(add_spread, spread, exchange(sent, E))
    grads = exchange(sent, E)
    fold = (rows_block // 4, 2 * slots)
    near, theirs = run(router_part, [fold, fold], grads, tokens)
    sent = run(add_copies, (chips,) + fold, near, to_partner(theirs))
    got, weights, rows = lax.optimization_barrier((exchange(sent, S, groups), weights, rows))
    near = run(add_all, fold, got)
    grad_tokens = run(
        token_grads, (rows_block, local_tokens), grads, weights, rows, turned
    )
    grad_router = run(unfold, (slots, rows_block), near, to_partner(near)).T
    return (grad_tokens, grad_router, grad_w_in, grad_w_out)


def solution(mesh):
    placed = (
        P("expert", "seq"),
        P("expert", None),
        P("expert", "seq", None),
        P("expert", "seq", None),
        P("expert", "seq"),
    )
    return jax.shard_map(
        per_device,
        mesh=mesh,
        in_specs=placed,
        out_specs=(
            P("expert", "seq"),
            P("expert", None),
            P("expert", "seq", None),
            P("expert", "seq", None),
        ),
        check_vma=False,
    )
```

```python
import functools

import jax
import jax.numpy as jnp
from jax import lax
from jax.experimental import pallas as pl
from jax.experimental.pallas import tpu as pltpu
from jax.sharding import PartitionSpec as P

FULL = lax.Precision.HIGHEST
THREE = lax.Precision.HIGH
S = "seq"
E = "expert"
LANES = 128
F32 = jnp.float32


def contract(left, right, left_dim, right_dim, precision=FULL):
    return lax.dot_general(
        left,
        right,
        (((left_dim,), (right_dim,)), ((), ())),
        precision=precision,
        preferred_element_type=F32,
    )


def exchange(blocks, axis, groups=None):
    return lax.all_to_all(blocks, axis, 0, 0, axis_index_groups=groups, tiled=True)


def run(kernel, shapes, *values, scratch=(), flops=0):
    single = not isinstance(shapes, list)
    shapes = [shapes] if single else shapes
    size = 4 * sum(v.size for v in values) + 4 * sum(functools.reduce(lambda a, b: a * b, s) for s in shapes)
    spec = pl.BlockSpec(memory_space=pltpu.VMEM)
    out = pl.pallas_call(
        kernel,
        out_shape=[jax.ShapeDtypeStruct(s, F32) for s in shapes],
        in_specs=[spec] * len(values),
        out_specs=[spec] * len(shapes),
        scratch_shapes=[pltpu.VMEM(s, F32) for s in scratch],
        compiler_params=pltpu.CompilerParams(vmem_limit_bytes=16 * 1024 * 1024),
        cost_estimate=pl.CostEstimate(flops=flops, bytes_accessed=size, transcendentals=0),
    )(*values)
    return out[0] if single else out


def row_of(shape):
    return lax.broadcasted_iota(jnp.int32, shape, len(shape) - 2) % 8


def lane_of(shape):
    return lax.broadcasted_iota(jnp.int32, shape, len(shape) - 1)


def swap(values):
    return jnp.concatenate([values[..., 4:8, :], values[..., 0:4, :]], axis=-2)


def core_index():
    return lax.axis_index(S) % 2


SEATS = (0xE680F7D5, 0xB291A3C4)


def seat(b, e, column):
    index = 2 * (((e >> 1) - (column >> 1)) & 3) + ((e ^ column) & 1)
    if isinstance(column, int):
        value = SEATS[b] >> (4 * index) & 15
    else:
        word = SEATS[b] - (1 << 32 if SEATS[b] >> 31 else 0)
        value = lax.shift_right_logical(jnp.int32(word), 4 * index) & 15
    return (((value >> 3) ^ (column >> 2)) << 3) | (((value & 7) + 2 * (column & 3)) & 7)


def seats(n):
    column = lax.axis_index(E)
    return [(b, e, seat(b, e, column)) for b in range(2) for e in range(n)]


def start_up(router, tokens, w_in, w_out, out, x, away, left, sems):
    half = away.shape[1]
    far = pl.ds(half * (1 - core_index()), half)
    pairs = [
        (router, left),
        (tokens, x),
        (w_in.at[far], away.at[0]),
        (w_out.at[far], away.at[1]),
    ]
    copies = [pltpu.make_async_copy(a, b, sems.at[i]) for i, (a, b) in enumerate(pairs)]
    for copy in copies:
        copy.start()
    copies[0].wait()
    copies[1].wait()
    part = contract(left[...], x[...], 1, 0)
    for i in range(out.shape[0]):
        out[i] = part[:, i * LANES : (i + 1) * LANES]
    copies[2].wait()
    copies[3].wait()


def load_own(w_in, w_out, own_in, own_out, sems):
    half = own_in.shape[0]
    own = pl.ds(half * core_index(), half)
    copies = [
        pltpu.make_async_copy(w_in.at[own], own_in, sems.at[0]),
        pltpu.make_async_copy(w_out.at[own], own_out, sems.at[1]),
    ]
    for copy in copies:
        copy.start()
    for copy in copies:
        copy.wait()


def add_spread(got, out):
    total = jnp.sum(got[...], axis=0)
    for e in range(out.shape[0]):
        out[e] = total


def partial_rows(got, tokens, grad_out, mine, near, shares, both):
    n, slots = got.shape[0], got.shape[1]
    logits = jnp.concatenate([got[e] for e in range(n)], axis=1)
    raised = jnp.exp(logits - jnp.max(logits, axis=0, keepdims=True))
    combine = raised / jnp.sum(raised, axis=0, keepdims=True)
    shares[...] = combine
    top = jnp.max(logits, axis=1, keepdims=True)
    raised = jnp.exp(logits - top)
    total = jnp.sum(raised, axis=1, keepdims=True)
    rows_in = contract(raised, tokens[...], 1, 1)
    rows_out = contract(combine, grad_out[...], 1, 1, THREE)
    piece = rows_in.shape[1] // 2
    lane = lane_of((slots, LANES))
    marks = jnp.where(lane == piece, top, jnp.where(lane == piece + 1, total, 0.0))
    plain = jnp.where(lane_of((4, LANES)) == piece + 1, 1.0, 0.0)
    for b, e, k in seats(n):
        for c in range(2):
            s, w = slice(8 * e + 4 * c, 8 * e + 4 * c + 4), slice(b * piece, (b + 1) * piece)
            both[c, k, 0:4] = marks[s]
            both[c, k, 4:8] = plain
            both[c, k, 0:4, 0:piece] = rows_in[s, w]
            both[c, k, 4:8, 0:piece] = rows_out[s, w]
    core = core_index()
    mine[...] = both[core]
    near[...] = both[1 - core]


def merge(parts, piece):
    top = functools.reduce(jnp.maximum, [p[:, piece : piece + 1] for p in parts])
    rows = sum(jnp.exp(p[:, piece : piece + 1] - top) * p for p in parts)
    return jnp.where(lane_of(rows.shape) == piece, top, rows)


def merge_cores(mine, near, out, piece):
    for k in range(out.shape[0]):
        out[k] = merge([mine[k], near[k]], piece)


def merge_chips(got, out, piece):
    out[...] = merge([got[k] for k in range(got.shape[0])], piece)


def hidden_parts(got, own_in, own_out, others, sent, keep, full):
    w = own_in.shape[1]
    piece = 2 * w
    hidden = own_in.shape[2]
    core = core_index()
    rows = got[...]
    scaled = (row_of((8, LANES)) < 4) & (lane_of((8, LANES)) < piece)
    rows = jnp.where(scaled, rows / rows[:, piece + 1 : piece + 2], rows)
    keep[...] = rows
    turned = jnp.transpose(rows)
    low, high = turned[0:w], turned[w:piece]
    own = jnp.where(core == 0, low, high)
    near = jnp.where(core == 0, high, low)
    for a in range(2):
        for kind, mine, theirs in ((0, own_in, others.at[0]), (1, own_out, others.at[1])):
            r = 4 * kind + 2 * a
            values = [
                jnp.concatenate(
                    [
                        jnp.broadcast_to(own[:, r + p : r + p + 1], (w, LANES)),
                        jnp.broadcast_to(near[:, r + p : r + p + 1], (w, LANES)),
                    ],
                    axis=0,
                )
                for p in range(2)
            ]
            for h in range(0, hidden, LANES):
                s = slice(h, h + LANES)
                block = jnp.concatenate([mine[a, :, s], theirs[a, :, s]], axis=0)
                for p in range(2):
                    full[r + p : r + p + 1, s] = jnp.sum(block * values[p], axis=0, keepdims=True)
    chips = sent.shape[0]
    share = hidden // chips
    for k in range(chips):
        sent[k, :, 0:share] = full[:, k * share : (k + 1) * share]
        sent[k, :, share:] = jnp.zeros((8, sent.shape[2] - share), F32)


def gate(got, out):
    z = jnp.sum(got[...], axis=0)
    other = swap(z)
    first = row_of(z.shape) < 4
    pre = jnp.where(first, z, other)
    grad = jnp.where(first, other, z)
    c = 0.7978845608028654
    t = jnp.tanh(c * (pre + 0.044715 * (pre * pre * pre)))
    act = 0.5 * pre * (1.0 + t)
    slope = 0.5 * (1.0 + t) + 0.5 * pre * (1.0 - t * t) * (c * (1.0 + 3 * 0.044715 * (pre * pre)))
    both = jnp.where(first, act, grad * slope)
    for k in range(out.shape[0]):
        out[k] = both


def slot_rows(got, keep, own_in, own_out, others, out, full):
    w = own_in.shape[1]
    piece = 2 * w
    hidden = own_in.shape[2]
    chips = got.shape[0]
    share = hidden // chips
    core = core_index()
    for k in range(chips):
        full[:, k * share : (k + 1) * share] = got[k, :, 0:share]
    lane = lane_of((piece, LANES))
    cols = jnp.zeros((piece, LANES), F32)
    for a in range(2):
        for kind, mine, theirs in ((0, own_out, others.at[1]), (1, own_in, others.at[0])):
            r = 4 * kind + 2 * a
            sums = [jnp.zeros((piece, LANES), F32) for _ in range(2)]
            for h in range(0, hidden, LANES):
                s = slice(h, h + LANES)
                block = jnp.concatenate([mine[a, :, s], theirs[a, :, s]], axis=0)
                for p in range(2):
                    sums[p] = sums[p] + block * full[r + p : r + p + 1, s]
            for p in range(2):
                cols = jnp.where(lane == r + p, jnp.sum(sums[p], axis=1, keepdims=True), cols)
    own, near = cols[0:w], cols[w:]
    low = jnp.where(core == 0, own, near)
    high = jnp.where(core == 0, near, own)
    square = jnp.concatenate([low, high, jnp.zeros((LANES - piece, LANES), F32)], axis=0)
    rows = jnp.transpose(square)[0:8]
    full[:, hidden:] = keep[...]
    held = swap(keep[...])
    lane = lane_of((8, LANES))
    column = jnp.sum(jnp.where(lane < piece, held * rows, 0.0), axis=1, keepdims=True)
    out[...] = jnp.where(lane < piece, rows, jnp.where(lane == piece + 2, column, held))


def copies(tile, out):
    value = tile[...]
    for k in range(out.shape[0]):
        out[k] = value


def width_products(mine, near, tokens, grad_out, logits, shares, out, weights, rows, outs, marks):
    n = out.shape[0]
    piece = rows.shape[1] // 2
    core = core_index()
    added = []
    for c in range(2):
        for b, e, k in seats(n):
            tile = jnp.where(core == c, mine[k], near[k])
            s, w = slice(8 * e + 4 * c, 8 * e + 4 * c + 4), slice(b * piece, (b + 1) * piece)
            outs[s, w] = tile[0:4, 0:piece]
            rows[s, w] = tile[4:8, 0:piece]
            if b == 0:
                marks[s] = tile[4:8]
            else:
                added.append((s, tile[4:8, piece + 2 : piece + 3]))
    lane = lane_of((4, LANES))
    for s, column in added:
        marks[s] = marks[s] + jnp.where(lane == piece + 2, column, 0.0)
    top, total, column = (marks[:, piece + i : piece + i + 1] for i in range(3))
    first = contract(outs[...], grad_out[...], 1, 0, THREE)
    second = contract(rows[...], tokens[...], 1, 0) - column
    for i in range(n):
        s = slice(i * LANES, (i + 1) * LANES)
        combine = shares[:, s]
        dispatch = jnp.exp(logits[i] - top) / total
        weights[i] = dispatch
        part = combine * first[:, s]
        line = jnp.sum(part, axis=0, keepdims=True)
        out[i] = part - combine * line + dispatch * second[:, s]


def router_part(got, tokens, mine, theirs):
    n = got.shape[0]
    grads = jnp.concatenate([got[e] for e in range(n)], axis=1)
    part = contract(tokens[...], grads, 1, 1, THREE)
    q = part.shape[0] // 4
    low = jnp.concatenate([part[0:q], part[q : 2 * q]], axis=1)
    high = jnp.concatenate([part[2 * q : 3 * q], part[3 * q :]], axis=1)
    core = core_index()
    mine[...] = jnp.where(core == 0, low, high)
    theirs[...] = jnp.where(core == 0, high, low)


def token_grads(got, weights, rows, router, out):
    left = jnp.transpose(jnp.concatenate([router[...], rows[...]], axis=0))
    for e in range(got.shape[0]):
        right = jnp.concatenate([got[e], weights[e]], axis=0)
        out[:, e * LANES : (e + 1) * LANES] = contract(left, right, 1, 0, THREE)


def add_copies(mine, theirs, out):
    both = mine[...] + theirs[...]
    for k in range(out.shape[0]):
        out[k] = both


def add_all(got, out):
    out[...] = jnp.sum(got[...], axis=0)


def unfold(mine, theirs, out):
    core = core_index()
    a, b = mine[...], theirs[...]
    q, h = out.shape[1] // 4, LANES // 2
    for i, values in enumerate((jnp.where(core == 0, a, b), jnp.where(core == 0, b, a))):
        turned = jnp.transpose(values)
        out[:, 2 * i * q : (2 * i + 1) * q] = turned[:h]
        out[:, (2 * i + 1) * q : (2 * i + 2) * q] = turned[h:]


def weight_grads(full, near, grad_in, grad_out):
    w = grad_in.shape[1]
    hidden = grad_in.shape[2]
    core = core_index()
    step = 512
    for base, values in ((2 * core, full), (2 - 2 * core, near)):
        held = values[:, hidden:]
        part = jnp.where(core == 0, held[:, 0:w], held[:, w : 2 * w])
        cols = jnp.transpose(part)
        for a in range(2):
            for h in range(0, hidden, step):
                s = slice(h, h + step)
                i, j = 2 * a, 2 * a + 1
                grad_out[base + a, :, s] = (
                    cols[:, 4 + i : 5 + i] * values[i : i + 1, s]
                    + cols[:, 4 + j : 5 + j] * values[j : j + 1, s]
                )
                grad_in[base + a, :, s] = (
                    cols[:, i : i + 1] * values[4 + i : 5 + i, s]
                    + cols[:, j : j + 1] * values[4 + j : 5 + j, s]
                )


def per_device(tokens, router, w_in, w_out, grad_out):
    n_seq, n_exp = lax.axis_size(S), lax.axis_size(E)
    experts, width_block, hidden = w_in.shape
    rows_block, local_tokens = tokens.shape
    slots = router.shape[1]
    chips = n_seq // 2
    piece = 2 * width_block
    core = core_index()
    partner = [(i, i ^ 1) for i in range(n_seq)]
    groups = [[2 * k + c for k in range(chips)] for c in range(2)]
    turned = router.T
    spread = (n_exp, slots, LANES)
    to_owner = [
        ((2 * seat(b, e, f) + c) * n_exp + f, (2 * (2 * f + b) + c) * n_exp + e)
        for b in range(2)
        for e in range(n_exp)
        for c in range(2)
        for f in range(n_exp)
    ]
    from_owner = [(there, here) for here, there in to_owner]

    def to_partner(values):
        return lax.ppermute(values, S, partner)

    def in_hbm(values):
        return pltpu.with_memory_space_constraint(values, pltpu.HBM)

    far_spec = pl.BlockSpec(memory_space=pltpu.HBM)
    vmem_spec = pl.BlockSpec(memory_space=pltpu.VMEM)
    limit = pltpu.CompilerParams(vmem_limit_bytes=16 * 1024 * 1024)
    half = (experts // 2,) + w_in.shape[1:]
    sent, tokens, away = pl.pallas_call(
        start_up,
        out_shape=[
            pltpu.VMEM(spread, F32),
            pltpu.VMEM(tokens.shape, F32),
            pltpu.VMEM((2,) + half, F32),
        ],
        in_specs=[far_spec] * 4,
        out_specs=[vmem_spec] * 3,
        scratch_shapes=[pltpu.VMEM(turned.shape, F32), pltpu.SemaphoreType.DMA((4,))],
        compiler_params=limit,
    )(in_hbm(turned), in_hbm(tokens), in_hbm(w_in), in_hbm(w_out))
    others = to_partner(away)
    logits = exchange(run(add_spread, spread, exchange(sent, E)), E)

    tiles = (chips, 8, LANES)
    mine, near, shares = run(
        partial_rows,
        [tiles, tiles, (slots, local_tokens)],
        logits,
        tokens,
        grad_out,
        scratch=[(2,) + tiles],
    )
    sent = run(functools.partial(merge_cores, piece=piece), tiles, mine, to_partner(near))
    tile = run(
        functools.partial(merge_chips, piece=piece), (8, LANES), exchange(sent, S, groups)
    )
    tile, w_in, w_out = lax.optimization_barrier((tile, w_in, w_out))
    own_in, own_out = pl.pallas_call(
        load_own,
        out_shape=[pltpu.VMEM(half, F32)] * 2,
        in_specs=[far_spec] * 2,
        out_specs=[vmem_spec] * 2,
        scratch_shapes=[pltpu.SemaphoreType.DMA((2,))],
        compiler_params=limit,
    )(in_hbm(w_in), in_hbm(w_out))
    tile, own_in, own_out = lax.optimization_barrier(
        (lax.ppermute(tile, (S, E), to_owner), own_in, own_out)
    )
    weights = (own_in, own_out, others)
    share = hidden // chips
    cut = -(-share // LANES) * LANES
    sent, held = run(
        hidden_parts,
        [(chips, 8, cut), (8, LANES)],
        tile,
        *weights,
        scratch=[(8, hidden)],
    )
    sent = run(gate, (chips, 8, cut), exchange(sent, S, groups))
    tile, full = run(
        slot_rows, [(8, LANES), (8, hidden + LANES)], exchange(sent, S, groups), held, *weights
    )
    grad_w_in, grad_w_out = run(
        weight_grads, [w_in.shape, w_out.shape], full, to_partner(full)
    )
    tile, grad_w_in, grad_w_out = lax.optimization_barrier(
        (lax.ppermute(tile, (S, E), from_owner), grad_w_in, grad_w_out)
    )
    sent = run(copies, tiles, tile)
    mine = exchange(sent, S, groups)
    near = to_partner(mine)
    sent, weights, rows = run(
        width_products,
        [spread, spread, (slots, rows_block)],
        mine,
        near,
        tokens,
        grad_out,
        logits,
        shares,
        scratch=[(slots, rows_block), (slots, LANES)],
    )
    sent = run(add_spread, spread, exchange(sent, E))
    grads = exchange(sent, E)
    fold = (rows_block // 4, 2 * slots)
    near, theirs = run(router_part, [fold, fold], grads, tokens)
    sent = run(add_copies, (chips,) + fold, near, to_partner(theirs))
    got, weights, rows = lax.optimization_barrier((exchange(sent, S, groups), weights, rows))
    near = run(add_all, fold, got)
    grad_tokens = run(
        token_grads, (rows_block, local_tokens), grads, weights, rows, turned
    )
    grad_router = run(unfold, (slots, rows_block), near, to_partner(near)).T
    return (grad_tokens, grad_router, grad_w_in, grad_w_out)


def solution(mesh):
    placed = (
        P("expert", "seq"),
        P("expert", None),
        P("expert", "seq", None),
        P("expert", "seq", None),
        P("expert", "seq"),
    )
    return jax.shard_map(
        per_device,
        mesh=mesh,
        in_specs=placed,
        out_specs=(
            P("expert", "seq"),
            P("expert", None),
            P("expert", "seq", None),
            P("expert", "seq", None),
        ),
        check_vma=False,
    )
```

```python
import functools

import jax
import jax.numpy as jnp
from jax import lax
from jax.experimental import pallas as pl
from jax.experimental.pallas import tpu as pltpu
from jax.sharding import PartitionSpec as P

FULL = lax.Precision.HIGHEST
THREE = lax.Precision.HIGH
S = "seq"
E = "expert"
LANES = 128
F32 = jnp.float32


def contract(left, right, left_dim, right_dim, precision=FULL):
    return lax.dot_general(
        left,
        right,
        (((left_dim,), (right_dim,)), ((), ())),
        precision=precision,
        preferred_element_type=F32,
    )


def exchange(blocks, axis, groups=None):
    return lax.all_to_all(blocks, axis, 0, 0, axis_index_groups=groups, tiled=True)


def run(kernel, shapes, *values, scratch=(), flops=0):
    single = not isinstance(shapes, list)
    shapes = [shapes] if single else shapes
    size = 4 * sum(v.size for v in values) + 4 * sum(functools.reduce(lambda a, b: a * b, s) for s in shapes)
    spec = pl.BlockSpec(memory_space=pltpu.VMEM)
    out = pl.pallas_call(
        kernel,
        out_shape=[jax.ShapeDtypeStruct(s, F32) for s in shapes],
        in_specs=[spec] * len(values),
        out_specs=[spec] * len(shapes),
        scratch_shapes=[pltpu.VMEM(s, F32) for s in scratch],
        compiler_params=pltpu.CompilerParams(vmem_limit_bytes=16 * 1024 * 1024),
        cost_estimate=pl.CostEstimate(flops=flops, bytes_accessed=size, transcendentals=0),
    )(*values)
    return out[0] if single else out


def row_of(shape):
    return lax.broadcasted_iota(jnp.int32, shape, len(shape) - 2) % 8


def lane_of(shape):
    return lax.broadcasted_iota(jnp.int32, shape, len(shape) - 1)


def swap(values):
    return jnp.concatenate([values[..., 4:8, :], values[..., 0:4, :]], axis=-2)


def core_index():
    return lax.axis_index(S) % 2


SEATS = (0xE680F7D5, 0xB291A3C4)


def seat(b, e, column):
    index = 2 * (((e >> 1) - (column >> 1)) & 3) + ((e ^ column) & 1)
    if isinstance(column, int):
        value = SEATS[b] >> (4 * index) & 15
    else:
        word = SEATS[b] - (1 << 32 if SEATS[b] >> 31 else 0)
        value = lax.shift_right_logical(jnp.int32(word), 4 * index) & 15
    return (((value >> 3) ^ (column >> 2)) << 3) | (((value & 7) + 2 * (column & 3)) & 7)


def seats(n):
    column = lax.axis_index(E)
    return [(b, e, seat(b, e, column)) for b in range(2) for e in range(n)]


def start_up(router, tokens, w_in, w_out, out, x, away, left, sems):
    half = away.shape[1]
    far = pl.ds(half * (1 - core_index()), half)
    pairs = [
        (router, left),
        (tokens, x),
        (w_in.at[far], away.at[0]),
        (w_out.at[far], away.at[1]),
    ]
    copies = [pltpu.make_async_copy(a, b, sems.at[i]) for i, (a, b) in enumerate(pairs)]
    for copy in copies:
        copy.start()
    copies[0].wait()
    copies[1].wait()
    part = contract(left[...], x[...], 1, 0)
    for i in range(out.shape[0]):
        out[i] = part[:, i * LANES : (i + 1) * LANES]
    copies[2].wait()
    copies[3].wait()


def load_own(w_in, w_out, own_in, own_out, sems):
    half = own_in.shape[0]
    own = pl.ds(half * core_index(), half)
    copies = [
        pltpu.make_async_copy(w_in.at[own], own_in, sems.at[0]),
        pltpu.make_async_copy(w_out.at[own], own_out, sems.at[1]),
    ]
    for copy in copies:
        copy.start()
    for copy in copies:
        copy.wait()


def add_spread(got, out):
    total = jnp.sum(got[...], axis=0)
    for e in range(out.shape[0]):
        out[e] = total


def partial_rows(got, tokens, grad_out, mine, near, shares, both):
    n, slots = got.shape[0], got.shape[1]
    logits = jnp.concatenate([got[e] for e in range(n)], axis=1)
    raised = jnp.exp(logits - jnp.max(logits, axis=0, keepdims=True))
    combine = raised / jnp.sum(raised, axis=0, keepdims=True)
    shares[...] = combine
    top = jnp.max(logits, axis=1, keepdims=True)
    raised = jnp.exp(logits - top)
    total = jnp.sum(raised, axis=1, keepdims=True)
    rows_in = contract(raised, tokens[...], 1, 1)
    rows_out = contract(combine, grad_out[...], 1, 1, THREE)
    piece = rows_in.shape[1] // 2
    lane = lane_of((slots, LANES))
    marks = jnp.where(lane == piece, top, jnp.where(lane == piece + 1, total, 0.0))
    plain = jnp.where(lane_of((4, LANES)) == piece + 1, 1.0, 0.0)
    for b, e, k in seats(n):
        for c in range(2):
            s, w = slice(8 * e + 4 * c, 8 * e + 4 * c + 4), slice(b * piece, (b + 1) * piece)
            both[c, k, 0:4] = marks[s]
            both[c, k, 4:8] = plain
            both[c, k, 0:4, 0:piece] = rows_in[s, w]
            both[c, k, 4:8, 0:piece] = rows_out[s, w]
    core = core_index()
    mine[...] = both[core]
    near[...] = both[1 - core]


def merge(parts, piece):
    top = functools.reduce(jnp.maximum, [p[:, piece : piece + 1] for p in parts])
    rows = sum(jnp.exp(p[:, piece : piece + 1] - top) * p for p in parts)
    return jnp.where(lane_of(rows.shape) == piece, top, rows)


def merge_cores(mine, near, out, piece):
    for k in range(out.shape[0]):
        out[k] = merge([mine[k], near[k]], piece)


def merge_chips(got, out, piece):
    out[...] = merge([got[k] for k in range(got.shape[0])], piece)


def hidden_parts(got, own_in, own_out, others, sent, keep, full):
    w = own_in.shape[1]
    piece = 2 * w
    hidden = own_in.shape[2]
    core = core_index()
    rows = got[...]
    scaled = (row_of((8, LANES)) < 4) & (lane_of((8, LANES)) < piece)
    rows = jnp.where(scaled, rows / rows[:, piece + 1 : piece + 2], rows)
    keep[...] = rows
    turned = jnp.transpose(rows)
    low, high = turned[0:w], turned[w:piece]
    own = jnp.where(core == 0, low, high)
    near = jnp.where(core == 0, high, low)
    for a in range(2):
        for kind, mine, theirs in ((0, own_in, others.at[0]), (1, own_out, others.at[1])):
            r = 4 * kind + 2 * a
            values = [
                jnp.concatenate(
                    [
                        jnp.broadcast_to(own[:, r + p : r + p + 1], (w, LANES)),
                        jnp.broadcast_to(near[:, r + p : r + p + 1], (w, LANES)),
                    ],
                    axis=0,
                )
                for p in range(2)
            ]
            for h in range(0, hidden, LANES):
                s = slice(h, h + LANES)
                block = jnp.concatenate([mine[a, :, s], theirs[a, :, s]], axis=0)
                for p in range(2):
                    full[r + p : r + p + 1, s] = jnp.sum(block * values[p], axis=0, keepdims=True)
    chips = sent.shape[0]
    share = hidden // chips
    for k in range(chips):
        sent[k, :, 0:share] = full[:, k * share : (k + 1) * share]
        sent[k, :, share:] = jnp.zeros((8, sent.shape[2] - share), F32)


def gate(got, out):
    z = jnp.sum(got[...], axis=0)
    other = swap(z)
    first = row_of(z.shape) < 4
    pre = jnp.where(first, z, other)
    grad = jnp.where(first, other, z)
    c = 0.7978845608028654
    t = jnp.tanh(c * (pre + 0.044715 * (pre * pre * pre)))
    act = 0.5 * pre * (1.0 + t)
    slope = 0.5 * (1.0 + t) + 0.5 * pre * (1.0 - t * t) * (c * (1.0 + 3 * 0.044715 * (pre * pre)))
    both = jnp.where(first, act, grad * slope)
    for k in range(out.shape[0]):
        out[k] = both


def slot_rows(got, keep, own_in, own_out, others, out, full):
    w = own_in.shape[1]
    piece = 2 * w
    hidden = own_in.shape[2]
    chips = got.shape[0]
    share = hidden // chips
    core = core_index()
    for k in range(chips):
        full[:, k * share : (k + 1) * share] = got[k, :, 0:share]
    lane = lane_of((piece, LANES))
    cols = jnp.zeros((piece, LANES), F32)
    for a in range(2):
        for kind, mine, theirs in ((0, own_out, others.at[1]), (1, own_in, others.at[0])):
            r = 4 * kind + 2 * a
            sums = [jnp.zeros((piece, LANES), F32) for _ in range(2)]
            for h in range(0, hidden, LANES):
                s = slice(h, h + LANES)
                block = jnp.concatenate([mine[a, :, s], theirs[a, :, s]], axis=0)
                for p in range(2):
                    sums[p] = sums[p] + block * full[r + p : r + p + 1, s]
            for p in range(2):
                cols = jnp.where(lane == r + p, jnp.sum(sums[p], axis=1, keepdims=True), cols)
    own, near = cols[0:w], cols[w:]
    low = jnp.where(core == 0, own, near)
    high = jnp.where(core == 0, near, own)
    square = jnp.concatenate([low, high, jnp.zeros((LANES - piece, LANES), F32)], axis=0)
    rows = jnp.transpose(square)[0:8]
    full[:, hidden:] = keep[...]
    held = swap(keep[...])
    lane = lane_of((8, LANES))
    column = jnp.sum(jnp.where(lane < piece, held * rows, 0.0), axis=1, keepdims=True)
    out[...] = jnp.where(lane < piece, rows, jnp.where(lane == piece + 2, column, held))


def copies(tile, out):
    value = tile[...]
    for k in range(out.shape[0]):
        out[k] = value


def width_products(mine, near, tokens, grad_out, logits, shares, out, weights, rows, outs, marks):
    n = out.shape[0]
    piece = rows.shape[1] // 2
    core = core_index()
    added = []
    for c in range(2):
        for b, e, k in seats(n):
            tile = jnp.where(core == c, mine[k], near[k])
            s, w = slice(8 * e + 4 * c, 8 * e + 4 * c + 4), slice(b * piece, (b + 1) * piece)
            outs[s, w] = tile[0:4, 0:piece]
            rows[s, w] = tile[4:8, 0:piece]
            if b == 0:
                marks[s] = tile[4:8]
            else:
                added.append((s, tile[4:8, piece + 2 : piece + 3]))
    lane = lane_of((4, LANES))
    for s, column in added:
        marks[s] = marks[s] + jnp.where(lane == piece + 2, column, 0.0)
    top, total, column = (marks[:, piece + i : piece + i + 1] for i in range(3))
    first = contract(outs[...], grad_out[...], 1, 0, THREE)
    second = contract(rows[...], tokens[...], 1, 0) - column
    for i in range(n):
        s = slice(i * LANES, (i + 1) * LANES)
        combine = shares[:, s]
        dispatch = jnp.exp(logits[i] - top) / total
        weights[i] = dispatch
        part = combine * first[:, s]
        line = jnp.sum(part, axis=0, keepdims=True)
        out[i] = part - combine * line + dispatch * second[:, s]


def router_part(got, tokens, mine, theirs):
    n = got.shape[0]
    grads = jnp.concatenate([got[e] for e in range(n)], axis=1)
    part = contract(tokens[...], grads, 1, 1, THREE)
    q = part.shape[0] // 4
    low = jnp.concatenate([part[0:q], part[q : 2 * q]], axis=1)
    high = jnp.concatenate([part[2 * q : 3 * q], part[3 * q :]], axis=1)
    core = core_index()
    mine[...] = jnp.where(core == 0, low, high)
    theirs[...] = jnp.where(core == 0, high, low)


def token_grads(got, weights, rows, router, out):
    left = jnp.transpose(jnp.concatenate([router[...], rows[...]], axis=0))
    for e in range(got.shape[0]):
        right = jnp.concatenate([got[e], weights[e]], axis=0)
        out[:, e * LANES : (e + 1) * LANES] = contract(left, right, 1, 0, THREE)


def add_copies(a, b, c, d, out):
    total = (a[...] + b[...]) + (c[...] + d[...])
    for k in range(out.shape[0]):
        out[k] = total


def add_all(got, out):
    out[...] = jnp.sum(got[...], axis=0)


def unfold(mine, theirs, out):
    core = core_index()
    a, b = mine[...], theirs[...]
    q, h = out.shape[1] // 4, LANES // 2
    for i, values in enumerate((jnp.where(core == 0, a, b), jnp.where(core == 0, b, a))):
        turned = jnp.transpose(values)
        out[:, 2 * i * q : (2 * i + 1) * q] = turned[:h]
        out[:, (2 * i + 1) * q : (2 * i + 2) * q] = turned[h:]


def weight_grads(full, near, grad_in, grad_out):
    w = grad_in.shape[1]
    hidden = grad_in.shape[2]
    core = core_index()
    step = 512
    for base, values in ((2 * core, full), (2 - 2 * core, near)):
        held = values[:, hidden:]
        part = jnp.where(core == 0, held[:, 0:w], held[:, w : 2 * w])
        cols = jnp.transpose(part)
        for a in range(2):
            for h in range(0, hidden, step):
                s = slice(h, h + step)
                i, j = 2 * a, 2 * a + 1
                grad_out[base + a, :, s] = (
                    cols[:, 4 + i : 5 + i] * values[i : i + 1, s]
                    + cols[:, 4 + j : 5 + j] * values[j : j + 1, s]
                )
                grad_in[base + a, :, s] = (
                    cols[:, i : i + 1] * values[4 + i : 5 + i, s]
                    + cols[:, j : j + 1] * values[4 + j : 5 + j, s]
                )


def per_device(tokens, router, w_in, w_out, grad_out):
    n_seq, n_exp = lax.axis_size(S), lax.axis_size(E)
    experts, width_block, hidden = w_in.shape
    rows_block, local_tokens = tokens.shape
    slots = router.shape[1]
    chips = n_seq // 2
    piece = 2 * width_block
    core = core_index()
    partner = [(i, i ^ 1) for i in range(n_seq)]
    groups = [[2 * k + c for k in range(chips)] for c in range(2)]
    turned = router.T
    spread = (n_exp, slots, LANES)
    to_owner = [
        ((2 * seat(b, e, f) + c) * n_exp + f, (2 * (2 * f + b) + c) * n_exp + e)
        for b in range(2)
        for e in range(n_exp)
        for c in range(2)
        for f in range(n_exp)
    ]
    from_owner = [(there, here) for here, there in to_owner]

    def to_partner(values):
        return lax.ppermute(values, S, partner)

    def in_hbm(values):
        return pltpu.with_memory_space_constraint(values, pltpu.HBM)

    far_spec = pl.BlockSpec(memory_space=pltpu.HBM)
    vmem_spec = pl.BlockSpec(memory_space=pltpu.VMEM)
    limit = pltpu.CompilerParams(vmem_limit_bytes=16 * 1024 * 1024)
    half = (experts // 2,) + w_in.shape[1:]
    sent, tokens, away = pl.pallas_call(
        start_up,
        out_shape=[
            pltpu.VMEM(spread, F32),
            pltpu.VMEM(tokens.shape, F32),
            pltpu.VMEM((2,) + half, F32),
        ],
        in_specs=[far_spec] * 4,
        out_specs=[vmem_spec] * 3,
        scratch_shapes=[pltpu.VMEM(turned.shape, F32), pltpu.SemaphoreType.DMA((4,))],
        compiler_params=limit,
    )(in_hbm(turned), in_hbm(tokens), in_hbm(w_in), in_hbm(w_out))
    others = to_partner(away)
    logits = exchange(run(add_spread, spread, exchange(sent, E)), E)

    tiles = (chips, 8, LANES)
    mine, near, shares = run(
        partial_rows,
        [tiles, tiles, (slots, local_tokens)],
        logits,
        tokens,
        grad_out,
        scratch=[(2,) + tiles],
    )
    sent = run(functools.partial(merge_cores, piece=piece), tiles, mine, to_partner(near))
    tile = run(
        functools.partial(merge_chips, piece=piece), (8, LANES), exchange(sent, S, groups)
    )
    tile, w_in, w_out = lax.optimization_barrier((tile, w_in, w_out))
    own_in, own_out = pl.pallas_call(
        load_own,
        out_shape=[pltpu.VMEM(half, F32)] * 2,
        in_specs=[far_spec] * 2,
        out_specs=[vmem_spec] * 2,
        scratch_shapes=[pltpu.SemaphoreType.DMA((2,))],
        compiler_params=limit,
    )(in_hbm(w_in), in_hbm(w_out))
    tile, own_in, own_out = lax.optimization_barrier(
        (lax.ppermute(tile, (S, E), to_owner), own_in, own_out)
    )
    weights = (own_in, own_out, others)
    share = hidden // chips
    cut = -(-share // LANES) * LANES
    sent, held = run(
        hidden_parts,
        [(chips, 8, cut), (8, LANES)],
        tile,
        *weights,
        scratch=[(8, hidden)],
    )
    sent = run(gate, (chips, 8, cut), exchange(sent, S, groups))
    tile, full = run(
        slot_rows, [(8, LANES), (8, hidden + LANES)], exchange(sent, S, groups), held, *weights
    )
    grad_w_in, grad_w_out = run(
        weight_grads, [w_in.shape, w_out.shape], full, to_partner(full)
    )
    tile, grad_w_in, grad_w_out = lax.optimization_barrier(
        (lax.ppermute(tile, (S, E), from_owner), grad_w_in, grad_w_out)
    )
    sent = run(copies, tiles, tile)
    mine = exchange(sent, S, groups)
    near = to_partner(mine)
    sent, weights, rows = run(
        width_products,
        [spread, spread, (slots, rows_block)],
        mine,
        near,
        tokens,
        grad_out,
        logits,
        shares,
        scratch=[(slots, rows_block), (slots, LANES)],
    )
    sent = run(add_spread, spread, exchange(sent, E))
    grads = exchange(sent, E)
    fold = (rows_block // 4, 2 * slots)
    near, theirs = run(router_part, [fold, fold], grads, tokens)
    across = n_seq // 2
    rows_z = [
        [across * x + 2 * z + c for z in range(across // 2)] for x in range(2) for c in range(2)
    ]
    pairs = [near, to_partner(theirs)]
    pairs.append(lax.ppermute(near, S, [(i, i ^ across) for i in range(n_seq)]))
    pairs.append(lax.ppermute(theirs, S, [(i, i ^ across ^ 1) for i in range(n_seq)]))
    grad_tokens = run(
        token_grads, (rows_block, local_tokens), grads, weights, rows, turned
    )
    *pairs, grad_tokens = lax.optimization_barrier((*pairs, grad_tokens))
    got = exchange(run(add_copies, (across // 2,) + fold, *pairs), S, rows_z)
    near = run(add_all, fold, got)
    grad_router = run(unfold, (slots, rows_block), near, to_partner(near)).T
    return (grad_tokens, grad_router, grad_w_in, grad_w_out)


def solution(mesh):
    placed = (
        P("expert", "seq"),
        P("expert", None),
        P("expert", "seq", None),
        P("expert", "seq", None),
        P("expert", "seq"),
    )
    return jax.shard_map(
        per_device,
        mesh=mesh,
        in_specs=placed,
        out_specs=(
            P("expert", "seq"),
            P("expert", None),
            P("expert", "seq", None),
            P("expert", "seq", None),
        ),
        check_vma=False,
    )
```

```python
import functools

import jax
import jax.numpy as jnp
from jax import lax
from jax.experimental import pallas as pl
from jax.experimental.pallas import tpu as pltpu
from jax.sharding import PartitionSpec as P

FULL = lax.Precision.HIGHEST
THREE = lax.Precision.HIGH
S = "seq"
E = "expert"
LANES = 128
F32 = jnp.float32


def contract(left, right, left_dim, right_dim, precision=FULL):
    return lax.dot_general(
        left,
        right,
        (((left_dim,), (right_dim,)), ((), ())),
        precision=precision,
        preferred_element_type=F32,
    )


def exchange(blocks, axis, groups=None):
    return lax.all_to_all(blocks, axis, 0, 0, axis_index_groups=groups, tiled=True)


def run(kernel, shapes, *values, scratch=(), flops=0):
    single = not isinstance(shapes, list)
    shapes = [shapes] if single else shapes
    size = 4 * sum(v.size for v in values) + 4 * sum(functools.reduce(lambda a, b: a * b, s) for s in shapes)
    spec = pl.BlockSpec(memory_space=pltpu.VMEM)
    out = pl.pallas_call(
        kernel,
        out_shape=[jax.ShapeDtypeStruct(s, F32) for s in shapes],
        in_specs=[spec] * len(values),
        out_specs=[spec] * len(shapes),
        scratch_shapes=[pltpu.VMEM(s, F32) for s in scratch],
        compiler_params=pltpu.CompilerParams(vmem_limit_bytes=16 * 1024 * 1024),
        cost_estimate=pl.CostEstimate(flops=flops, bytes_accessed=size, transcendentals=0),
    )(*values)
    return out[0] if single else out


def row_of(shape):
    return lax.broadcasted_iota(jnp.int32, shape, len(shape) - 2) % 8


def lane_of(shape):
    return lax.broadcasted_iota(jnp.int32, shape, len(shape) - 1)


def swap(values):
    return jnp.concatenate([values[..., 4:8, :], values[..., 0:4, :]], axis=-2)


def core_index():
    return lax.axis_index(S) % 2


SEATS = (0xE680F7D5, 0xB291A3C4)


def seat(b, e, column):
    index = 2 * (((e >> 1) - (column >> 1)) & 3) + ((e ^ column) & 1)
    if isinstance(column, int):
        value = SEATS[b] >> (4 * index) & 15
    else:
        word = SEATS[b] - (1 << 32 if SEATS[b] >> 31 else 0)
        value = lax.shift_right_logical(jnp.int32(word), 4 * index) & 15
    return (((value >> 3) ^ (column >> 2)) << 3) | (((value & 7) + 2 * (column & 3)) & 7)


def seats(n):
    column = lax.axis_index(E)
    return [(b, e, seat(b, e, column)) for b in range(2) for e in range(n)]


def start_up(router, tokens, w_in, w_out, out, x, away, left, sems):
    half = away.shape[1]
    far = pl.ds(half * (1 - core_index()), half)
    pairs = [
        (router, left),
        (tokens, x),
        (w_in.at[far], away.at[0]),
        (w_out.at[far], away.at[1]),
    ]
    copies = [pltpu.make_async_copy(a, b, sems.at[i]) for i, (a, b) in enumerate(pairs)]
    for copy in copies:
        copy.start()
    copies[0].wait()
    copies[1].wait()
    part = contract(left[...], x[...], 1, 0)
    for i in range(out.shape[0]):
        out[i] = part[:, i * LANES : (i + 1) * LANES]
    copies[2].wait()
    copies[3].wait()


def load_own(w_in, w_out, own_in, own_out, sems):
    half = own_in.shape[0]
    own = pl.ds(half * core_index(), half)
    copies = [
        pltpu.make_async_copy(w_in.at[own], own_in, sems.at[0]),
        pltpu.make_async_copy(w_out.at[own], own_out, sems.at[1]),
    ]
    for copy in copies:
        copy.start()
    for copy in copies:
        copy.wait()


def add_spread(got, out):
    total = jnp.sum(got[...], axis=0)
    for e in range(out.shape[0]):
        out[e] = total


def partial_rows(got, tokens, grad_out, mine, near, shares, both):
    n, slots = got.shape[0], got.shape[1]
    logits = jnp.concatenate([got[e] for e in range(n)], axis=1)
    raised = jnp.exp(logits - jnp.max(logits, axis=0, keepdims=True))
    combine = raised / jnp.sum(raised, axis=0, keepdims=True)
    shares[...] = combine
    top = jnp.max(logits, axis=1, keepdims=True)
    raised = jnp.exp(logits - top)
    total = jnp.sum(raised, axis=1, keepdims=True)
    rows_in = contract(raised, tokens[...], 1, 1)
    rows_out = contract(combine, grad_out[...], 1, 1, THREE)
    piece = rows_in.shape[1] // 2
    lane = lane_of((slots, LANES))
    marks = jnp.where(lane == piece, top, jnp.where(lane == piece + 1, total, 0.0))
    plain = jnp.where(lane_of((4, LANES)) == piece + 1, 1.0, 0.0)
    for b, e, k in seats(n):
        for c in range(2):
            s, w = slice(8 * e + 4 * c, 8 * e + 4 * c + 4), slice(b * piece, (b + 1) * piece)
            both[c, k, 0:4] = marks[s]
            both[c, k, 4:8] = plain
            both[c, k, 0:4, 0:piece] = rows_in[s, w]
            both[c, k, 4:8, 0:piece] = rows_out[s, w]
    core = core_index()
    mine[...] = both[core]
    near[...] = both[1 - core]


def merge(parts, piece):
    top = functools.reduce(jnp.maximum, [p[:, piece : piece + 1] for p in parts])
    rows = sum(jnp.exp(p[:, piece : piece + 1] - top) * p for p in parts)
    return jnp.where(lane_of(rows.shape) == piece, top, rows)


def merge_cores(mine, near, out, piece):
    for k in range(out.shape[0]):
        out[k] = merge([mine[k], near[k]], piece)


def merge_chips(got, out, piece):
    out[...] = merge([got[k] for k in range(got.shape[0])], piece)


def hidden_parts(got, own_in, own_out, others, sent, keep, full):
    w = own_in.shape[1]
    piece = 2 * w
    hidden = own_in.shape[2]
    core = core_index()
    rows = got[...]
    scaled = (row_of((8, LANES)) < 4) & (lane_of((8, LANES)) < piece)
    rows = jnp.where(scaled, rows / rows[:, piece + 1 : piece + 2], rows)
    keep[...] = rows
    turned = jnp.transpose(rows)
    low, high = turned[0:w], turned[w:piece]
    own = jnp.where(core == 0, low, high)
    near = jnp.where(core == 0, high, low)
    for a in range(2):
        for kind, mine, theirs in ((0, own_in, others.at[0]), (1, own_out, others.at[1])):
            r = 4 * kind + 2 * a
            values = [
                jnp.concatenate(
                    [
                        jnp.broadcast_to(own[:, r + p : r + p + 1], (w, LANES)),
                        jnp.broadcast_to(near[:, r + p : r + p + 1], (w, LANES)),
                    ],
                    axis=0,
                )
                for p in range(2)
            ]
            for h in range(0, hidden, LANES):
                s = slice(h, h + LANES)
                block = jnp.concatenate([mine[a, :, s], theirs[a, :, s]], axis=0)
                for p in range(2):
                    full[r + p : r + p + 1, s] = jnp.sum(block * values[p], axis=0, keepdims=True)
    chips = sent.shape[0]
    share = hidden // chips
    for k in range(chips):
        sent[k, :, 0:share] = full[:, k * share : (k + 1) * share]
        sent[k, :, share:] = jnp.zeros((8, sent.shape[2] - share), F32)


def gate(got, out):
    z = jnp.sum(got[...], axis=0)
    other = swap(z)
    first = row_of(z.shape) < 4
    pre = jnp.where(first, z, other)
    grad = jnp.where(first, other, z)
    c = 0.7978845608028654
    t = jnp.tanh(c * (pre + 0.044715 * (pre * pre * pre)))
    act = 0.5 * pre * (1.0 + t)
    slope = 0.5 * (1.0 + t) + 0.5 * pre * (1.0 - t * t) * (c * (1.0 + 3 * 0.044715 * (pre * pre)))
    both = jnp.where(first, act, grad * slope)
    for k in range(out.shape[0]):
        out[k] = both


def slot_rows(got, keep, own_in, own_out, others, out, full):
    w = own_in.shape[1]
    piece = 2 * w
    hidden = own_in.shape[2]
    chips = got.shape[0]
    share = hidden // chips
    core = core_index()
    for k in range(chips):
        full[:, k * share : (k + 1) * share] = got[k, :, 0:share]
    lane = lane_of((piece, LANES))
    cols = jnp.zeros((piece, LANES), F32)
    for a in range(2):
        for kind, mine, theirs in ((0, own_out, others.at[1]), (1, own_in, others.at[0])):
            r = 4 * kind + 2 * a
            sums = [jnp.zeros((piece, LANES), F32) for _ in range(2)]
            for h in range(0, hidden, LANES):
                s = slice(h, h + LANES)
                block = jnp.concatenate([mine[a, :, s], theirs[a, :, s]], axis=0)
                for p in range(2):
                    sums[p] = sums[p] + block * full[r + p : r + p + 1, s]
            for p in range(2):
                cols = jnp.where(lane == r + p, jnp.sum(sums[p], axis=1, keepdims=True), cols)
    own, near = cols[0:w], cols[w:]
    low = jnp.where(core == 0, own, near)
    high = jnp.where(core == 0, near, own)
    square = jnp.concatenate([low, high, jnp.zeros((LANES - piece, LANES), F32)], axis=0)
    rows = jnp.transpose(square)[0:8]
    full[:, hidden:] = keep[...]
    out[0:8] = jnp.where(lane_of((8, LANES)) < piece, rows, swap(keep[...]))
    out[8:16] = keep[...]


def copies(tile, out):
    value = tile[...]
    for k in range(out.shape[0]):
        out[k] = value


def width_products(
    mine, near, tokens, grad_out, logits, shares, out, weights, rows, outs, ins, marks
):
    n = out.shape[0]
    piece = rows.shape[1] // 2
    core = core_index()
    for c in range(2):
        for b, e, k in seats(n):
            tile = jnp.where(core == c, mine[k], near[k])
            s, w = slice(8 * e + 4 * c, 8 * e + 4 * c + 4), slice(b * piece, (b + 1) * piece)
            outs[s, w] = tile[0:4, 0:piece]
            rows[s, w] = tile[4:8, 0:piece]
            ins[s, w] = tile[8:12, 0:piece]
            if b == 0:
                marks[s] = tile[4:8]
    top, total = (marks[:, piece + i : piece + i + 1] for i in range(2))
    slots = rows.shape[0]
    ins[slots:] = jnp.zeros(ins[slots:].shape, F32)
    cross = contract(rows[...], jnp.transpose(ins[...]), 1, 0)
    own = lane_of(cross.shape) == lax.broadcasted_iota(jnp.int32, cross.shape, 0)
    column = jnp.sum(jnp.where(own, cross, 0.0), axis=1, keepdims=True)
    first = contract(outs[...], grad_out[...], 1, 0, THREE)
    second = contract(rows[...], tokens[...], 1, 0) - column
    for i in range(n):
        s = slice(i * LANES, (i + 1) * LANES)
        combine = shares[:, s]
        dispatch = jnp.exp(logits[i] - top) / total
        weights[i] = dispatch
        part = combine * first[:, s]
        line = jnp.sum(part, axis=0, keepdims=True)
        out[i] = part - combine * line + dispatch * second[:, s]


def router_part(got, tokens, mine, theirs):
    n = got.shape[0]
    grads = jnp.concatenate([got[e] for e in range(n)], axis=1)
    part = contract(tokens[...], grads, 1, 1, THREE)
    q = part.shape[0] // 4
    low = jnp.concatenate([part[0:q], part[q : 2 * q]], axis=1)
    high = jnp.concatenate([part[2 * q : 3 * q], part[3 * q :]], axis=1)
    core = core_index()
    mine[...] = jnp.where(core == 0, low, high)
    theirs[...] = jnp.where(core == 0, high, low)


def token_grads(got, weights, rows, router, out):
    left = jnp.transpose(jnp.concatenate([router[...], rows[...]], axis=0))
    for e in range(got.shape[0]):
        right = jnp.concatenate([got[e], weights[e]], axis=0)
        out[:, e * LANES : (e + 1) * LANES] = contract(left, right, 1, 0, THREE)


def add_copies(a, b, c, d, out):
    total = (a[...] + b[...]) + (c[...] + d[...])
    for k in range(out.shape[0]):
        out[k] = total


def add_all(got, out):
    out[...] = jnp.sum(got[...], axis=0)


def unfold(mine, theirs, out):
    core = core_index()
    a, b = mine[...], theirs[...]
    q, h = out.shape[1] // 4, LANES // 2
    for i, values in enumerate((jnp.where(core == 0, a, b), jnp.where(core == 0, b, a))):
        turned = jnp.transpose(values)
        out[:, 2 * i * q : (2 * i + 1) * q] = turned[:h]
        out[:, (2 * i + 1) * q : (2 * i + 2) * q] = turned[h:]


def weight_grads(full, near, grad_in, grad_out):
    w = grad_in.shape[1]
    hidden = grad_in.shape[2]
    core = core_index()
    step = 512
    for base, values in ((2 * core, full), (2 - 2 * core, near)):
        held = values[:, hidden:]
        part = jnp.where(core == 0, held[:, 0:w], held[:, w : 2 * w])
        cols = jnp.transpose(part)
        for a in range(2):
            for h in range(0, hidden, step):
                s = slice(h, h + step)
                i, j = 2 * a, 2 * a + 1
                grad_out[base + a, :, s] = (
                    cols[:, 4 + i : 5 + i] * values[i : i + 1, s]
                    + cols[:, 4 + j : 5 + j] * values[j : j + 1, s]
                )
                grad_in[base + a, :, s] = (
                    cols[:, i : i + 1] * values[4 + i : 5 + i, s]
                    + cols[:, j : j + 1] * values[4 + j : 5 + j, s]
                )


def per_device(tokens, router, w_in, w_out, grad_out):
    n_seq, n_exp = lax.axis_size(S), lax.axis_size(E)
    experts, width_block, hidden = w_in.shape
    rows_block, local_tokens = tokens.shape
    slots = router.shape[1]
    chips = n_seq // 2
    piece = 2 * width_block
    core = core_index()
    partner = [(i, i ^ 1) for i in range(n_seq)]
    groups = [[2 * k + c for k in range(chips)] for c in range(2)]
    turned = router.T
    spread = (n_exp, slots, LANES)
    to_owner = [
        ((2 * seat(b, e, f) + c) * n_exp + f, (2 * (2 * f + b) + c) * n_exp + e)
        for b in range(2)
        for e in range(n_exp)
        for c in range(2)
        for f in range(n_exp)
    ]
    from_owner = [(there, here) for here, there in to_owner]

    def to_partner(values):
        return lax.ppermute(values, S, partner)

    def in_hbm(values):
        return pltpu.with_memory_space_constraint(values, pltpu.HBM)

    far_spec = pl.BlockSpec(memory_space=pltpu.HBM)
    vmem_spec = pl.BlockSpec(memory_space=pltpu.VMEM)
    limit = pltpu.CompilerParams(vmem_limit_bytes=16 * 1024 * 1024)
    half = (experts // 2,) + w_in.shape[1:]
    sent, tokens, away = pl.pallas_call(
        start_up,
        out_shape=[
            pltpu.VMEM(spread, F32),
            pltpu.VMEM(tokens.shape, F32),
            pltpu.VMEM((2,) + half, F32),
        ],
        in_specs=[far_spec] * 4,
        out_specs=[vmem_spec] * 3,
        scratch_shapes=[pltpu.VMEM(turned.shape, F32), pltpu.SemaphoreType.DMA((4,))],
        compiler_params=limit,
    )(in_hbm(turned), in_hbm(tokens), in_hbm(w_in), in_hbm(w_out))
    others = to_partner(away)
    logits = exchange(run(add_spread, spread, exchange(sent, E)), E)

    tiles = (chips, 8, LANES)
    mine, near, shares = run(
        partial_rows,
        [tiles, tiles, (slots, local_tokens)],
        logits,
        tokens,
        grad_out,
        scratch=[(2,) + tiles],
    )
    sent = run(functools.partial(merge_cores, piece=piece), tiles, mine, to_partner(near))
    tile = run(
        functools.partial(merge_chips, piece=piece), (8, LANES), exchange(sent, S, groups)
    )
    tile, w_in, w_out = lax.optimization_barrier((tile, w_in, w_out))
    own_in, own_out = pl.pallas_call(
        load_own,
        out_shape=[pltpu.VMEM(half, F32)] * 2,
        in_specs=[far_spec] * 2,
        out_specs=[vmem_spec] * 2,
        scratch_shapes=[pltpu.SemaphoreType.DMA((2,))],
        compiler_params=limit,
    )(in_hbm(w_in), in_hbm(w_out))
    tile, own_in, own_out = lax.optimization_barrier(
        (lax.ppermute(tile, (S, E), to_owner), own_in, own_out)
    )
    weights = (own_in, own_out, others)
    share = hidden // chips
    cut = -(-share // LANES) * LANES
    sent, held = run(
        hidden_parts,
        [(chips, 8, cut), (8, LANES)],
        tile,
        *weights,
        scratch=[(8, hidden)],
    )
    sent = run(gate, (chips, 8, cut), exchange(sent, S, groups))
    tile, full = run(
        slot_rows, [(16, LANES), (8, hidden + LANES)], exchange(sent, S, groups), held, *weights
    )
    grad_w_in, grad_w_out = run(
        weight_grads, [w_in.shape, w_out.shape], full, to_partner(full)
    )
    tile, grad_w_in, grad_w_out = lax.optimization_barrier(
        (lax.ppermute(tile, (S, E), from_owner), grad_w_in, grad_w_out)
    )
    sent = run(copies, (chips, 16, LANES), tile)
    mine = exchange(sent, S, groups)
    near = to_partner(mine)
    sent, weights, rows = run(
        width_products,
        [spread, spread, (slots, rows_block)],
        mine,
        near,
        tokens,
        grad_out,
        logits,
        shares,
        scratch=[(slots, rows_block), (LANES, rows_block), (slots, LANES)],
    )
    sent = run(add_spread, spread, exchange(sent, E))
    grads = exchange(sent, E)
    fold = (rows_block // 4, 2 * slots)
    near, theirs = run(router_part, [fold, fold], grads, tokens)
    across = n_seq // 2
    rows_z = [
        [across * x + 2 * z + c for z in range(across // 2)] for x in range(2) for c in range(2)
    ]
    pairs = [near, to_partner(theirs)]
    pairs.append(lax.ppermute(near, S, [(i, i ^ across) for i in range(n_seq)]))
    pairs.append(lax.ppermute(theirs, S, [(i, i ^ across ^ 1) for i in range(n_seq)]))
    grad_tokens = run(
        token_grads, (rows_block, local_tokens), grads, weights, rows, turned
    )
    *pairs, grad_tokens = lax.optimization_barrier((*pairs, grad_tokens))
    got = exchange(run(add_copies, (across // 2,) + fold, *pairs), S, rows_z)
    near = run(add_all, fold, got)
    grad_router = run(unfold, (slots, rows_block), near, to_partner(near)).T
    return (grad_tokens, grad_router, grad_w_in, grad_w_out)


def solution(mesh):
    placed = (
        P("expert", "seq"),
        P("expert", None),
        P("expert", "seq", None),
        P("expert", "seq", None),
        P("expert", "seq"),
    )
    return jax.shard_map(
        per_device,
        mesh=mesh,
        in_specs=placed,
        out_specs=(
            P("expert", "seq"),
            P("expert", None),
            P("expert", "seq", None),
            P("expert", "seq", None),
        ),
        check_vma=False,
    )
```

```python
import functools

import jax
import jax.numpy as jnp
from jax import lax
from jax.experimental import pallas as pl
from jax.experimental.pallas import tpu as pltpu
from jax.sharding import PartitionSpec as P

FULL = lax.Precision.HIGHEST
THREE = lax.Precision.HIGH
S = "seq"
E = "expert"
LANES = 128
F32 = jnp.float32


def contract(left, right, left_dim, right_dim, precision=FULL):
    return lax.dot_general(
        left,
        right,
        (((left_dim,), (right_dim,)), ((), ())),
        precision=precision,
        preferred_element_type=F32,
    )


def exchange(blocks, axis, groups=None):
    return lax.all_to_all(blocks, axis, 0, 0, axis_index_groups=groups, tiled=True)


def run(kernel, shapes, *values, scratch=(), flops=0):
    single = not isinstance(shapes, list)
    shapes = [shapes] if single else shapes
    size = 4 * sum(v.size for v in values) + 4 * sum(functools.reduce(lambda a, b: a * b, s) for s in shapes)
    spec = pl.BlockSpec(memory_space=pltpu.VMEM)
    out = pl.pallas_call(
        kernel,
        out_shape=[jax.ShapeDtypeStruct(s, F32) for s in shapes],
        in_specs=[spec] * len(values),
        out_specs=[spec] * len(shapes),
        scratch_shapes=[pltpu.VMEM(s, F32) for s in scratch],
        compiler_params=pltpu.CompilerParams(vmem_limit_bytes=16 * 1024 * 1024),
        cost_estimate=pl.CostEstimate(flops=flops, bytes_accessed=size, transcendentals=0),
    )(*values)
    return out[0] if single else out


def row_of(shape):
    return lax.broadcasted_iota(jnp.int32, shape, len(shape) - 2) % 8


def lane_of(shape):
    return lax.broadcasted_iota(jnp.int32, shape, len(shape) - 1)


def swap(values):
    return jnp.concatenate([values[..., 4:8, :], values[..., 0:4, :]], axis=-2)


def core_index():
    return lax.axis_index(S) % 2


SEATS = (0xE680F7D5, 0xB291A3C4)


def seat(b, e, column):
    index = 2 * (((e >> 1) - (column >> 1)) & 3) + ((e ^ column) & 1)
    if isinstance(column, int):
        value = SEATS[b] >> (4 * index) & 15
    else:
        word = SEATS[b] - (1 << 32 if SEATS[b] >> 31 else 0)
        value = lax.shift_right_logical(jnp.int32(word), 4 * index) & 15
    return (((value >> 3) ^ (column >> 2)) << 3) | (((value & 7) + 2 * (column & 3)) & 7)


def seats(n):
    column = lax.axis_index(E)
    return [(b, e, seat(b, e, column)) for b in range(2) for e in range(n)]


def start_up(router, tokens, w_in, w_out, out, x, away, left, sems):
    half = away.shape[1]
    far = pl.ds(half * (1 - core_index()), half)
    pairs = [
        (router, left),
        (tokens, x),
        (w_in.at[far], away.at[0]),
        (w_out.at[far], away.at[1]),
    ]
    copies = [pltpu.make_async_copy(a, b, sems.at[i]) for i, (a, b) in enumerate(pairs)]
    for copy in copies:
        copy.start()
    copies[0].wait()
    copies[1].wait()
    part = contract(left[...], x[...], 1, 0)
    for i in range(out.shape[0]):
        out[i] = part[:, i * LANES : (i + 1) * LANES]
    copies[2].wait()
    copies[3].wait()


def load_own(w_in, w_out, own_in, own_out, sems):
    half = own_in.shape[0]
    own = pl.ds(half * core_index(), half)
    copies = [
        pltpu.make_async_copy(w_in.at[own], own_in, sems.at[0]),
        pltpu.make_async_copy(w_out.at[own], own_out, sems.at[1]),
    ]
    for copy in copies:
        copy.start()
    for copy in copies:
        copy.wait()


def add_spread(got, out):
    total = jnp.sum(got[...], axis=0)
    for e in range(out.shape[0]):
        out[e] = total


def partial_rows(got, tokens, grad_out, sent, shares, both):
    n, slots = got.shape[0], got.shape[1]
    logits = jnp.concatenate([got[e] for e in range(n)], axis=1)
    raised = jnp.exp(logits - jnp.max(logits, axis=0, keepdims=True))
    combine = raised / jnp.sum(raised, axis=0, keepdims=True)
    shares[...] = combine
    top = jnp.max(logits, axis=1, keepdims=True)
    raised = jnp.exp(logits - top)
    total = jnp.sum(raised, axis=1, keepdims=True)
    rows_in = contract(raised, tokens[...], 1, 1)
    rows_out = contract(combine, grad_out[...], 1, 1, THREE)
    piece = rows_in.shape[1] // 2
    lane = lane_of((slots, LANES))
    marks = jnp.where(lane == piece, top, jnp.where(lane == piece + 1, total, 0.0))
    plain = jnp.where(lane_of((4, LANES)) == piece + 1, 1.0, 0.0)
    for b, e, k in seats(n):
        for c in range(2):
            s, w = slice(8 * e + 4 * c, 8 * e + 4 * c + 4), slice(b * piece, (b + 1) * piece)
            both[c, k, 0:4] = marks[s]
            both[c, k, 4:8] = plain
            both[c, k, 0:4, 0:piece] = rows_in[s, w]
            both[c, k, 4:8, 0:piece] = rows_out[s, w]
    core = core_index()
    sent[:, 0:8] = both[core]
    sent[:, 8:16] = both[1 - core]


def merge(parts, piece):
    top = functools.reduce(jnp.maximum, [p[:, piece : piece + 1] for p in parts])
    rows = sum(jnp.exp(p[:, piece : piece + 1] - top) * p for p in parts)
    return jnp.where(lane_of(rows.shape) == piece, top, rows)


def merge_chips(got, mine, near, piece):
    rows = merge([got[k] for k in range(got.shape[0])], piece)
    mine[...] = rows[0:8]
    near[...] = rows[8:16]


def hidden_parts(got, other, own_in, own_out, others, sent, keep, full):
    w = own_in.shape[1]
    piece = 2 * w
    hidden = own_in.shape[2]
    core = core_index()
    rows = merge([got[...], other[...]], piece)
    scaled = (row_of((8, LANES)) < 4) & (lane_of((8, LANES)) < piece)
    rows = jnp.where(scaled, rows / rows[:, piece + 1 : piece + 2], rows)
    keep[...] = rows
    turned = jnp.transpose(rows)
    low, high = turned[0:w], turned[w:piece]
    own = jnp.where(core == 0, low, high)
    near = jnp.where(core == 0, high, low)
    for a in range(2):
        for kind, mine, theirs in ((0, own_in, others.at[0]), (1, own_out, others.at[1])):
            r = 4 * kind + 2 * a
            values = [
                jnp.concatenate(
                    [
                        jnp.broadcast_to(own[:, r + p : r + p + 1], (w, LANES)),
                        jnp.broadcast_to(near[:, r + p : r + p + 1], (w, LANES)),
                    ],
                    axis=0,
                )
                for p in range(2)
            ]
            for h in range(0, hidden, LANES):
                s = slice(h, h + LANES)
                block = jnp.concatenate([mine[a, :, s], theirs[a, :, s]], axis=0)
                for p in range(2):
                    full[r + p : r + p + 1, s] = jnp.sum(block * values[p], axis=0, keepdims=True)
    chips = sent.shape[0]
    share = hidden // chips
    for k in range(chips):
        sent[k, :, 0:share] = full[:, k * share : (k + 1) * share]
        sent[k, :, share:] = jnp.zeros((8, sent.shape[2] - share), F32)


def gate(got, out):
    z = jnp.sum(got[...], axis=0)
    other = swap(z)
    first = row_of(z.shape) < 4
    pre = jnp.where(first, z, other)
    grad = jnp.where(first, other, z)
    c = 0.7978845608028654
    t = jnp.tanh(c * (pre + 0.044715 * (pre * pre * pre)))
    act = 0.5 * pre * (1.0 + t)
    slope = 0.5 * (1.0 + t) + 0.5 * pre * (1.0 - t * t) * (c * (1.0 + 3 * 0.044715 * (pre * pre)))
    both = jnp.where(first, act, grad * slope)
    for k in range(out.shape[0]):
        out[k] = both


def slot_rows(got, keep, own_in, own_out, others, out, full):
    w = own_in.shape[1]
    piece = 2 * w
    hidden = own_in.shape[2]
    chips = got.shape[0]
    share = hidden // chips
    core = core_index()
    for k in range(chips):
        full[:, k * share : (k + 1) * share] = got[k, :, 0:share]
    lane = lane_of((piece, LANES))
    cols = jnp.zeros((piece, LANES), F32)
    for a in range(2):
        for kind, mine, theirs in ((0, own_out, others.at[1]), (1, own_in, others.at[0])):
            r = 4 * kind + 2 * a
            sums = [jnp.zeros((piece, LANES), F32) for _ in range(2)]
            for h in range(0, hidden, LANES):
                s = slice(h, h + LANES)
                block = jnp.concatenate([mine[a, :, s], theirs[a, :, s]], axis=0)
                for p in range(2):
                    sums[p] = sums[p] + block * full[r + p : r + p + 1, s]
            for p in range(2):
                cols = jnp.where(lane == r + p, jnp.sum(sums[p], axis=1, keepdims=True), cols)
    own, near = cols[0:w], cols[w:]
    low = jnp.where(core == 0, own, near)
    high = jnp.where(core == 0, near, own)
    square = jnp.concatenate([low, high, jnp.zeros((LANES - piece, LANES), F32)], axis=0)
    rows = jnp.transpose(square)[0:8]
    full[:, hidden:] = keep[...]
    out[0:8] = jnp.where(lane_of((8, LANES)) < piece, rows, swap(keep[...]))
    out[8:16] = keep[...]


def copies(tile, out):
    value = tile[...]
    for k in range(out.shape[0]):
        out[k] = value


def width_products(
    mine, near, tokens, grad_out, logits, shares, out, weights, rows, outs, ins, marks
):
    n = out.shape[0]
    piece = rows.shape[1] // 2
    core = core_index()
    for c in range(2):
        for b, e, k in seats(n):
            tile = jnp.where(core == c, mine[k], near[k])
            s, w = slice(8 * e + 4 * c, 8 * e + 4 * c + 4), slice(b * piece, (b + 1) * piece)
            outs[s, w] = tile[0:4, 0:piece]
            rows[s, w] = tile[4:8, 0:piece]
            ins[s, w] = tile[8:12, 0:piece]
            if b == 0:
                marks[s] = tile[4:8]
    top, total = (marks[:, piece + i : piece + i + 1] for i in range(2))
    slots = rows.shape[0]
    ins[slots:] = jnp.zeros(ins[slots:].shape, F32)
    cross = contract(rows[...], jnp.transpose(ins[...]), 1, 0)
    own = lane_of(cross.shape) == lax.broadcasted_iota(jnp.int32, cross.shape, 0)
    column = jnp.sum(jnp.where(own, cross, 0.0), axis=1, keepdims=True)
    first = contract(outs[...], grad_out[...], 1, 0, THREE)
    second = contract(rows[...], tokens[...], 1, 0) - column
    for i in range(n):
        s = slice(i * LANES, (i + 1) * LANES)
        combine = shares[:, s]
        dispatch = jnp.exp(logits[i] - top) / total
        weights[i] = dispatch
        part = combine * first[:, s]
        line = jnp.sum(part, axis=0, keepdims=True)
        out[i] = part - combine * line + dispatch * second[:, s]


def router_part(got, tokens, mine, theirs):
    n = got.shape[0]
    grads = jnp.concatenate([got[e] for e in range(n)], axis=1)
    part = contract(tokens[...], grads, 1, 1, THREE)
    q = part.shape[0] // 4
    low = jnp.concatenate([part[0:q], part[q : 2 * q]], axis=1)
    high = jnp.concatenate([part[2 * q : 3 * q], part[3 * q :]], axis=1)
    core = core_index()
    mine[...] = jnp.where(core == 0, low, high)
    theirs[...] = jnp.where(core == 0, high, low)


def token_grads(got, weights, rows, router, out):
    left = jnp.transpose(jnp.concatenate([router[...], rows[...]], axis=0))
    for e in range(got.shape[0]):
        right = jnp.concatenate([got[e], weights[e]], axis=0)
        out[:, e * LANES : (e + 1) * LANES] = contract(left, right, 1, 0, THREE)


def add_copies(a, b, c, d, out):
    total = (a[...] + b[...]) + (c[...] + d[...])
    for k in range(out.shape[0]):
        out[k] = total


def add_all(got, out):
    out[...] = jnp.sum(got[...], axis=0)


def unfold(mine, theirs, out):
    core = core_index()
    a, b = mine[...], theirs[...]
    q, h = out.shape[1] // 4, LANES // 2
    for i, values in enumerate((jnp.where(core == 0, a, b), jnp.where(core == 0, b, a))):
        turned = jnp.transpose(values)
        out[:, 2 * i * q : (2 * i + 1) * q] = turned[:h]
        out[:, (2 * i + 1) * q : (2 * i + 2) * q] = turned[h:]


def weight_grads(full, near, grad_in, grad_out):
    w = grad_in.shape[1]
    hidden = grad_in.shape[2]
    core = core_index()
    step = 512
    for base, values in ((2 * core, full), (2 - 2 * core, near)):
        held = values[:, hidden:]
        part = jnp.where(core == 0, held[:, 0:w], held[:, w : 2 * w])
        cols = jnp.transpose(part)
        for a in range(2):
            for h in range(0, hidden, step):
                s = slice(h, h + step)
                i, j = 2 * a, 2 * a + 1
                grad_out[base + a, :, s] = (
                    cols[:, 4 + i : 5 + i] * values[i : i + 1, s]
                    + cols[:, 4 + j : 5 + j] * values[j : j + 1, s]
                )
                grad_in[base + a, :, s] = (
                    cols[:, i : i + 1] * values[4 + i : 5 + i, s]
                    + cols[:, j : j + 1] * values[4 + j : 5 + j, s]
                )


def per_device(tokens, router, w_in, w_out, grad_out):
    n_seq, n_exp = lax.axis_size(S), lax.axis_size(E)
    experts, width_block, hidden = w_in.shape
    rows_block, local_tokens = tokens.shape
    slots = router.shape[1]
    chips = n_seq // 2
    piece = 2 * width_block
    core = core_index()
    partner = [(i, i ^ 1) for i in range(n_seq)]
    groups = [[2 * k + c for k in range(chips)] for c in range(2)]
    turned = router.T
    spread = (n_exp, slots, LANES)
    to_owner = [
        ((2 * seat(b, e, f) + c) * n_exp + f, (2 * (2 * f + b) + c) * n_exp + e)
        for b in range(2)
        for e in range(n_exp)
        for c in range(2)
        for f in range(n_exp)
    ]
    from_owner = [(there, here) for here, there in to_owner]

    def to_partner(values):
        return lax.ppermute(values, S, partner)

    def in_hbm(values):
        return pltpu.with_memory_space_constraint(values, pltpu.HBM)

    far_spec = pl.BlockSpec(memory_space=pltpu.HBM)
    vmem_spec = pl.BlockSpec(memory_space=pltpu.VMEM)
    limit = pltpu.CompilerParams(vmem_limit_bytes=16 * 1024 * 1024)
    half = (experts // 2,) + w_in.shape[1:]
    sent, tokens, away = pl.pallas_call(
        start_up,
        out_shape=[
            pltpu.VMEM(spread, F32),
            pltpu.VMEM(tokens.shape, F32),
            pltpu.VMEM((2,) + half, F32),
        ],
        in_specs=[far_spec] * 4,
        out_specs=[vmem_spec] * 3,
        scratch_shapes=[pltpu.VMEM(turned.shape, F32), pltpu.SemaphoreType.DMA((4,))],
        compiler_params=limit,
    )(in_hbm(turned), in_hbm(tokens), in_hbm(w_in), in_hbm(w_out))
    others = to_partner(away)
    logits = exchange(run(add_spread, spread, exchange(sent, E)), E)

    tiles = (chips, 8, LANES)
    sent, shares = run(
        partial_rows,
        [(chips, 16, LANES), (slots, local_tokens)],
        logits,
        tokens,
        grad_out,
        scratch=[(2,) + tiles],
    )
    tile, other = run(
        functools.partial(merge_chips, piece=piece), [(8, LANES)] * 2, exchange(sent, S, groups)
    )
    tile, other, w_in, w_out = lax.optimization_barrier((tile, other, w_in, w_out))
    own_in, own_out = pl.pallas_call(
        load_own,
        out_shape=[pltpu.VMEM(half, F32)] * 2,
        in_specs=[far_spec] * 2,
        out_specs=[vmem_spec] * 2,
        scratch_shapes=[pltpu.SemaphoreType.DMA((2,))],
        compiler_params=limit,
    )(in_hbm(w_in), in_hbm(w_out))
    crossed = [(here, there ^ n_exp) for here, there in to_owner]
    tile, other, own_in, own_out = lax.optimization_barrier(
        (
            lax.ppermute(tile, (S, E), to_owner),
            lax.ppermute(other, (S, E), crossed),
            own_in,
            own_out,
        )
    )
    weights = (own_in, own_out, others)
    share = hidden // chips
    cut = -(-share // LANES) * LANES
    sent, held = run(
        hidden_parts,
        [(chips, 8, cut), (8, LANES)],
        tile,
        other,
        *weights,
        scratch=[(8, hidden)],
    )
    sent = run(gate, (chips, 8, cut), exchange(sent, S, groups))
    tile, full = run(
        slot_rows, [(16, LANES), (8, hidden + LANES)], exchange(sent, S, groups), held, *weights
    )
    grad_w_in, grad_w_out = run(
        weight_grads, [w_in.shape, w_out.shape], full, to_partner(full)
    )
    tile, grad_w_in, grad_w_out = lax.optimization_barrier(
        (lax.ppermute(tile, (S, E), from_owner), grad_w_in, grad_w_out)
    )
    sent = run(copies, (chips, 16, LANES), tile)
    mine = exchange(sent, S, groups)
    near = to_partner(mine)
    sent, weights, rows = run(
        width_products,
        [spread, spread, (slots, rows_block)],
        mine,
        near,
        tokens,
        grad_out,
        logits,
        shares,
        scratch=[(slots, rows_block), (LANES, rows_block), (slots, LANES)],
    )
    sent = run(add_spread, spread, exchange(sent, E))
    grads = exchange(sent, E)
    fold = (rows_block // 4, 2 * slots)
    near, theirs = run(router_part, [fold, fold], grads, tokens)
    across = n_seq // 2
    rows_z = [
        [across * x + 2 * z + c for z in range(across // 2)] for x in range(2) for c in range(2)
    ]
    pairs = [near, to_partner(theirs)]
    pairs.append(lax.ppermute(near, S, [(i, i ^ across) for i in range(n_seq)]))
    pairs.append(lax.ppermute(theirs, S, [(i, i ^ across ^ 1) for i in range(n_seq)]))
    grad_tokens = run(
        token_grads, (rows_block, local_tokens), grads, weights, rows, turned
    )
    *pairs, grad_tokens = lax.optimization_barrier((*pairs, grad_tokens))
    got = exchange(run(add_copies, (across // 2,) + fold, *pairs), S, rows_z)
    near = run(add_all, fold, got)
    grad_router = run(unfold, (slots, rows_block), near, to_partner(near)).T
    return (grad_tokens, grad_router, grad_w_in, grad_w_out)


def solution(mesh):
    placed = (
        P("expert", "seq"),
        P("expert", None),
        P("expert", "seq", None),
        P("expert", "seq", None),
        P("expert", "seq"),
    )
    return jax.shard_map(
        per_device,
        mesh=mesh,
        in_specs=placed,
        out_specs=(
            P("expert", "seq"),
            P("expert", None),
            P("expert", "seq", None),
            P("expert", "seq", None),
        ),
        check_vma=False,
    )
```
